256 devices in a mesh: slab: 8 (over x, core), bulk: 32 (over y, z).
Axes of the slice: x: 4, y: 4, z: 8, core: 2. Of those that a mesh axis runs over, the one named last changes fastest.
Arguments:
- seg_offset: float32 [3, 1048576], P(None, ('slab', 'bulk')), may hold values from -1 to 1
- tangent: float32 [3, 1048576], P(None, ('slab', 'bulk')), may hold values from -3 to 3
- burgers: float32 [3, 1048576], P(None, ('slab', 'bulk')), may hold values from -3.6 to 3.6
- box_matrix: float32 [3, 3], replicated, may hold values from -1 to 1
- applied_stress: float32 [3, 3], replicated, may hold values from -3 to 3
- far_kernel: float32 [84, 10752], replicated, may hold values from -0.0024414062 to 0.0024414062
- block_cell: int32 [8192], P(('slab', 'bulk')), may hold values from 0 to 15
- fetch_table: int32 [8192, 5], P(('slab', 'bulk')), may hold values from 0 to 31
- pair_list: int32 [2, 49152], P(None, ('slab', 'bulk')), may hold values from 0 to 191, as said below
- image_shift: int32 [3, 49152], P(None, ('slab', 'bulk')), may hold values from -1 to 1
- pair_count: int32 [256], P(('slab', 'bulk')), may hold values from 161 to 192, as said below
- node_conn: int32 [2, 1048576], P(None, ('slab', 'bulk')), may hold values from 0 to 4095
Outputs:
- nodal_force: float32 [3, 1048576], P(None, ('slab', 'bulk'))
The draws below stay inside these ranges and needn't reach their ends.
Inputs may be any that keep to these rules, and one draw needn't show every extreme that they name: `pair_list`: in columns d * 192 + k with k < 160 the second entry is 32 + k; in the others both entries are below 32 and differ. `pair_count`: at least 161; some device holds 192.
All inputs are finite; a program needn't handle non-finite values.
Results may differ from the reference program's by a relative error of at most 0.0003.
Values sent between devices are 32-bit elements; how exact they have to be, the bound alone decides.
No kernel may reach another device: no remote copies, remote signals or barrier semaphores. Data moves between devices by JAX's collectives and lax.ppermute only.
A program may use at most 64 MiB of HBM per device.

```python
import jax
import jax.numpy as jnp
import numpy as np
from jax import lax

SEG = 128
BLK_DEV = 32
SEND = 5
CS = 16
NM = 84
NC = 128
NR = 160
PAIR_DEV = 192
SEG_DEV = 4096
NSEG = 1048576
NBLK = 8192
N_BULK = 32
DEVICES = 256


def draw_pair_list(key, part):
    key = jax.random.fold_in(key, 11)
    key_one, key_two = jax.random.split(key)
    total = DEVICES * PAIR_DEV
    position = jnp.arange(total, dtype=jnp.int32) % PAIR_DEV
    home = jax.random.randint(key_one, (total,), 0, BLK_DEV)
    other = (home + jax.random.randint(key_two, (total,), 1, BLK_DEV)) % BLK_DEV
    partner = jnp.where(position < NR, BLK_DEV + position, other)
    return jnp.stack([home, partner]).astype(jnp.int32)


def draw_pair_count(key, part):
    key = jax.random.fold_in(key, 23)
    key_one, key_two = jax.random.split(key)
    extra = jax.random.randint(key_one, (DEVICES,), 0, BLK_DEV)
    counts = NR + 1 + extra * extra // BLK_DEV
    chosen = jax.random.randint(key_two, (), 0, DEVICES)
    return counts.at[chosen].set(PAIR_DEV).astype(jnp.int32)


def set_ends(entries, rng, least, top_value):
    longest = entries.shape.index(max(entries.shape))
    spots = []
    for shift in (0, 1):
        where = [jax.random.randint(jax.random.fold_in(rng, axis), (), 0, length) for axis, length in enumerate(entries.shape)]
        where[longest] = (where[longest] + shift) % entries.shape[longest]
        spots.append(tuple(where))
    return entries.at[spots[0]].set(least).at[spots[1]].set(top_value)


def levels(key, dims, cuts, low, top_value):
    level = 1.0
    for dim, shards_of in cuts:
        heights = jax.random.uniform(jax.random.fold_in(jax.random.fold_in(key, 6), dim), (shards_of,), jnp.float32, low / len(cuts), top_value / len(cuts))
        level = level * jnp.repeat(jnp.exp(heights), dims[dim] // shards_of).reshape((-1,) + (1,) * (len(dims) - 1 - dim))
    return level


def gaussian(stream_key, dims, spread, limit, shards=(), held_as=jnp.bfloat16):
    factor_of = levels(stream_key, dims, shards, -0.22, 0.18) if shards else 1.0
    values = jax.random.normal(stream_key, dims, jnp.float32) * spread * factor_of
    return jnp.minimum(jnp.maximum(values, -limit), limit).astype(held_as)


def setup_inputs(seed: int = 0) -> dict:
    splits = jax.random.split(jax.random.key(seed), 13)
    return {
        "seg_offset": jnp.clip(jax.random.uniform(splits[0], (3, NSEG), jnp.float32, -1.0, 1.0) * levels(splits[0], (3, NSEG), ((1, 256),), -0.4, 0.0), -1.0, 1.0),
        "tangent": gaussian(splits[1], (3, NSEG), 0.5, 3.0, ((1, 256),), jnp.float32),
        "burgers": gaussian(splits[2], (3, NSEG), 0.6, 3.6, ((1, 256),), jnp.float32),
        "box_matrix": jnp.clip(jax.random.uniform(splits[3], (3, 3), jnp.float32, -1.0, 1.0), -1.0, 1.0),
        "applied_stress": gaussian(splits[4], (3, 3), 0.5, 3.0, (), jnp.float32),
        "far_kernel": gaussian(splits[5], (NM, NC * NM), (NM * NSEG // 16) ** -0.5, 0.0024414062, (), jnp.float32),
        "block_cell": set_ends(jax.random.randint(splits[6], (NBLK,), 0, CS), jax.random.fold_in(splits[6], 1), 0, CS - 1).astype(jnp.int32),
        "fetch_table": set_ends(jax.random.randint(splits[7], (DEVICES * N_BULK, SEND), 0, BLK_DEV), jax.random.fold_in(splits[7], 1), 0, BLK_DEV - 1).astype(jnp.int32),
        "pair_list": draw_pair_list(jax.random.fold_in(splits[12], 71), 0),
        "image_shift": set_ends(jax.random.randint(splits[9], (3, DEVICES * PAIR_DEV), -1, 2), jax.random.fold_in(splits[9], 1), -1, 1).astype(jnp.int32),
        "pair_count": draw_pair_count(jax.random.fold_in(splits[12], 71), 0),
        "node_conn": set_ends(jax.random.randint(splits[11], (2, NSEG), 0, SEG_DEV), jax.random.fold_in(splits[11], 1), 0, SEG_DEV - 1).astype(jnp.int32),
    }


KAPPA = 0.2
CORE_SQ = 0.25
HIGH = lax.Precision.HIGHEST

def exponents():
    listed = [(power_x, power_y, power_z) for power_x in range(7) for power_y in range(7 - power_x) for power_z in range(7 - power_x - power_y)]
    return np.array(listed, dtype=np.int32)

def basis(offset):
    table = exponents()
    powers = [jnp.ones_like(offset)]
    for degree in range(6):
        powers.append(powers[-1] * offset)
    stacked = jnp.stack(powers)
    return stacked[table[:, 0], 0] * stacked[table[:, 1], 1] * stacked[table[:, 2], 2]

def pair_tile(left, right, shift_vec):
    gap = left[0:3, :, None] - right[0:3, None, :] - shift_vec[:, None, None]
    dist_sq = lax.optimization_barrier(jnp.sum(gap * gap, axis=0)) + CORE_SQ
    tan_tan = lax.optimization_barrier(jnp.sum(left[3:6, :, None] * right[3:6, None, :], axis=0))
    bur_bur = lax.optimization_barrier(jnp.sum(left[6:9, :, None] * right[6:9, None, :], axis=0))
    bur_tan = lax.optimization_barrier(jnp.sum(left[6:9, :, None] * right[3:6, None, :], axis=0))
    tan_bur = lax.optimization_barrier(jnp.sum(left[3:6, :, None] * right[6:9, None, :], axis=0))
    weight = KAPPA * (bur_bur * tan_tan + bur_tan * tan_bur) / (dist_sq * jnp.sqrt(dist_sq))
    pushed = weight[None] * gap
    return (lax.optimization_barrier(jnp.sum(pushed, axis=2)), -lax.optimization_barrier(jnp.sum(pushed, axis=1)))

def applied_force(applied_stress, burgers, tangent):
    sym_stress = 0.5 * (applied_stress + applied_stress.T)
    traction = lax.optimization_barrier(jnp.sum(sym_stress[:, :, None] * burgers[None], axis=1))
    return jnp.cross(traction, tangent, axis=0)

def reference(seg_offset, tangent, burgers, box_matrix, applied_stress, far_kernel, block_cell, fetch_table, pair_list, image_shift, pair_count, node_conn):
    seg_data = jnp.concatenate([seg_offset, tangent, burgers], axis=0)
    blocks = seg_data.reshape(9, NBLK, SEG).transpose(1, 0, 2)

    def device_pairs(device):
        slab_first = device // N_BULK * N_BULK
        peer_dev = slab_first + jnp.arange(NR, dtype=jnp.int32) // SEND
        wanted = lax.dynamic_slice_in_dim(fetch_table, device * N_BULK, N_BULK, 0).reshape(NR)
        global_ids = jnp.concatenate([device * BLK_DEV + jnp.arange(BLK_DEV, dtype=jnp.int32), peer_dev * BLK_DEV + wanted])
        pairs = lax.dynamic_slice_in_dim(pair_list, device * PAIR_DEV, PAIR_DEV, 1)
        shifts = lax.dynamic_slice_in_dim(image_shift, device * PAIR_DEV, PAIR_DEV, 1)
        shift_vecs = lax.optimization_barrier(jnp.sum(box_matrix[:, :, None] * shifts.astype(jnp.float32)[None], axis=1))
        left_ids = global_ids[pairs[0]]
        right_ids = global_ids[pairs[1]]
        valid = (jnp.arange(PAIR_DEV, dtype=jnp.int32) < pair_count[device]).astype(jnp.float32)
        near_left, near_right = jax.vmap(pair_tile, in_axes=(0, 0, 1))(blocks[left_ids], blocks[right_ids], shift_vecs)
        return (near_left * valid[:, None, None], near_right * valid[:, None, None], left_ids, right_ids)
    near_left, near_right, left_ids, right_ids = lax.map(device_pairs, jnp.arange(DEVICES, dtype=jnp.int32))
    near = jnp.zeros((NBLK, 3, SEG), jnp.float32)
    near = near.at[left_ids.reshape(-1)].add(near_left.reshape(-1, 3, SEG))
    near = near.at[right_ids.reshape(-1)].add(near_right.reshape(-1, 3, SEG))
    near_force = near.transpose(1, 0, 2).reshape(3, NSEG)
    phi = basis(seg_offset)
    charge = lax.optimization_barrier(jnp.sum(burgers * tangent, axis=0))
    block_moments = jnp.einsum('kbs,bs->bk', phi.reshape(NM, NBLK, SEG), charge.reshape(NBLK, SEG), precision=HIGH)
    block_slab = jnp.arange(NBLK, dtype=jnp.int32) // (N_BULK * BLK_DEV)
    global_cell = block_slab * CS + block_cell
    moments = jax.ops.segment_sum(block_moments, global_cell, num_segments=NC)
    cell_ids = jnp.arange(NC, dtype=jnp.int32)
    shifted = moments[(cell_ids[:, None] - cell_ids[None, :]) % NC]
    kernel_three = far_kernel.reshape(NM, NC, NM)
    masked_kernel = kernel_three * (cell_ids != 0).astype(jnp.float32)[None, :, None]
    local_exp = jnp.einsum('cdm,kdm->ck', shifted, masked_kernel, precision=HIGH)
    block_exp = local_exp[global_cell]
    potential = jnp.einsum('bk,kbs->bs', block_exp, phi.reshape(NM, NBLK, SEG), precision=HIGH).reshape(NSEG)
    far_force = potential[None] * burgers
    seg_force = near_force + far_force + applied_force(applied_stress, burgers, tangent)
    node_base = jnp.arange(NSEG, dtype=jnp.int32) // SEG_DEV * SEG_DEV
    first_end = jax.ops.segment_sum(seg_force.T, node_base + node_conn[0], num_segments=NSEG)
    second_end = jax.ops.segment_sum(seg_force.T, node_base + node_conn[1], num_segments=NSEG)
    return (0.5 * (first_end + second_end)).T
```

```python
import functools

import jax
import jax.numpy as jnp
import numpy as np
from jax import lax
from jax.experimental import pallas as pl
from jax.experimental.pallas import tpu as pltpu
from jax.sharding import PartitionSpec as P

SEG = 128
CS = 16
NM = 84
SEND = 5
ROWS = 48
META = 45
KAPPA = 0.2
CORE_SQ = 0.25
HIGH = lax.Precision.HIGHEST
VMEM = pl.BlockSpec(memory_space=pltpu.VMEM)
SMEM = pl.BlockSpec(memory_space=pltpu.SMEM)
f32 = jnp.float32


def exponents():
    return [(a, b, c) for a in range(7) for b in range(7 - a) for c in range(7 - a - b)]


def iota(shape, dim):
    return lax.broadcasted_iota(jnp.int32, shape, dim)


def lane_block(index):
    return pl.ds(pl.multiple_of(index * SEG, SEG), SEG)


def fill_table(table, off, tan, bur, diag, cross):
    b = [bur[i : i + 1, :] for i in range(3)]
    t = [tan[i : i + 1, :] for i in range(3)]
    table[0:3, :] = off[...]
    for i in range(3):
        table[3 + i : 4 + i, :] = diag * (b[i] * t[i])
    for row, (i, j) in enumerate(((0, 1), (0, 2), (1, 2))):
        table[6 + row : 7 + row, :] = cross * (b[i] * t[j] + b[j] * t[i])


def shift_of(box, shift, k):
    s = [shift[i, k].astype(f32) for i in range(3)]
    return [box[c, 0] * s[0] + box[c, 1] * s[1] + box[c, 2] * s[2] for c in range(3)]


def shift_rows(vec, shape):
    row = iota(shape, 0)
    return jnp.where(row == 0, vec[0], jnp.where(row == 1, vec[1], jnp.where(row == 2, vec[2], 0.0)))


def pack_kernel(pairs, shift, box, fetch, off, tan, bur, send, table):
    fill_table(table, off, tan, bur, 2.0 * KAPPA, KAPPA)
    row, lane = iota((ROWS - META, SEG), 0), iota((ROWS - META, SEG), 1)

    def peer(p, carry):
        meta = jnp.zeros((ROWS - META, SEG), f32)
        for s in range(SEND):
            k = p * SEND + s
            at = lane_block(pairs[0, k])
            vec = shift_rows(shift_of(box, shift, k), (8, SEG))
            send[p, 8 * s : 8 * s + 8, :] = table[0:8, at] - vec
            send[p, 40 + s : 41 + s, :] = table[8:9, at]
            meta = jnp.where((row == 0) & (lane == s), fetch[p, s].astype(f32), meta)
        send[p, META:ROWS, :] = meta
        return carry

    lax.fori_loop(0, send.shape[0], peer, 0)


def tile(left, col, acc, b):
    sums = [jnp.zeros((8, SEG), f32) for _ in range(3)]
    for r in range(SEG // 8):
        gap = [left[c] - col(c, r) for c in range(3)]
        dist = gap[0] * gap[0] + CORE_SQ + gap[1] * gap[1] + gap[2] * gap[2]
        coupling = left[3] * col(3, r)
        for c in range(4, 9):
            coupling = coupling + left[c] * col(c, r)
        inv = lax.rsqrt(dist)
        weight = coupling * (inv * inv * inv)
        for c in range(3):
            push = weight * gap[c]
            acc[b, c, 8 * r : 8 * r + 8, :] += push
            sums[c] = sums[c] + push
    return [jnp.sum(s, axis=0, keepdims=True) for s in sums]


def fold(acc, near):
    lane = iota((SEG, SEG), 1)

    def block(b, total):
        for c in range(3):
            total = jnp.where(lane == 4 * b + c, jnp.sum(acc[b, c], axis=1, keepdims=True), total)
        return total

    near[...] = -lax.fori_loop(0, acc.shape[0], block, jnp.zeros((SEG, SEG), f32)).T


def clear(acc):
    def block(b, carry):
        acc[b] = jnp.zeros(acc.shape[1:], f32)
        return carry

    lax.fori_loop(0, acc.shape[0], block, 0)


def fill_columns(table, at, col):
    turned = table[0:16, at].T
    for c in range(9):
        col(c, jnp.broadcast_to(turned[:, c : c + 1], (SEG, SEG)))


def own_kernel(pairs, shift, box, count, off, tan, bur, near, table, column, acc, left_acc):
    fill_table(table, off, tan, bur, 1.0, 1.0)
    table[9:16, :] = jnp.zeros((7, table.shape[1]), f32)
    clear(acc)
    clear(left_acc)
    row = iota((8, SEG), 0)
    first = pairs.shape[1] - acc.shape[0]

    def pair(k, carry):
        a, b = pairs[0, k], pairs[1, k]

        def put(c, value):
            column[c] = value

        fill_columns(table, lane_block(b), put)
        at = lane_block(a)
        scale = jnp.where(row < 3, 1.0, jnp.where(row < 6, 2.0 * KAPPA, KAPPA))
        head = table[0:8, at] * scale - shift_rows(shift_of(box, shift, k), (8, SEG))
        left = [head[i : i + 1, :] for i in range(8)] + [table[8:9, at] * KAPPA]
        rows = tile(left, lambda c, r: column[c, 8 * r : 8 * r + 8, :], acc, b)
        for c in range(3):
            left_acc[a, c : c + 1, :] += rows[c]
        return carry

    lax.fori_loop(first, count[0], pair, 0)
    fold(acc, near)
    for b in range(acc.shape[0]):
        near[4 * b : 4 * b + 3, :] += left_acc[b, 0:3, :]


def pair_kernel(recv, off, tan, bur, ret, near, table, columns, acc, ids_vmem, ids, sem):
    peers = recv.shape[0]
    for p in range(peers):
        ids_vmem[p : p + 1, :] = recv[p, META : META + 1, :].astype(jnp.int32)
    copy = pltpu.make_async_copy(ids_vmem, ids, sem)
    copy.start()
    fill_table(table, off, tan, bur, 1.0, 1.0)
    table[9:16, :] = jnp.zeros((7, table.shape[1]), f32)
    clear(acc)

    def block(b, carry):
        def put(c, value):
            columns[b, c] = value

        fill_columns(table, lane_block(b), put)
        return carry

    lax.fori_loop(0, acc.shape[0], block, 0)
    copy.wait()

    def peer(p, carry):
        for s in range(SEND):
            b = ids[p, s]
            left = [recv[p, 8 * s + i : 8 * s + i + 1, :] for i in range(8)]
            left.append(recv[p, 40 + s : 41 + s, :])
            rows = tile(left, lambda c, r: columns[b, c, 8 * r : 8 * r + 8, :], acc, b)
            for c in range(3):
                ret[p, 3 * s + c : 3 * s + c + 1, :] = rows[c]
        ret[p, 15:16, :] = jnp.zeros((1, SEG), f32)
        return carry

    lax.fori_loop(0, peers, peer, 0)
    fold(acc, near)


def fill_phi(phi, off):
    powers = []
    for i in range(3):
        x = off[i : i + 1, :]
        made = [None, x]
        for _ in range(5):
            made.append(made[-1] * x)
        powers.append(made)
    pairs_of = {}
    for k, (a, b, c) in enumerate(exponents()):
        if (a, b) not in pairs_of:
            got = [p for p in (powers[0][a], powers[1][b]) if p is not None]
            pairs_of[a, b] = got[0] * got[1] if len(got) == 2 else got[0] if got else None
        value = pairs_of[a, b]
        if c:
            value = powers[2][c] if value is None else value * powers[2][c]
        phi[k : k + 1, :] = jnp.ones_like(powers[0][1]) if value is None else value


def dot_nt(left, right, precision=None):
    return lax.dot_general(
        left, right, (((1,), (1,)), ((), ())), precision=precision, preferred_element_type=f32
    )


def moment_kernel(cell, off, tan, bur, out, phi, charged):
    fill_phi(phi, off)
    charge = jnp.sum(bur[...] * tan[...], axis=0, keepdims=True)
    row = iota((CS, SEG), 0)
    for b in range(cell.shape[0]):
        part = charge[:, b * SEG : (b + 1) * SEG]
        charged[:, b * SEG : (b + 1) * SEG] = jnp.where(row == cell[b], part, 0.0)
    part = dot_nt(charged[...], phi[...], HIGH)
    whole = jnp.concatenate([part, jnp.zeros((CS, SEG - NM), f32)], axis=1)
    for p in range(out.shape[0]):
        out[p] = whole


def far_kernel_body(cell, stress, operator, off, tan, bur, *rest):
    count = len(rest) - 5
    sources, (out, around, shifted, phi, pots) = rest[:count], rest[count:]
    cells = count * CS
    for q in range(count):
        around[q * CS : (q + 1) * CS, :] = sources[(count - q) % count][...]
    around[cells : cells + CS, :] = sources[0][...]
    shifted[:, 0:NM] = jnp.zeros((CS, NM), f32)
    for o in range(1, cells):
        shifted[:, o * NM : (o + 1) * NM] = around[cells - o : cells - o + CS, 0:NM]
    local_exp = dot_nt(shifted[...], operator[...], HIGH)
    fill_phi(phi, off)
    pots[...] = lax.dot_general(
        local_exp, phi[...], (((1,), (0,)), ((), ())), precision=HIGH, preferred_element_type=f32
    )
    b = [bur[i : i + 1, :] for i in range(3)]
    t = [tan[i : i + 1, :] for i in range(3)]
    sym = [[0.5 * (stress[i, j] + stress[j, i]) for j in range(3)] for i in range(3)]
    trac = [sym[i][0] * b[0] + sym[i][1] * b[1] + sym[i][2] * b[2] for i in range(3)]
    for i in range(3):
        j, k = (i + 1) % 3, (i + 2) % 3
        out[i : i + 1, :] = trac[j] * t[k] - trac[k] * t[j]
    row = iota((CS, SEG), 0)
    for block in range(cell.shape[0]):
        at = slice(block * SEG, (block + 1) * SEG)
        mine = jnp.where(row == cell[block], pots[:, at], 0.0)
        out[:, at] += jnp.sum(mine, axis=0, keepdims=True) * bur[:, at]


def final_kernel(pairs, back, near_own, near_pair, far, conn, out, left_acc, force, split):
    clear(left_acc)

    def peer(p, carry):
        for s in range(SEND):
            a = pairs[0, p * SEND + s]
            left_acc[a, 0:3, :] += back[p, 3 * s : 3 * s + 3, :]
        return carry

    lax.fori_loop(0, back.shape[0], peer, 0)
    for b in range(left_acc.shape[0]):
        at = slice(b * SEG, (b + 1) * SEG)
        near = near_own[4 * b : 4 * b + 3, :] + near_pair[4 * b : 4 * b + 3, :]
        force[0:3, at] = 0.5 * (far[:, at] + near + left_acc[b, 0:3, :])
    value = force[0:3, :]
    high = value.astype(jnp.bfloat16).astype(f32)
    split[0:3, :] = high
    split[3:6, :] = value - high
    chunk = 1024
    segs = conn.shape[1]
    groups = segs // SEG
    total = jnp.zeros((6 * groups, SEG), f32)
    low_row, high_row = iota((SEG, chunk), 0), iota((groups, chunk), 0)
    for end in range(2):
        for start in range(0, segs, chunk):
            at = slice(start, start + chunk)
            node = conn[end : end + 1, at]
            low = jnp.where(low_row == (node & (SEG - 1)), 1.0, 0.0).astype(jnp.bfloat16)
            mark = high_row == (node >> 7)
            parts = [
                jnp.where(mark, split[i : i + 1, at], 0.0).astype(jnp.bfloat16) for i in range(6)
            ]
            total = total + dot_nt(jnp.concatenate(parts, axis=0), low)
    for c in range(3):
        whole = total[c * groups : (c + 1) * groups] + total[(3 + c) * groups : (4 + c) * groups]
        for g in range(groups):
            out[c : c + 1, g * SEG : (g + 1) * SEG] = whole[g : g + 1, :]


def call(body, out_shape, in_specs, scratch, flops, size=48):
    return pl.pallas_call(
        body,
        out_shape=out_shape,
        in_specs=in_specs,
        out_specs=jax.tree.map(lambda _: VMEM, out_shape),
        scratch_shapes=scratch,
        compiler_params=pltpu.CompilerParams(vmem_limit_bytes=size << 20),
        cost_estimate=pl.CostEstimate(flops=flops, bytes_accessed=1 << 20, transcendentals=0),
    )


def local(
    seg_offset,
    tangent,
    burgers,
    box_matrix,
    applied_stress,
    far_kernel,
    block_cell,
    fetch_table,
    pair_list,
    image_shift,
    pair_count,
    node_conn,
):
    blocks = block_cell.shape[0]
    segs = seg_offset.shape[1]
    peers = lax.axis_size("bulk")
    slabs = lax.axis_size("slab")
    shape = lambda *dims: jax.ShapeDtypeStruct(dims, f32)
    table = pltpu.VMEM((16, segs), f32)
    acc = pltpu.VMEM((blocks, 3, SEG, SEG), f32)
    left_acc = pltpu.VMEM((blocks, 8, SEG), f32)

    send = call(
        pack_kernel, shape(peers, ROWS, SEG), [SMEM] * 4 + [VMEM] * 3, [table], 10**6, 16
    )(pair_list, image_shift, box_matrix, fetch_table, seg_offset, tangent, burgers)
    recv = lax.all_to_all(send, "bulk", 0, 0, tiled=True)

    moments_here = call(
        moment_kernel,
        shape(peers, CS, SEG),
        [SMEM] + [VMEM] * 3,
        [pltpu.VMEM((NM, segs), f32), pltpu.VMEM((CS, segs), f32)],
        10**9,
        16,
    )(block_cell, seg_offset, tangent, burgers)
    moments = jnp.sum(lax.all_to_all(moments_here, "bulk", 0, 0, tiled=True), axis=0)
    sources = [moments] + [
        lax.ppermute(moments, "slab", [(s, (s + k) % slabs) for s in range(slabs)])
        for k in range(1, slabs)
    ]

    near_own = call(
        own_kernel,
        shape(SEG, SEG),
        [SMEM] * 4 + [VMEM] * 3,
        [table, pltpu.VMEM((9, SEG, SEG), f32), acc, left_acc],
        10**9,
        24,
    )(pair_list, image_shift, box_matrix, pair_count, seg_offset, tangent, burgers)

    ret, near_pair = call(
        pair_kernel,
        (shape(peers, 16, SEG), shape(SEG, SEG)),
        [VMEM] * 4,
        [
            table,
            pltpu.VMEM((blocks, 9, SEG, SEG), f32),
            acc,
            pltpu.VMEM((peers, SEG), jnp.int32),
            pltpu.SMEM((peers, SEG), jnp.int32),
            pltpu.SemaphoreType.DMA,
        ],
        10**10,
        40,
    )(recv, seg_offset, tangent, burgers)
    back = lax.all_to_all(ret, "bulk", 0, 0, tiled=True)

    far = call(
        far_kernel_body,
        shape(3, segs),
        [SMEM] * 2 + [VMEM] * (4 + slabs),
        [
            pltpu.VMEM((slabs * CS + CS, SEG), f32),
            pltpu.VMEM((CS, slabs * CS * NM), f32),
            pltpu.VMEM((NM, segs), f32),
            pltpu.VMEM((CS, segs), f32),
        ],
        10**9,
        24,
    )(block_cell, applied_stress, far_kernel, seg_offset, tangent, burgers, *sources)

    return call(
        final_kernel,
        shape(3, segs),
        [SMEM] + [VMEM] * 5,
        [left_acc, pltpu.VMEM((8, segs), f32), pltpu.VMEM((8, segs), f32)],
        10**9,
        24,
    )(pair_list, back, near_own, near_pair, far, node_conn)


def solution(mesh):
    both = P(None, ("slab", "bulk"))
    in_specs = (
        both,
        both,
        both,
        P(),
        P(),
        P(),
        P(("slab", "bulk")),
        P(("slab", "bulk"), None),
        both,
        both,
        P(("slab", "bulk")),
        both,
    )
    return jax.shard_map(local, mesh=mesh, in_specs=in_specs, out_specs=both, check_vma=False)
```

```python
import functools

import jax
import jax.numpy as jnp
import numpy as np
from jax import lax
from jax.experimental import pallas as pl
from jax.experimental.pallas import tpu as pltpu
from jax.sharding import PartitionSpec as P

SEG = 128
CS = 16
NM = 84
SEND = 5
META = 45
MOMENTS = 48
ROWS = MOMENTS + CS
KAPPA = 0.2
CORE_SQ = 0.25
HIGH = lax.Precision.HIGHEST
VMEM = pl.BlockSpec(memory_space=pltpu.VMEM)
SMEM = pl.BlockSpec(memory_space=pltpu.SMEM)
f32 = jnp.float32


def exponents():
    return [(a, b, c) for a in range(7) for b in range(7 - a) for c in range(7 - a - b)]


def iota(shape, dim):
    return lax.broadcasted_iota(jnp.int32, shape, dim)


def lane_block(index):
    return pl.ds(pl.multiple_of(index * SEG, SEG), SEG)


def fill_table(table, off, tan, bur, diag, cross):
    b = [bur[i : i + 1, :] for i in range(3)]
    t = [tan[i : i + 1, :] for i in range(3)]
    table[0:3, :] = off[...]
    for i in range(3):
        table[3 + i : 4 + i, :] = diag * (b[i] * t[i])
    for row, (i, j) in enumerate(((0, 1), (0, 2), (1, 2))):
        table[6 + row : 7 + row, :] = cross * (b[i] * t[j] + b[j] * t[i])


def shift_of(box, shift, k):
    s = [shift[i, k].astype(f32) for i in range(3)]
    return [box[c, 0] * s[0] + box[c, 1] * s[1] + box[c, 2] * s[2] for c in range(3)]


def shift_rows(vec, shape):
    row = iota(shape, 0)
    return jnp.where(row == 0, vec[0], jnp.where(row == 1, vec[1], jnp.where(row == 2, vec[2], 0.0)))


def fetch_all(sources, targets, sems):
    copies = [
        pltpu.make_async_copy(source, target, sems.at[i])
        for i, (source, target) in enumerate(zip(sources, targets, strict=True))
    ]
    for copy in copies:
        copy.start()
    return copies


def pack_kernel(*refs):
    sources, send, scratch = refs[:8], refs[8], refs[9:]
    pairs, shift, box, fetch, cell, off, tan, bur, sems, table, phi, charged = scratch
    for copy in fetch_all(sources, scratch[:8], sems):
        copy.wait()
    fill_table(table, off, tan, bur, 2.0 * KAPPA, KAPPA)
    row, lane = iota((MOMENTS - META, SEG), 0), iota((MOMENTS - META, SEG), 1)
    moments = cell_moments(cell, off, tan, bur, phi, charged)

    def peer(p, carry):
        meta = jnp.zeros((MOMENTS - META, SEG), f32)
        for s in range(SEND):
            k = p * SEND + s
            at = lane_block(pairs[0, k])
            vec = shift_rows(shift_of(box, shift, k), (8, SEG))
            send[p, 8 * s : 8 * s + 8, :] = table[0:8, at] - vec
            send[p, 40 + s : 41 + s, :] = table[8:9, at]
            meta = jnp.where((row == 0) & (lane == s), fetch[s, p].astype(f32), meta)
        send[p, META:MOMENTS, :] = meta
        send[p, MOMENTS:ROWS, :] = moments
        return carry

    lax.fori_loop(0, send.shape[0], peer, 0)


def tile(left, col, acc, b):
    sums = [jnp.zeros((8, SEG), f32) for _ in range(3)]
    for r in range(SEG // 8):
        gap = [left[c] - col(c, r) for c in range(3)]
        dist = gap[0] * gap[0] + CORE_SQ + gap[1] * gap[1] + gap[2] * gap[2]
        coupling = left[3] * col(3, r)
        for c in range(4, 9):
            coupling = coupling + left[c] * col(c, r)
        inv = lax.rsqrt(dist)
        weight = coupling * (inv * inv * inv)
        for c in range(3):
            push = weight * gap[c]
            acc[b, c, 8 * r : 8 * r + 8, :] += push
            sums[c] = sums[c] + push
    return [jnp.sum(s, axis=0, keepdims=True) for s in sums]


def clear(acc):
    def block(b, carry):
        acc[b] = jnp.zeros(acc.shape[1:], f32)
        return carry

    lax.fori_loop(0, acc.shape[0], block, 0)


def own_kernel(pairs, shift, box, count, off, tan, bur, columns, acc, left_acc, table):
    fill_table(table, off, tan, bur, 1.0, 1.0)
    clear(acc)
    clear(left_acc)
    blocks = acc.shape[0]

    def block(b, carry):
        at = lane_block(b)
        for c in range(9):
            columns[b, c] = jnp.broadcast_to(table[c : c + 1, at], (SEG, SEG)).T
        return carry

    lax.fori_loop(0, blocks, block, 0)
    row = iota((8, SEG), 0)
    scale = jnp.where(row < 3, 1.0, jnp.where(row < 6, 2.0 * KAPPA, KAPPA))

    def pair(k, carry):
        a, b = pairs[0, k], pairs[1, k]
        at = lane_block(a)
        head = table[0:8, at] * scale - shift_rows(shift_of(box, shift, k), (8, SEG))
        left = [head[i : i + 1, :] for i in range(8)] + [table[8:9, at] * KAPPA]
        rows = tile(left, lambda c, r: columns[b, c, 8 * r : 8 * r + 8, :], acc, b)
        for c in range(3):
            left_acc[a, c : c + 1, :] += rows[c]
        return carry

    lax.fori_loop(pairs.shape[1] - blocks, count[0], pair, 0)


def pair_kernel(recv, columns, _, left_acc, ret, near, moments, acc, ids_vmem, ids, sem):
    peers = recv.shape[0]
    for p in range(peers):
        ids_vmem[p : p + 1, :] = recv[p, META : META + 1, :].astype(jnp.int32)
    copy = pltpu.make_async_copy(ids_vmem, ids, sem)
    copy.start()
    total = recv[0, MOMENTS:ROWS, :]
    for p in range(1, peers):
        total = total + recv[p, MOMENTS:ROWS, :]
    moments[...] = total
    copy.wait()

    def peer(p, carry):
        for s in range(SEND):
            b = ids[p, s]
            left = [recv[p, 8 * s + i : 8 * s + i + 1, :] for i in range(8)]
            left.append(recv[p, 40 + s : 41 + s, :])
            rows = tile(left, lambda c, r: columns[b, c, 8 * r : 8 * r + 8, :], acc, b)
            for c in range(3):
                ret[p, 3 * s + c : 3 * s + c + 1, :] = rows[c]
        ret[p, 15:16, :] = jnp.zeros((1, SEG), f32)
        return carry

    lax.fori_loop(0, peers, peer, 0)

    def fold(half, carry):
        rows = []
        for b in (2 * half, 2 * half + 1):
            for c in range(3):
                rows.append(left_acc[b, c : c + 1, :] - jnp.sum(acc[b, c].T, axis=0, keepdims=True))
            rows.append(jnp.zeros((1, SEG), f32))
        near[pl.ds(pl.multiple_of(8 * half, 8), 8), :] = jnp.concatenate(rows, axis=0)
        return carry

    lax.fori_loop(0, acc.shape[0] // 2, fold, 0)


def fill_phi(phi, off):
    powers = []
    for i in range(3):
        x = off[i : i + 1, :]
        made = [None, x]
        for _ in range(5):
            made.append(made[-1] * x)
        powers.append(made)
    pairs_of = {}
    for k, (a, b, c) in enumerate(exponents()):
        if (a, b) not in pairs_of:
            got = [p for p in (powers[0][a], powers[1][b]) if p is not None]
            pairs_of[a, b] = got[0] * got[1] if len(got) == 2 else got[0] if got else None
        value = pairs_of[a, b]
        if c:
            value = powers[2][c] if value is None else value * powers[2][c]
        phi[k : k + 1, :] = jnp.ones_like(powers[0][1]) if value is None else value


def dot_nt(left, right, precision=None):
    return lax.dot_general(
        left, right, (((1,), (1,)), ((), ())), precision=precision, preferred_element_type=f32
    )


def cell_moments(cell, off, tan, bur, phi, charged):
    fill_phi(phi, off)
    charge = jnp.sum(bur[...] * tan[...], axis=0, keepdims=True)
    row = iota((CS, SEG), 0)
    for b in range(cell.shape[0]):
        part = charge[:, b * SEG : (b + 1) * SEG]
        charged[:, b * SEG : (b + 1) * SEG] = jnp.where(row == cell[b], part, 0.0)
    part = dot_nt(charged[...], phi[...], HIGH)
    return jnp.concatenate([part, jnp.zeros((CS, SEG - NM), f32)], axis=1)


def far_kernel_body(cell, stress, operator, off, tan, bur, *rest):
    count = len(rest) - 5
    sources, (out, around, shifted, phi, pots) = rest[:count], rest[count:]
    cells = count * CS
    for q in range(count):
        around[q * CS : (q + 1) * CS, :] = sources[(count - q) % count][...]
    around[cells : cells + CS, :] = sources[0][...]
    shifted[:, 0:NM] = jnp.zeros((CS, NM), f32)
    for o in range(1, cells):
        shifted[:, o * NM : (o + 1) * NM] = around[cells - o : cells - o + CS, 0:NM]
    local_exp = dot_nt(shifted[...], operator[...], HIGH)
    fill_phi(phi, off)
    pots[...] = lax.dot_general(
        local_exp, phi[...], (((1,), (0,)), ((), ())), precision=HIGH, preferred_element_type=f32
    )
    b = [bur[i : i + 1, :] for i in range(3)]
    t = [tan[i : i + 1, :] for i in range(3)]
    sym = [[0.5 * (stress[i, j] + stress[j, i]) for j in range(3)] for i in range(3)]
    trac = [sym[i][0] * b[0] + sym[i][1] * b[1] + sym[i][2] * b[2] for i in range(3)]
    for i in range(3):
        j, k = (i + 1) % 3, (i + 2) % 3
        out[i : i + 1, :] = trac[j] * t[k] - trac[k] * t[j]
    row = iota((CS, SEG), 0)
    for block in range(cell.shape[0]):
        at = slice(block * SEG, (block + 1) * SEG)
        mine = jnp.where(row == cell[block], pots[:, at], 0.0)
        out[:, at] += jnp.sum(mine, axis=0, keepdims=True) * bur[:, at]


def final_kernel(pairs, back, near_all, far, conn, out, left_acc, force, split):
    clear(left_acc)

    def peer(p, carry):
        for s in range(SEND):
            a = pairs[0, p * SEND + s]
            left_acc[a, 0:3, :] += back[p, 3 * s : 3 * s + 3, :]
        return carry

    lax.fori_loop(0, back.shape[0], peer, 0)
    for b in range(left_acc.shape[0]):
        at = slice(b * SEG, (b + 1) * SEG)
        near = near_all[4 * b : 4 * b + 3, :]
        force[0:3, at] = 0.5 * (far[:, at] + near + left_acc[b, 0:3, :])
    value = force[0:3, :]
    high = value.astype(jnp.bfloat16).astype(f32)
    split[0:3, :] = high
    split[3:6, :] = value - high
    chunk = 1024
    segs = conn.shape[1]
    groups = segs // SEG
    total = jnp.zeros((6 * groups, SEG), f32)
    low_row, high_row = iota((SEG, chunk), 0), iota((groups, chunk), 0)
    for end in range(2):
        for start in range(0, segs, chunk):
            at = slice(start, start + chunk)
            node = conn[end : end + 1, at]
            low = jnp.where(low_row == (node & (SEG - 1)), 1.0, 0.0).astype(jnp.bfloat16)
            mark = high_row == (node >> 7)
            parts = [
                jnp.where(mark, split[i : i + 1, at], 0.0).astype(jnp.bfloat16) for i in range(6)
            ]
            total = total + dot_nt(jnp.concatenate(parts, axis=0), low)
    for c in range(3):
        whole = total[c * groups : (c + 1) * groups] + total[(3 + c) * groups : (4 + c) * groups]
        for g in range(groups):
            out[c : c + 1, g * SEG : (g + 1) * SEG] = whole[g : g + 1, :]


def call(body, out_shape, in_specs, scratch, flops, size, aliases=None):
    return pl.pallas_call(
        body,
        out_shape=out_shape,
        in_specs=in_specs,
        out_specs=jax.tree.map(lambda _: VMEM, out_shape),
        scratch_shapes=scratch,
        input_output_aliases=aliases or {},
        compiler_params=pltpu.CompilerParams(vmem_limit_bytes=size << 20),
        cost_estimate=pl.CostEstimate(flops=flops, bytes_accessed=1 << 20, transcendentals=0),
    )


def local(
    seg_offset,
    tangent,
    burgers,
    box_matrix,
    applied_stress,
    far_kernel,
    block_cell,
    fetch_table,
    pair_list,
    image_shift,
    pair_count,
    node_conn,
):
    blocks = block_cell.shape[0]
    segs = seg_offset.shape[1]
    peers = lax.axis_size("bulk")
    slabs = lax.axis_size("slab")
    shape = lambda *dims: jax.ShapeDtypeStruct(dims, f32)
    table = pltpu.VMEM((16, segs), f32)

    raw = [pair_list, image_shift, box_matrix, fetch_table.T, block_cell]
    segments = [seg_offset, tangent, burgers]
    send = call(
        pack_kernel,
        shape(peers, ROWS, SEG),
        [pl.BlockSpec(memory_space=pltpu.HBM)] * 8,
        [pltpu.SMEM(x.shape, x.dtype) for x in raw]
        + [pltpu.VMEM(x.shape, x.dtype) for x in segments]
        + [pltpu.SemaphoreType.DMA((8,))]
        + [table, pltpu.VMEM((NM, segs), f32), pltpu.VMEM((CS, segs), f32)],
        10**6,
        60,
    )(*raw, *segments)
    recv = lax.all_to_all(send, "bulk", 0, 0, tiled=True)

    columns, acc, left_acc = call(
        own_kernel,
        (shape(blocks, 9, SEG, SEG), shape(blocks, 3, SEG, SEG), shape(blocks, 8, SEG)),
        [SMEM] * 4 + [VMEM] * 3,
        [table],
        10**9,
        8,
    )(pair_list, image_shift, box_matrix, pair_count, *segments)

    ret, near, moments, _ = call(
        pair_kernel,
        (shape(peers, 16, SEG), shape(SEG, SEG), shape(CS, SEG), shape(blocks, 3, SEG, SEG)),
        [VMEM] * 4,
        [
            pltpu.VMEM((peers, SEG), jnp.int32),
            pltpu.SMEM((peers, SEG), jnp.int32),
            pltpu.SemaphoreType.DMA,
        ],
        10**10,
        8,
        {2: 3},
    )(recv, columns, acc, left_acc)
    back = lax.all_to_all(ret, "bulk", 0, 0, tiled=True)
    sources = [moments] + [
        lax.ppermute(moments, "slab", [(s, (s + k) % slabs) for s in range(slabs)])
        for k in range(1, slabs)
    ]

    far = call(
        far_kernel_body,
        shape(3, segs),
        [SMEM] * 2 + [VMEM] * (4 + slabs),
        [
            pltpu.VMEM((slabs * CS + CS, SEG), f32),
            pltpu.VMEM((CS, slabs * CS * NM), f32),
            pltpu.VMEM((NM, segs), f32),
            pltpu.VMEM((CS, segs), f32),
        ],
        10**9,
        24,
    )(block_cell, applied_stress, far_kernel, seg_offset, tangent, burgers, *sources)

    return call(
        final_kernel,
        shape(3, segs),
        [SMEM] + [VMEM] * 4,
        [pltpu.VMEM((blocks, 8, SEG), f32), pltpu.VMEM((8, segs), f32), pltpu.VMEM((8, segs), f32)],
        10**9,
        24,
    )(pair_list, back, near, far, node_conn)


def solution(mesh):
    both = P(None, ("slab", "bulk"))
    in_specs = (
        both,
        both,
        both,
        P(),
        P(),
        P(),
        P(("slab", "bulk")),
        P(("slab", "bulk"), None),
        both,
        both,
        P(("slab", "bulk")),
        both,
    )
    return jax.shard_map(local, mesh=mesh, in_specs=in_specs, out_specs=both, check_vma=False)
```

```python
import functools

import jax
import jax.numpy as jnp
from jax import lax
from jax.experimental import pallas as pl
from jax.experimental.pallas import tpu as pltpu
from jax.sharding import PartitionSpec as P

SEG = 128
CS = 16
NM = 84
SEND = 5
META = 45
MOMENTS = 48
ROWS = MOMENTS + CS
FEATURES = 48
KAPPA = 0.2
CORE_SQ = 0.25
HIGH = lax.Precision.HIGHEST
VMEM = pl.BlockSpec(memory_space=pltpu.VMEM)
HBM = pl.BlockSpec(memory_space=pltpu.HBM)
SMEM = pl.BlockSpec(memory_space=pltpu.SMEM)
f32 = jnp.float32
bf16 = jnp.bfloat16


def exponents():
    return [(a, b, c) for a in range(7) for b in range(7 - a) for c in range(7 - a - b)]


def iota(shape, dim):
    return lax.broadcasted_iota(jnp.int32, shape, dim)


def lane_block(index):
    return pl.ds(pl.multiple_of(index * SEG, SEG), SEG)


def fill_table(table, off, tan, bur, diag, cross):
    b = [bur[i : i + 1, :] for i in range(3)]
    t = [tan[i : i + 1, :] for i in range(3)]
    table[0:3, :] = off[...]
    for i in range(3):
        table[3 + i : 4 + i, :] = diag * (b[i] * t[i])
    for row, (i, j) in enumerate(((0, 1), (0, 2), (1, 2))):
        table[6 + row : 7 + row, :] = cross * (b[i] * t[j] + b[j] * t[i])


def shift_of(box, shift, k):
    s = [shift[i, k].astype(f32) for i in range(3)]
    return [box[c, 0] * s[0] + box[c, 1] * s[1] + box[c, 2] * s[2] for c in range(3)]


def shift_rows(vec, shape):
    row = iota(shape, 0)
    return jnp.where(row == 0, vec[0], jnp.where(row == 1, vec[1], jnp.where(row == 2, vec[2], 0.0)))


def fetch_all(sources, targets, sems):
    copies = [
        pltpu.make_async_copy(source, target, sems.at[i])
        for i, (source, target) in enumerate(zip(sources, targets, strict=True))
    ]
    for copy in copies:
        copy.start()
    return copies


def pack_kernel(*refs):
    sources, send, scratch = refs[:8], refs[8], refs[9:]
    pairs, shift, box, fetch, cell, off, tan, bur, sems, table, phi, charged = scratch
    for copy in fetch_all(sources, scratch[:8], sems):
        copy.wait()
    fill_table(table, off, tan, bur, 2.0 * KAPPA, KAPPA)
    row, lane = iota((MOMENTS - META, SEG), 0), iota((MOMENTS - META, SEG), 1)
    moments = cell_moments(cell, off, tan, bur, phi, charged)

    def peer(p, carry):
        meta = jnp.zeros((MOMENTS - META, SEG), f32)
        for s in range(SEND):
            k = p * SEND + s
            at = lane_block(pairs[0, k])
            vec = shift_rows(shift_of(box, shift, k), (8, SEG))
            send[p, 8 * s : 8 * s + 8, :] = table[0:8, at] - vec
            send[p, 40 + s : 41 + s, :] = table[8:9, at]
            meta = jnp.where((row == 0) & (lane == s), fetch[s, p].astype(f32), meta)
        send[p, META:MOMENTS, :] = meta
        send[p, MOMENTS:ROWS, :] = moments
        return carry

    lax.fori_loop(0, send.shape[0], peer, 0)


def split(value):
    high = value.astype(bf16).astype(f32)
    rest = value - high
    mid = rest.astype(bf16).astype(f32)
    return high, mid, (rest - mid).astype(bf16).astype(f32)


def fill_features(table, features):
    row = iota((8, SEG), 0)
    first = row < 3

    def block(b, carry):
        at = lane_block(b)
        high, mid, low = split(table[0:8, at])
        last_high, last_mid, _ = split(table[8:9, at])
        groups = [jnp.where(first, 1.0, high)] * 2
        groups.append(
            jnp.where(first, 1.0, jnp.where(row < 5, last_high, jnp.where(row == 5, last_mid, 0.0)))
        )
        groups.append(jnp.where(first, high, mid))
        groups.append(jnp.concatenate([mid[0:3], low[0:3], jnp.zeros((2, SEG), f32)], axis=0))
        groups.append(jnp.zeros((SEG - 40, SEG), f32))
        turned = jnp.concatenate(groups, axis=0).T
        features[b] = turned[:, 0:FEATURES].astype(bf16)
        return carry

    lax.fori_loop(0, features.shape[0], block, 0)


def weights(head, last):
    row = iota((8, SEG), 0)
    high, mid, low = split(head)
    last_high, last_mid, _ = split(last)
    none = jnp.zeros((8, SEG), f32)
    columns = []
    for i in range(3):
        own = row == i
        parts = [jnp.where(own, part, 0.0) for part in (high, mid, low, -1.0)]
        parts += [jnp.where(own | (row == i + 3), -1.0, 0.0), none]
        columns.append(jnp.concatenate(parts, axis=0))
    tail = row >= 3
    high = jnp.where(tail, high, 0.0)
    edge = jnp.where((row == 3) | (row == 5), last_high, jnp.where(row == 4, last_mid, 0.0))
    columns.append(
        jnp.concatenate([high, jnp.where(tail, mid, 0.0), edge, high, none, none], axis=0)
    )
    return jnp.concatenate(columns, axis=1).astype(bf16)


def tile(head, last, features, acc, b):
    both = weights(head, last)
    sums = [jnp.zeros((8, SEG), f32) for _ in range(3)]
    step = 32
    for start in range(0, SEG, step):
        at = slice(start, start + step)
        made = jnp.dot(features[b, at, :], both, preferred_element_type=f32)
        gap = [made[:, i * SEG : (i + 1) * SEG] for i in range(3)]
        dist = gap[0] * gap[0] + CORE_SQ + gap[1] * gap[1] + gap[2] * gap[2]
        inv = lax.rsqrt(dist)
        weight = made[:, 3 * SEG :] * (inv * inv * inv)
        for c in range(3):
            push = weight * gap[c]
            acc[b, c, at, :] += push
            for r in range(0, step, 8):
                sums[c] = sums[c] + push[r : r + 8]
    return [jnp.sum(part, axis=0, keepdims=True) for part in sums]


def fold(acc, near, others):
    def pair(half, carry):
        at = pl.ds(pl.multiple_of(8 * half, 8), 8)
        rows = []
        for b in (2 * half, 2 * half + 1):
            rows += [jnp.sum(acc[b, c].T, axis=0, keepdims=True) for c in range(3)]
            rows.append(jnp.zeros((1, SEG), f32))
        near[at, :] = others[at, :] - jnp.concatenate(rows, axis=0)
        return carry

    lax.fori_loop(0, acc.shape[0] // 2, pair, 0)


def clear(acc):
    def block(b, carry):
        acc[b] = jnp.zeros(acc.shape[1:], f32)
        return carry

    lax.fori_loop(0, acc.shape[0], block, 0)


def own_kernel(*refs):
    sources, (features, near), scratch = refs[:7], refs[7:9], refs[9:]
    pairs, shift, box, count, off, tan, bur, sems, table, acc, left_acc = scratch
    copies = fetch_all(sources, scratch[:7], sems)
    clear(acc)
    left_acc[...] = jnp.zeros_like(left_acc)
    for copy in copies:
        copy.wait()
    fill_table(table, off, tan, bur, 1.0, 1.0)
    fill_features(table, features)
    blocks = acc.shape[0]
    row = iota((8, SEG), 0)
    scale = jnp.where(row < 3, 1.0, jnp.where(row < 6, 2.0 * KAPPA, KAPPA))

    def pair(k, carry):
        a, b = pairs[0, k], pairs[1, k]
        at = lane_block(a)
        head = table[0:8, at] * scale - shift_rows(shift_of(box, shift, k), (8, SEG))
        rows = tile(head, table[8:9, at] * KAPPA, features, acc, b)
        for c in range(3):
            left_acc[a, c : c + 1, :] += rows[c]
        return carry

    lax.fori_loop(pairs.shape[1] - blocks, count[0], pair, 0)
    for b in range(blocks):
        near[4 * b : 4 * b + 4, :] = left_acc[b, 0:4, :]
    fold(acc, near, near)


def pair_kernel(recv, features, near_own, ret, near, acc, ids_vmem, ids, sem):
    peers = recv.shape[0]
    for p in range(peers):
        ids_vmem[p : p + 1, :] = recv[p, META : META + 1, :].astype(jnp.int32)
    copy = pltpu.make_async_copy(ids_vmem, ids, sem)
    copy.start()
    clear(acc)
    copy.wait()

    def peer(p, carry):
        for s in range(SEND):
            head, last = recv[p, 8 * s : 8 * s + 8, :], recv[p, 40 + s : 41 + s, :]
            rows = tile(head, last, features, acc, ids[p, s])
            for c in range(3):
                ret[p, 3 * s + c : 3 * s + c + 1, :] = rows[c]
        ret[p, 15:16, :] = jnp.zeros((1, SEG), f32)
        return carry

    lax.fori_loop(0, peers, peer, 0)
    fold(acc, near, near_own)


def fill_phi(phi, off):
    powers = []
    for i in range(3):
        x = off[i : i + 1, :]
        made = [None, x]
        for _ in range(5):
            made.append(made[-1] * x)
        powers.append(made)
    pairs_of = {}
    for k, (a, b, c) in enumerate(exponents()):
        if (a, b) not in pairs_of:
            got = [p for p in (powers[0][a], powers[1][b]) if p is not None]
            pairs_of[a, b] = got[0] * got[1] if len(got) == 2 else got[0] if got else None
        value = pairs_of[a, b]
        if c:
            value = powers[2][c] if value is None else value * powers[2][c]
        phi[k : k + 1, :] = jnp.ones_like(powers[0][1]) if value is None else value


def dot_nt(left, right, precision=None):
    return lax.dot_general(
        left, right, (((1,), (1,)), ((), ())), precision=precision, preferred_element_type=f32
    )


def cell_moments(cell, off, tan, bur, phi, charged):
    fill_phi(phi, off)
    charge = jnp.sum(bur[...] * tan[...], axis=0, keepdims=True)
    row = iota((CS, SEG), 0)
    for b in range(cell.shape[0]):
        part = charge[:, b * SEG : (b + 1) * SEG]
        charged[:, b * SEG : (b + 1) * SEG] = jnp.where(row == cell[b], part, 0.0)
    part = dot_nt(charged[...], phi[...], HIGH)
    return jnp.concatenate([part, jnp.zeros((CS, SEG - NM), f32)], axis=1)


def far_kernel_body(count, *refs):
    raw, sources, out, scratch = refs[:6], refs[6 : 6 + count], refs[6 + count], refs[7 + count :]
    cell, stress, off, tan, bur, operator, sems, around, shifted, phi, pots = scratch
    copies = fetch_all(raw, scratch[:6], sems)
    cells = count * CS
    for q in range(count):
        around[q * CS : (q + 1) * CS, :] = sources[(count - q) % count][...]
    around[cells : cells + CS, :] = sources[0][...]
    shifted[:, 0:NM] = jnp.zeros((CS, NM), f32)
    for o in range(1, cells):
        shifted[:, o * NM : (o + 1) * NM] = around[cells - o : cells - o + CS, 0:NM]
    for copy in copies[:5]:
        copy.wait()
    fill_phi(phi, off)
    copies[5].wait()
    local_exp = dot_nt(shifted[...], operator[...], HIGH)
    pots[...] = lax.dot_general(
        local_exp, phi[...], (((1,), (0,)), ((), ())), precision=HIGH, preferred_element_type=f32
    )
    b = [bur[i : i + 1, :] for i in range(3)]
    t = [tan[i : i + 1, :] for i in range(3)]
    sym = [[0.5 * (stress[i, j] + stress[j, i]) for j in range(3)] for i in range(3)]
    trac = [sym[i][0] * b[0] + sym[i][1] * b[1] + sym[i][2] * b[2] for i in range(3)]
    for i in range(3):
        j, k = (i + 1) % 3, (i + 2) % 3
        out[i : i + 1, :] = trac[j] * t[k] - trac[k] * t[j]
    row = iota((CS, SEG), 0)
    for block in range(cell.shape[0]):
        at = slice(block * SEG, (block + 1) * SEG)
        mine = jnp.where(row == cell[block], pots[:, at], 0.0)
        out[:, at] += jnp.sum(mine, axis=0, keepdims=True) * bur[:, at]


def final_kernel(pairs, back, near_all, far, conn, out, left_acc, force, halves):
    clear(left_acc)

    def peer(p, carry):
        for s in range(SEND):
            a = pairs[0, p * SEND + s]
            left_acc[a, 0:3, :] += back[p, 3 * s : 3 * s + 3, :]
        return carry

    lax.fori_loop(0, back.shape[0], peer, 0)
    for b in range(left_acc.shape[0]):
        at = slice(b * SEG, (b + 1) * SEG)
        near = near_all[4 * b : 4 * b + 3, :]
        force[0:3, at] = 0.5 * (far[:, at] + near + left_acc[b, 0:3, :])
    value = force[0:3, :]
    high = value.astype(bf16).astype(f32)
    halves[0:3, :] = high
    halves[3:6, :] = value - high
    chunk = 1024
    segs = conn.shape[1]
    groups = segs // SEG
    total = jnp.zeros((6 * groups, SEG), f32)
    low_row, high_row = iota((SEG, chunk), 0), iota((groups, chunk), 0)
    for end in range(2):
        for start in range(0, segs, chunk):
            at = slice(start, start + chunk)
            node = conn[end : end + 1, at]
            low = jnp.where(low_row == (node & (SEG - 1)), 1.0, 0.0).astype(bf16)
            mark = high_row == (node >> 7)
            parts = [
                jnp.where(mark, halves[i : i + 1, at], 0.0).astype(bf16) for i in range(6)
            ]
            total = total + dot_nt(jnp.concatenate(parts, axis=0), low)
    for c in range(3):
        whole = total[c * groups : (c + 1) * groups] + total[(3 + c) * groups : (4 + c) * groups]
        for g in range(groups):
            out[c : c + 1, g * SEG : (g + 1) * SEG] = whole[g : g + 1, :]


def call(body, out_shape, in_specs, scratch, flops, size):
    return pl.pallas_call(
        body,
        out_shape=out_shape,
        in_specs=in_specs,
        out_specs=jax.tree.map(lambda _: VMEM, out_shape),
        scratch_shapes=scratch,
        compiler_params=pltpu.CompilerParams(vmem_limit_bytes=size << 20),
        cost_estimate=pl.CostEstimate(flops=flops, bytes_accessed=1 << 20, transcendentals=0),
    )


def local(
    seg_offset,
    tangent,
    burgers,
    box_matrix,
    applied_stress,
    far_kernel,
    block_cell,
    fetch_table,
    pair_list,
    image_shift,
    pair_count,
    node_conn,
):
    blocks = block_cell.shape[0]
    segs = seg_offset.shape[1]
    peers = lax.axis_size("bulk")
    slabs = lax.axis_size("slab")
    shape = lambda *dims: jax.ShapeDtypeStruct(dims, f32)
    table = pltpu.VMEM((16, segs), f32)

    raw = [pair_list, image_shift, box_matrix, fetch_table.T, block_cell]
    segments = [seg_offset, tangent, burgers]
    send = call(
        pack_kernel,
        shape(peers, ROWS, SEG),
        [HBM] * 8,
        [pltpu.SMEM(x.shape, x.dtype) for x in raw]
        + [pltpu.VMEM(x.shape, x.dtype) for x in segments]
        + [pltpu.SemaphoreType.DMA((8,))]
        + [table, pltpu.VMEM((NM, segs), f32), pltpu.VMEM((CS, segs), f32)],
        10**6,
        60,
    )(*raw, *segments)
    recv = lax.all_to_all(send, "bulk", 0, 0, tiled=True)

    raw = [pair_list, image_shift, box_matrix, pair_count]
    features, near_own = call(
        own_kernel,
        (jax.ShapeDtypeStruct((blocks, SEG, FEATURES), bf16), shape(SEG, SEG)),
        [HBM] * 7,
        [pltpu.SMEM(x.shape, x.dtype) for x in raw]
        + [pltpu.VMEM(x.shape, x.dtype) for x in segments]
        + [pltpu.SemaphoreType.DMA((7,)), table]
        + [pltpu.VMEM((blocks, 3, SEG, SEG), f32), pltpu.VMEM((blocks, 8, SEG), f32)],
        10**9,
        60,
    )(*raw, *segments)

    moments = jnp.sum(recv[:, MOMENTS:, :], axis=0)
    sources = [moments] + [
        lax.ppermute(moments, "slab", [(s, (s + k) % slabs) for s in range(slabs)])
        for k in range(1, slabs)
    ]

    ret, near = call(
        pair_kernel,
        (shape(peers, 16, SEG), shape(SEG, SEG)),
        [VMEM] * 3,
        [
            pltpu.VMEM((blocks, 3, SEG, SEG), f32),
            pltpu.VMEM((peers, SEG), jnp.int32),
            pltpu.SMEM((peers, SEG), jnp.int32),
            pltpu.SemaphoreType.DMA,
        ],
        10**10,
        16,
    )(recv, features, near_own)
    back = lax.all_to_all(ret, "bulk", 0, 0, tiled=True)
    raw = [block_cell, applied_stress]
    far = call(
        functools.partial(far_kernel_body, slabs),
        shape(3, segs),
        [HBM] * 6 + [VMEM] * slabs,
        [pltpu.SMEM(x.shape, x.dtype) for x in raw]
        + [pltpu.VMEM(x.shape, x.dtype) for x in segments + [far_kernel]]
        + [
            pltpu.SemaphoreType.DMA((6,)),
            pltpu.VMEM((slabs * CS + CS, SEG), f32),
            pltpu.VMEM((CS, slabs * CS * NM), f32),
            pltpu.VMEM((NM, segs), f32),
            pltpu.VMEM((CS, segs), f32),
        ],
        10**9,
        61,
    )(*raw, *segments, far_kernel, *sources)

    return call(
        final_kernel,
        shape(3, segs),
        [SMEM] + [VMEM] * 4,
        [pltpu.VMEM((blocks, 8, SEG), f32), pltpu.VMEM((8, segs), f32), pltpu.VMEM((8, segs), f32)],
        10**9,
        24,
    )(pair_list, back, near, far, node_conn)


def solution(mesh):
    both = P(None, ("slab", "bulk"))
    in_specs = (
        both,
        both,
        both,
        P(),
        P(),
        P(),
        P(("slab", "bulk")),
        P(("slab", "bulk"), None),
        both,
        both,
        P(("slab", "bulk")),
        both,
    )
    return jax.shard_map(local, mesh=mesh, in_specs=in_specs, out_specs=both, check_vma=False)
```

```python
import jax
import jax.numpy as jnp
from jax import lax
from jax.experimental import pallas as pl
from jax.experimental.pallas import tpu as pltpu
from jax.sharding import PartitionSpec as P

SEG = 128
CS = 16
NM = 84
SEND = 5
LAST = 40
MOMENTS = 45
ROWS = 56
GROUP = 11
META = 112
FEATURES = 48
KAPPA = 0.2
CORE_SQ = 0.25
HIGH = lax.Precision.HIGHEST
VMEM = pl.BlockSpec(memory_space=pltpu.VMEM)
HBM = pl.BlockSpec(memory_space=pltpu.HBM)
SMEM = pl.BlockSpec(memory_space=pltpu.SMEM)
f32 = jnp.float32
bf16 = jnp.bfloat16


def exponents():
    return [(a, b, c) for a in range(7) for b in range(7 - a) for c in range(7 - a - b)]


def iota(shape, dim):
    return lax.broadcasted_iota(jnp.int32, shape, dim)


def lane_block(index):
    return pl.ds(pl.multiple_of(index * SEG, SEG), SEG)


def fill_table(table, off, tan, bur, diag, cross):
    b = [bur[i : i + 1, :] for i in range(3)]
    t = [tan[i : i + 1, :] for i in range(3)]
    table[0:3, :] = off[...]
    for i in range(3):
        table[3 + i : 4 + i, :] = diag * (b[i] * t[i])
    for row, (i, j) in enumerate(((0, 1), (0, 2), (1, 2))):
        table[6 + row : 7 + row, :] = cross * (b[i] * t[j] + b[j] * t[i])


def shift_of(box, shift, k):
    s = [shift[i, k].astype(f32) for i in range(3)]
    return [box[c, 0] * s[0] + box[c, 1] * s[1] + box[c, 2] * s[2] for c in range(3)]


def shift_rows(vec, shape):
    row = iota(shape, 0)
    return jnp.where(row == 0, vec[0], jnp.where(row == 1, vec[1], jnp.where(row == 2, vec[2], 0.0)))


def fetch_all(sources, targets, sems):
    copies = [
        pltpu.make_async_copy(source, target, sems.at[i])
        for i, (source, target) in enumerate(zip(sources, targets, strict=True))
    ]
    for copy in copies:
        copy.start()
    return copies


def pack_kernel(*refs):
    sources, send, scratch = refs[:8], refs[8], refs[9:]
    pairs, shift, box, fetch, cell, off, tan, bur, sems, table, phi, charged = scratch
    for copy in fetch_all(sources, scratch[:8], sems):
        copy.wait()
    fill_table(table, off, tan, bur, 2.0 * KAPPA, KAPPA)
    packed = cell_moments(cell, off, tan, bur, phi, charged)
    row, lane = iota((ROWS - LAST, SEG), 0), iota((ROWS - LAST, SEG), 1)

    def peer(p, carry):
        rest = packed
        for s in range(SEND):
            k = p * SEND + s
            at = lane_block(pairs[0, k])
            vec = shift_rows(shift_of(box, shift, k), (8, SEG))
            send[p, 8 * s : 8 * s + 8, :] = table[0:8, at] - vec
            rest = jnp.where(row == s, table[8:9, at], rest)
            mine = (row == ROWS - LAST - 1) & (lane == META + s)
            rest = jnp.where(mine, fetch[s, p].astype(f32), rest)
        send[p, LAST:ROWS, :] = rest
        return carry

    lax.fori_loop(0, send.shape[0], peer, 0)


def split(value):
    high = value.astype(bf16).astype(f32)
    rest = value - high
    mid = rest.astype(bf16).astype(f32)
    return high, mid, (rest - mid).astype(bf16).astype(f32)


def fill_features(table, features):
    row = iota((8, SEG), 0)
    first = row < 3

    def block(b, carry):
        at = lane_block(b)
        high, mid, low = split(table[0:8, at])
        last_high, last_mid, _ = split(table[8:9, at])
        groups = [jnp.where(first, 1.0, high)] * 2
        groups.append(
            jnp.where(first, 1.0, jnp.where(row < 5, last_high, jnp.where(row == 5, last_mid, 0.0)))
        )
        groups.append(jnp.where(first, high, mid))
        groups.append(jnp.concatenate([mid[0:3], low[0:3], jnp.zeros((2, SEG), f32)], axis=0))
        groups.append(jnp.zeros((SEG - 40, SEG), f32))
        turned = jnp.concatenate(groups, axis=0).T
        features[b] = turned[:, 0:FEATURES].astype(bf16)
        return carry

    lax.fori_loop(0, features.shape[0], block, 0)


def weights(head, last):
    row = iota((8, SEG), 0)
    high, mid, low = split(head)
    last_high, last_mid, _ = split(last)
    none = jnp.zeros((8, SEG), f32)
    columns = []
    for i in range(3):
        own = row == i
        parts = [jnp.where(own, part, 0.0) for part in (high, mid, low, -1.0)]
        parts += [jnp.where(own | (row == i + 3), -1.0, 0.0), none]
        columns.append(jnp.concatenate(parts, axis=0))
    tail = row >= 3
    high = jnp.where(tail, high, 0.0)
    edge = jnp.where((row == 3) | (row == 5), last_high, jnp.where(row == 4, last_mid, 0.0))
    columns.append(
        jnp.concatenate([high, jnp.where(tail, mid, 0.0), edge, high, none, none], axis=0)
    )
    return jnp.concatenate(columns, axis=1).astype(bf16)


def tile(head, last, features, acc, b):
    both = weights(head, last)
    sums = [jnp.zeros((8, SEG), f32) for _ in range(3)]
    step = 32
    for start in range(0, SEG, step):
        at = slice(start, start + step)
        made = jnp.dot(features[b, at, :], both, preferred_element_type=f32)
        gap = [made[:, i * SEG : (i + 1) * SEG] for i in range(3)]
        dist = gap[0] * gap[0] + CORE_SQ + gap[1] * gap[1] + gap[2] * gap[2]
        inv = lax.rsqrt(dist)
        weight = made[:, 3 * SEG :] * (inv * inv * inv)
        for c in range(3):
            push = weight * gap[c]
            acc[b, c, at, :] += push
            for r in range(0, step, 8):
                sums[c] = sums[c] + push[r : r + 8]
    return [jnp.sum(part, axis=0, keepdims=True) for part in sums]


def fold(acc, near, others):
    def pair(half, carry):
        at = pl.ds(pl.multiple_of(8 * half, 8), 8)
        rows = []
        for b in (2 * half, 2 * half + 1):
            rows += [jnp.sum(acc[b, c].T, axis=0, keepdims=True) for c in range(3)]
            rows.append(jnp.zeros((1, SEG), f32))
        near[at, :] = others[at, :] - jnp.concatenate(rows, axis=0)
        return carry

    lax.fori_loop(0, acc.shape[0] // 2, pair, 0)


def clear(acc):
    def block(b, carry):
        acc[b] = jnp.zeros(acc.shape[1:], f32)
        return carry

    lax.fori_loop(0, acc.shape[0], block, 0)


def own_kernel(pairs, shift, box, count, off, tan, bur, features, near, table, acc, left_acc):
    clear(acc)
    left_acc[...] = jnp.zeros_like(left_acc)
    fill_table(table, off, tan, bur, 1.0, 1.0)
    fill_features(table, features)
    blocks = acc.shape[0]
    row = iota((8, SEG), 0)
    scale = jnp.where(row < 3, 1.0, jnp.where(row < 6, 2.0 * KAPPA, KAPPA))

    def pair(k, carry):
        a, b = pairs[0, k], pairs[1, k]
        at = lane_block(a)
        head = table[0:8, at] * scale - shift_rows(shift_of(box, shift, k), (8, SEG))
        rows = tile(head, table[8:9, at] * KAPPA, features, acc, b)
        for c in range(3):
            left_acc[a, c : c + 1, :] += rows[c]
        return carry

    lax.fori_loop(pairs.shape[1] - blocks, count[0], pair, 0)
    for b in range(blocks):
        near[4 * b : 4 * b + 4, :] = left_acc[b, 0:4, :]
    fold(acc, near, near)


def pair_kernel(recv, features, near_own, ret, near, acc, ids_vmem, ids, sem):
    peers = recv.shape[0]
    for p in range(peers):
        ids_vmem[p : p + 1, :] = recv[p, ROWS - 1 : ROWS, :].astype(jnp.int32)
    copy = pltpu.make_async_copy(ids_vmem, ids, sem)
    copy.start()
    clear(acc)
    copy.wait()

    def peer(p, carry):
        for s in range(SEND):
            head, last = recv[p, 8 * s : 8 * s + 8, :], recv[p, LAST + s : LAST + s + 1, :]
            rows = tile(head, last, features, acc, ids[p, META + s])
            for c in range(3):
                ret[p, 3 * s + c : 3 * s + c + 1, :] = rows[c]
        ret[p, 15:16, :] = jnp.zeros((1, SEG), f32)
        return carry

    lax.fori_loop(0, peers, peer, 0)
    fold(acc, near, near_own)


def fill_phi(phi, off):
    powers = []
    for i in range(3):
        x = off[i : i + 1, :]
        made = [None, x]
        for _ in range(5):
            made.append(made[-1] * x)
        powers.append(made)
    pairs_of = {}
    for k, (a, b, c) in enumerate(exponents()):
        if (a, b) not in pairs_of:
            got = [p for p in (powers[0][a], powers[1][b]) if p is not None]
            pairs_of[a, b] = got[0] * got[1] if len(got) == 2 else got[0] if got else None
        value = pairs_of[a, b]
        if c:
            value = powers[2][c] if value is None else value * powers[2][c]
        phi[k : k + 1, :] = jnp.ones_like(powers[0][1]) if value is None else value


def dot_nt(left, right, precision=None):
    return lax.dot_general(
        left, right, (((1,), (1,)), ((), ())), precision=precision, preferred_element_type=f32
    )


def cell_moments(cell, off, tan, bur, phi, charged):
    fill_phi(phi, off)
    charge = jnp.sum(bur[...] * tan[...], axis=0, keepdims=True)
    row = iota((CS, SEG), 0)
    for b in range(cell.shape[0]):
        part = charge[:, b * SEG : (b + 1) * SEG]
        charged[:, b * SEG : (b + 1) * SEG] = jnp.where(row == cell[b], part, 0.0)
    part = dot_nt(phi[...], charged[...], HIGH)
    part = jnp.concatenate([part, jnp.zeros((8 * GROUP - NM, CS), f32)], axis=0)
    groups = [part[GROUP * g : GROUP * (g + 1), :] for g in range(8)]
    return jnp.concatenate([jnp.zeros((MOMENTS - LAST, SEG), f32), jnp.concatenate(groups, axis=1)], axis=0)


def far_kernel_body(*refs):
    raw, sources, out, scratch = refs[:6], refs[6:10], refs[10], refs[11:]
    cell, stress, off, tan, bur, operator, sems, around, shifted, phi, pots = scratch
    copies = fetch_all(raw, scratch[:6], sems)
    half = len(sources)
    count = 2 * half
    cells = count * CS
    turned = jnp.concatenate([source[...] for source in sources], axis=0).T
    first = MOMENTS - LAST
    for q in range(count):
        back = (count - q) % count
        at = CS * (2 * (back % half) + back // half) + first
        for g in range(8):
            piece = turned[CS * g : CS * (g + 1), at : at + GROUP]
            around[q * CS : (q + 1) * CS, GROUP * g : GROUP * (g + 1)] = piece
    around[cells : cells + CS, :] = around[0:CS, :]
    shifted[:, 0:NM] = jnp.zeros((CS, NM), f32)
    for o in range(1, cells):
        shifted[:, o * NM : (o + 1) * NM] = around[cells - o : cells - o + CS, 0:NM]
    for copy in copies[:5]:
        copy.wait()
    fill_phi(phi, off)
    copies[5].wait()
    local_exp = dot_nt(shifted[...], operator[...], HIGH)
    pots[...] = lax.dot_general(
        local_exp, phi[...], (((1,), (0,)), ((), ())), precision=HIGH, preferred_element_type=f32
    )
    b = [bur[i : i + 1, :] for i in range(3)]
    t = [tan[i : i + 1, :] for i in range(3)]
    sym = [[0.5 * (stress[i, j] + stress[j, i]) for j in range(3)] for i in range(3)]
    trac = [sym[i][0] * b[0] + sym[i][1] * b[1] + sym[i][2] * b[2] for i in range(3)]
    for i in range(3):
        j, k = (i + 1) % 3, (i + 2) % 3
        out[i : i + 1, :] = trac[j] * t[k] - trac[k] * t[j]
    row = iota((CS, SEG), 0)
    for block in range(cell.shape[0]):
        at = slice(block * SEG, (block + 1) * SEG)
        mine = jnp.where(row == cell[block], pots[:, at], 0.0)
        out[:, at] += jnp.sum(mine, axis=0, keepdims=True) * bur[:, at]


def final_kernel(pairs, back, near_all, far, conn, out, left_acc, force, halves):
    clear(left_acc)

    def peer(p, carry):
        for s in range(SEND):
            a = pairs[0, p * SEND + s]
            left_acc[a, 0:3, :] += back[p, 3 * s : 3 * s + 3, :]
        return carry

    lax.fori_loop(0, back.shape[0], peer, 0)
    for b in range(left_acc.shape[0]):
        at = slice(b * SEG, (b + 1) * SEG)
        near = near_all[4 * b : 4 * b + 3, :]
        force[0:3, at] = 0.5 * (far[:, at] + near + left_acc[b, 0:3, :])
    value = force[0:3, :]
    high = value.astype(bf16).astype(f32)
    halves[0:3, :] = high
    halves[3:6, :] = value - high
    chunk = 1024
    segs = conn.shape[1]
    groups = segs // SEG
    total = jnp.zeros((6 * groups, SEG), f32)
    low_row, high_row = iota((SEG, chunk), 0), iota((groups, chunk), 0)
    for end in range(2):
        for start in range(0, segs, chunk):
            at = slice(start, start + chunk)
            node = conn[end : end + 1, at]
            low = jnp.where(low_row == (node & (SEG - 1)), 1.0, 0.0).astype(bf16)
            mark = high_row == (node >> 7)
            parts = [
                jnp.where(mark, halves[i : i + 1, at], 0.0).astype(bf16) for i in range(6)
            ]
            total = total + dot_nt(jnp.concatenate(parts, axis=0), low)
    for c in range(3):
        whole = total[c * groups : (c + 1) * groups] + total[(3 + c) * groups : (4 + c) * groups]
        for g in range(groups):
            out[c : c + 1, g * SEG : (g + 1) * SEG] = whole[g : g + 1, :]


def call(body, out_shape, in_specs, scratch, flops, size):
    return pl.pallas_call(
        body,
        out_shape=out_shape,
        in_specs=in_specs,
        out_specs=jax.tree.map(lambda _: VMEM, out_shape),
        scratch_shapes=scratch,
        compiler_params=pltpu.CompilerParams(vmem_limit_bytes=size << 20),
        cost_estimate=pl.CostEstimate(flops=flops, bytes_accessed=1 << 20, transcendentals=0),
    )


def local(
    seg_offset,
    tangent,
    burgers,
    box_matrix,
    applied_stress,
    far_kernel,
    block_cell,
    fetch_table,
    pair_list,
    image_shift,
    pair_count,
    node_conn,
):
    blocks = block_cell.shape[0]
    segs = seg_offset.shape[1]
    peers = lax.axis_size("bulk")
    slabs = lax.axis_size("slab")
    shape = lambda *dims: jax.ShapeDtypeStruct(dims, f32)
    table = pltpu.VMEM((16, segs), f32)

    raw = [pair_list, image_shift, box_matrix, fetch_table.T, block_cell]
    segments = [seg_offset, tangent, burgers]
    send = call(
        pack_kernel,
        shape(peers, ROWS, SEG),
        [HBM] * 8,
        [pltpu.SMEM(x.shape, x.dtype) for x in raw]
        + [pltpu.VMEM(x.shape, x.dtype) for x in segments]
        + [pltpu.SemaphoreType.DMA((8,))]
        + [table, pltpu.VMEM((NM, segs), f32), pltpu.VMEM((CS, segs), f32)],
        10**6,
        60,
    )(*raw, *segments)
    recv = lax.all_to_all(send, "bulk", 0, 0, tiled=True)

    features, near_own = call(
        own_kernel,
        (jax.ShapeDtypeStruct((blocks, SEG, FEATURES), bf16), shape(SEG, SEG)),
        [SMEM] * 4 + [VMEM] * 3,
        [
            table,
            pltpu.VMEM((blocks, 3, SEG, SEG), f32),
            pltpu.VMEM((blocks, 8, SEG), f32),
        ],
        10**9,
        12,
    )(pair_list, image_shift, box_matrix, pair_count, *segments)

    def from_slab(value, back):
        return lax.ppermute(value, "slab", [(s, (s + back) % slabs) for s in range(slabs)])

    half = slabs // 2
    moments = jnp.sum(recv[:, LAST:, :], axis=0)
    other = from_slab(moments, half)

    ret, near = call(
        pair_kernel,
        (shape(peers, 16, SEG), shape(SEG, SEG)),
        [VMEM] * 3,
        [
            pltpu.VMEM((blocks, 3, SEG, SEG), f32),
            pltpu.VMEM((peers, SEG), jnp.int32),
            pltpu.SMEM((peers, SEG), jnp.int32),
            pltpu.SemaphoreType.DMA,
        ],
        10**10,
        16,
    )(recv, features, near_own)
    ret, other = lax.optimization_barrier((ret, other))
    back = lax.all_to_all(ret, "bulk", 0, 0, tiled=True)
    two = jnp.concatenate([moments, other], axis=0)
    sources = [two] + [from_slab(two, k) for k in range(1, half)]
    raw = [block_cell, applied_stress]
    far = call(
        far_kernel_body,
        shape(3, segs),
        [HBM] * 6 + [VMEM] * half,
        [pltpu.SMEM(x.shape, x.dtype) for x in raw]
        + [pltpu.VMEM(x.shape, x.dtype) for x in segments + [far_kernel]]
        + [
            pltpu.SemaphoreType.DMA((6,)),
            pltpu.VMEM((slabs * CS + CS, SEG), f32),
            pltpu.VMEM((CS, slabs * CS * NM), f32),
            pltpu.VMEM((NM, segs), f32),
            pltpu.VMEM((CS, segs), f32),
        ],
        10**9,
        52,
    )(*raw, *segments, far_kernel, *sources)

    return call(
        final_kernel,
        shape(3, segs),
        [SMEM] + [VMEM] * 4,
        [pltpu.VMEM((blocks, 8, SEG), f32), pltpu.VMEM((8, segs), f32), pltpu.VMEM((8, segs), f32)],
        10**9,
        24,
    )(pair_list, back, near, far, node_conn)


def solution(mesh):
    both = P(None, ("slab", "bulk"))
    in_specs = (
        both,
        both,
        both,
        P(),
        P(),
        P(),
        P(("slab", "bulk")),
        P(("slab", "bulk"), None),
        both,
        both,
        P(("slab", "bulk")),
        both,
    )
    return jax.shard_map(local, mesh=mesh, in_specs=in_specs, out_specs=both, check_vma=False)
```

```python
import jax
import jax.numpy as jnp
from jax import lax
from jax.experimental import pallas as pl
from jax.experimental.pallas import tpu as pltpu
from jax.sharding import PartitionSpec as P

SEG = 128
CS = 16
NM = 84
SEND = 5
LAST = 40
MOMENTS = 45
ROWS = 56
GROUP = 11
META = 112
FEATURES = 64
KAPPA = 0.2
CORE_SQ = 0.25
VMEM = pl.BlockSpec(memory_space=pltpu.VMEM)
HBM = pl.BlockSpec(memory_space=pltpu.HBM)
SMEM = pl.BlockSpec(memory_space=pltpu.SMEM)
f32 = jnp.float32
bf16 = jnp.bfloat16


def exponents():
    return [(a, b, c) for a in range(7) for b in range(7 - a) for c in range(7 - a - b)]


def iota(shape, dim):
    return lax.broadcasted_iota(jnp.int32, shape, dim)


def lane_block(index):
    return pl.ds(pl.multiple_of(index * SEG, SEG), SEG)


def fill_table(table, off, tan, bur, diag, cross):
    b = [bur[i : i + 1, :] for i in range(3)]
    t = [tan[i : i + 1, :] for i in range(3)]
    table[0:3, :] = off[...]
    for i in range(3):
        table[3 + i : 4 + i, :] = diag * (b[i] * t[i])
    for row, (i, j) in enumerate(((0, 1), (0, 2), (1, 2))):
        table[6 + row : 7 + row, :] = cross * (b[i] * t[j] + b[j] * t[i])


def shift_of(box, shift, k):
    s = [shift[i, k].astype(f32) for i in range(3)]
    return [box[c, 0] * s[0] + box[c, 1] * s[1] + box[c, 2] * s[2] for c in range(3)]


def shift_rows(vec, shape):
    row = iota(shape, 0)
    return jnp.where(row == 0, vec[0], jnp.where(row == 1, vec[1], jnp.where(row == 2, vec[2], 0.0)))


def fetch_all(sources, targets, sems):
    copies = [
        pltpu.make_async_copy(source, target, sems.at[i])
        for i, (source, target) in enumerate(zip(sources, targets, strict=True))
    ]
    for copy in copies:
        copy.start()
    return copies


def shift_table(box, shift):
    steps = [shift[i : i + 1, :].astype(f32) for i in range(3)]
    rows = [box[c, 0] * steps[0] + box[c, 1] * steps[1] + box[c, 2] * steps[2] for c in range(3)]
    return jnp.concatenate(rows + [jnp.zeros((5, shift.shape[1]), f32)], axis=0)


def pack_kernel(*refs):
    sources, send, scratch = refs[:8], refs[8], refs[9:]
    pairs, box, cell, shift, fetch, off, tan, bur, sems, table, phi, charged = scratch
    for copy in fetch_all(sources, scratch[:8], sems):
        copy.wait()
    fill_table(table, off, tan, bur, 2.0 * KAPPA, KAPPA)
    packed = cell_moments(cell, off, tan, bur, phi, charged)
    vectors = shift_table(box, shift)
    peers = send.shape[0]
    wide = jnp.concatenate([fetch[...].astype(f32), jnp.zeros((SEND, SEG - peers), f32)], axis=1)
    tall = jnp.concatenate([wide, jnp.zeros((8 - SEND, SEG), f32)], axis=0).T
    meta = jnp.concatenate(
        [jnp.zeros((SEG, META), f32), tall, jnp.zeros((SEG, SEG - META - 8), f32)], axis=1
    )
    row, lane = iota((ROWS - LAST, SEG), 0), iota((ROWS - LAST, SEG), 1)
    mark = (row == ROWS - LAST - 1) & (lane >= META)
    for p in range(peers):
        rest = jnp.where(mark, meta[p : p + 1, :], packed)
        for s in range(SEND):
            k = p * SEND + s
            at = lane_block(pairs[0, k])
            vec = jnp.broadcast_to(vectors[:, k : k + 1], (8, SEG))
            send[p, 8 * s : 8 * s + 8, :] = table[0:8, at] - vec
            rest = jnp.where(row == s, table[8:9, at], rest)
        send[p, LAST:ROWS, :] = rest


def split(value):
    high = value.astype(bf16).astype(f32)
    rest = value - high
    mid = rest.astype(bf16).astype(f32)
    return high, mid, (rest - mid).astype(bf16).astype(f32)


def fill_features(table, features):
    first = iota((8, SEG), 0) < 3
    one, none = jnp.ones((3, SEG), f32), jnp.zeros((1, SEG), f32)

    def block(b, carry):
        at = lane_block(b)
        head = table[0:8, at]
        high, mid, low = split(head)
        last_high, last_mid, _ = split(table[8:9, at])
        square = split(jnp.sum(jnp.where(first, head * head, 0.0), axis=0, keepdims=True))
        groups = [jnp.where(first, 1.0, high)] * 2
        groups.append(
            jnp.concatenate([one, last_high, last_high, last_mid, square[0], square[1]], axis=0)
        )
        groups.append(jnp.where(first, high, mid))
        groups.append(jnp.concatenate([mid[0:3], low[0:3], square[2], none], axis=0))
        groups.append(jnp.concatenate([high[0:3], high[0:3], none, none], axis=0))
        groups.append(jnp.concatenate([mid[0:3], one, none, none], axis=0))
        groups.append(jnp.zeros((SEG - 56, SEG), f32))
        turned = jnp.concatenate(groups, axis=0).T
        features[b] = turned[:, 0:FEATURES].astype(bf16)
        return carry

    lax.fori_loop(0, features.shape[0], block, 0, unroll=4)


def weights(head, last):
    row = iota((8, SEG), 0)
    first, second = row < 3, (row >= 3) & (row < 6)
    high, mid, low = split(head)
    last_high, last_mid, _ = split(last)
    square = split(jnp.sum(jnp.where(first, head * head, 0.0), axis=0, keepdims=True) + CORE_SQ)
    none = jnp.zeros((8, SEG), f32)
    columns = []
    for i in range(3):
        own = row == i
        parts = [jnp.where(own, part, 0.0) for part in (high, mid, low, -1.0)]
        parts += [jnp.where(own | (row == i + 3), -1.0, 0.0), none, none, none]
        columns.append(jnp.concatenate(parts, axis=0))
    tail = jnp.where(first, 0.0, high)
    edge = jnp.where((row == 3) | (row == 5), last_high, jnp.where(row == 4, last_mid, 0.0))
    parts = [tail, jnp.where(first, 0.0, mid), edge, tail, none, none, none, none]
    columns.append(jnp.concatenate(parts, axis=0))
    twice = [-2.0 * part for part in (high, mid, low)]
    below = [jnp.concatenate([part[0:3], part[0:3], part[0:2]], axis=0) for part in twice]
    norm = jnp.where(row == 3, square[0], jnp.where(row == 4, square[1], square[2]))
    parts = [none, none, jnp.where(row >= 6, 1.0, 0.0), jnp.where(first, twice[0], 0.0)]
    parts.append(jnp.where(row < 6, below[0], jnp.where(row == 6, 1.0, 0.0)))
    parts.append(jnp.where(first, twice[1], jnp.where(second, below[2], 0.0)))
    parts += [jnp.where(first, twice[1], jnp.where(second, norm, 0.0)), none]
    columns.append(jnp.concatenate(parts, axis=0))
    return jnp.concatenate(columns, axis=1).astype(bf16)


def tile(head, last, features, acc, b):
    both = weights(head, last)
    sums = [jnp.zeros((8, SEG), f32) for _ in range(3)]
    step = 64
    for start in range(0, SEG, step):
        at = slice(start, start + step)
        made = jnp.dot(features[b, at, :], both, preferred_element_type=f32)
        inv = lax.rsqrt(made[:, 4 * SEG :])
        weight = made[:, 3 * SEG : 4 * SEG] * (inv * inv * inv)
        for c in range(3):
            push = weight * made[:, c * SEG : (c + 1) * SEG]
            acc[b, c, at, :] += push
            for r in range(0, step, 8):
                sums[c] = sums[c] + push[r : r + 8]
    return [jnp.sum(part, axis=0, keepdims=True) for part in sums]


def fold(acc, near, others):
    def pair(half, carry):
        at = pl.ds(pl.multiple_of(8 * half, 8), 8)
        rows = []
        for b in (2 * half, 2 * half + 1):
            rows += [jnp.sum(acc[b, c].T, axis=0, keepdims=True) for c in range(3)]
            rows.append(jnp.zeros((1, SEG), f32))
        near[at, :] = others[at, :] - jnp.concatenate(rows, axis=0)
        return carry

    lax.fori_loop(0, acc.shape[0] // 2, pair, 0, unroll=True)


def clear(acc):
    def block(b, carry):
        acc[b] = jnp.zeros(acc.shape[1:], f32)
        return carry

    lax.fori_loop(0, acc.shape[0], block, 0, unroll=4)


def own_kernel(pairs, shift, box, count, off, tan, bur, features, near, table, acc, left_acc):
    clear(acc)
    left_acc[...] = jnp.zeros_like(left_acc)
    fill_table(table, off, tan, bur, 1.0, 1.0)
    fill_features(table, features)
    blocks = acc.shape[0]
    row = iota((8, SEG), 0)
    scale = jnp.where(row < 3, 1.0, jnp.where(row < 6, 2.0 * KAPPA, KAPPA))

    def pair(k, carry):
        a, b = pairs[0, k], pairs[1, k]
        at = lane_block(a)
        head = table[0:8, at] * scale - shift_rows(shift_of(box, shift, k), (8, SEG))
        rows = tile(head, table[8:9, at] * KAPPA, features, acc, b)
        for c in range(3):
            left_acc[a, c : c + 1, :] += rows[c]
        return carry

    lax.fori_loop(pairs.shape[1] - blocks, count[0], pair, 0)
    for b in range(blocks):
        near[4 * b : 4 * b + 4, :] = left_acc[b, 0:4, :]
    fold(acc, near, near)


def pair_kernel(recv, features, near_own, ret, near, acc, ids_vmem, ids, sem):
    peers = recv.shape[0]
    for p in range(peers):
        ids_vmem[p : p + 1, :] = recv[p, ROWS - 1 : ROWS, :].astype(jnp.int32)
    copy = pltpu.make_async_copy(ids_vmem, ids, sem)
    copy.start()
    clear(acc)
    copy.wait()

    def peer(p, carry):
        for s in range(SEND):
            head, last = recv[p, 8 * s : 8 * s + 8, :], recv[p, LAST + s : LAST + s + 1, :]
            rows = tile(head, last, features, acc, ids[p, META + s])
            for c in range(3):
                ret[p, 3 * s + c : 3 * s + c + 1, :] = rows[c]
        ret[p, 15:16, :] = jnp.zeros((1, SEG), f32)
        return carry

    lax.fori_loop(0, peers, peer, 0, unroll=8)
    fold(acc, near, near_own)


def fill_phi(phi, off):
    powers = []
    for i in range(3):
        x = off[i : i + 1, :]
        made = [None, x]
        for _ in range(5):
            made.append(made[-1] * x)
        powers.append(made)
    pairs_of = {}
    for k, (a, b, c) in enumerate(exponents()):
        if (a, b) not in pairs_of:
            got = [p for p in (powers[0][a], powers[1][b]) if p is not None]
            pairs_of[a, b] = got[0] * got[1] if len(got) == 2 else got[0] if got else None
        value = pairs_of[a, b]
        if c:
            value = powers[2][c] if value is None else value * powers[2][c]
        phi[k : k + 1, :] = jnp.ones_like(powers[0][1]) if value is None else value


def dot_nt(left, right):
    return lax.dot_general(
        left, right, (((1,), (1,)), ((), ())), preferred_element_type=f32
    )


def halves_of(value):
    high = value.astype(bf16)
    return high, (value - high.astype(f32)).astype(bf16)


def dot_halves(left, right, axis):
    left_high, left_low = halves_of(left)
    right_high, right_low = halves_of(right)
    dims = (((1,), (axis,)), ((), ()))
    count = right.shape[1 - axis]
    both = jnp.concatenate([right_high, right_low], axis=1 - axis)
    made = lax.dot_general(left_high, both, dims, preferred_element_type=f32)
    made = made[:, :count] + made[:, count:]
    return made + lax.dot_general(left_low, right_high, dims, preferred_element_type=f32)


def cell_moments(cell, off, tan, bur, phi, charged):
    fill_phi(phi, off)
    charge = jnp.sum(bur[...] * tan[...], axis=0, keepdims=True)
    row = iota((CS, SEG), 0)
    for b in range(cell.shape[0]):
        part = charge[:, b * SEG : (b + 1) * SEG]
        charged[:, b * SEG : (b + 1) * SEG] = jnp.where(row == cell[b], part, 0.0)
    part = dot_halves(phi[...], charged[...], 1)
    part = jnp.concatenate([part, jnp.zeros((8 * GROUP - NM, CS), f32)], axis=0)
    groups = [part[GROUP * g : GROUP * (g + 1), :] for g in range(8)]
    return jnp.concatenate([jnp.zeros((MOMENTS - LAST, SEG), f32), jnp.concatenate(groups, axis=1)], axis=0)


def far_kernel_body(*refs):
    raw, sources, out, scratch = refs[:6], refs[6:10], refs[10], refs[11:]
    cell, stress, off, tan, bur, operator, sems, around, shifted, phi, pots = scratch
    copies = fetch_all(raw, scratch[:6], sems)
    for copy in copies[:5]:
        copy.wait()
    fill_phi(phi, off)
    half = len(sources)
    count = 2 * half
    cells = count * CS
    turned = jnp.concatenate([source[...] for source in sources], axis=0).T
    first = MOMENTS - LAST
    for q in range(count):
        back = (count - q) % count
        at = CS * (2 * (back % half) + back // half) + first
        for g in range(8):
            piece = turned[CS * g : CS * (g + 1), at : at + GROUP]
            around[q * CS : (q + 1) * CS, GROUP * g : GROUP * (g + 1)] = piece
    around[cells : cells + CS, :] = around[0:CS, :]
    shifted[:, 0:NM] = jnp.zeros((CS, NM), f32)
    for o in range(1, cells):
        shifted[:, o * NM : (o + 1) * NM] = around[cells - o : cells - o + CS, 0:NM]
    copies[5].wait()
    local_exp = dot_halves(operator[...], shifted[...], 1).T
    high, low = halves_of(local_exp)
    phi_high, phi_low = halves_of(phi[...])
    made = jnp.dot(jnp.concatenate([high, low], axis=0), phi_high, preferred_element_type=f32)
    made = made[0:CS] + made[CS:]
    pots[...] = made + jnp.dot(high, phi_low, preferred_element_type=f32)
    b = [bur[i : i + 1, :] for i in range(3)]
    t = [tan[i : i + 1, :] for i in range(3)]
    sym = [[0.5 * (stress[i, j] + stress[j, i]) for j in range(3)] for i in range(3)]
    trac = [sym[i][0] * b[0] + sym[i][1] * b[1] + sym[i][2] * b[2] for i in range(3)]
    for i in range(3):
        j, k = (i + 1) % 3, (i + 2) % 3
        out[i : i + 1, :] = trac[j] * t[k] - trac[k] * t[j]
    row = iota((CS, SEG), 0)
    for block in range(cell.shape[0]):
        at = slice(block * SEG, (block + 1) * SEG)
        mine = jnp.where(row == cell[block], pots[:, at], 0.0)
        out[:, at] += jnp.sum(mine, axis=0, keepdims=True) * bur[:, at]


def final_kernel(pairs, back, near_all, far, conn, out, left_acc, force, halves):
    clear(left_acc)

    def peer(p, carry):
        for s in range(SEND):
            a = pairs[0, p * SEND + s]
            left_acc[a, 0:3, :] += back[p, 3 * s : 3 * s + 3, :]
        return carry

    lax.fori_loop(0, back.shape[0], peer, 0)
    for b in range(left_acc.shape[0]):
        at = slice(b * SEG, (b + 1) * SEG)
        near = near_all[4 * b : 4 * b + 3, :]
        force[0:3, at] = 0.5 * (far[:, at] + near + left_acc[b, 0:3, :])
    value = force[0:3, :]
    high = value.astype(bf16).astype(f32)
    halves[0:3, :] = high
    halves[3:6, :] = value - high
    chunk = 1024
    segs = conn.shape[1]
    groups = segs // SEG
    total = jnp.zeros((6 * groups, SEG), f32)
    low_row, high_row = iota((SEG, chunk), 0), iota((groups, chunk), 0)
    for end in range(2):
        for start in range(0, segs, chunk):
            at = slice(start, start + chunk)
            node = conn[end : end + 1, at]
            low = jnp.where(low_row == (node & (SEG - 1)), 1.0, 0.0).astype(bf16)
            mark = high_row == (node >> 7)
            parts = [
                jnp.where(mark, halves[i : i + 1, at], 0.0).astype(bf16) for i in range(6)
            ]
            total = total + dot_nt(jnp.concatenate(parts, axis=0), low)
    for c in range(3):
        whole = total[c * groups : (c + 1) * groups] + total[(3 + c) * groups : (4 + c) * groups]
        for g in range(groups):
            out[c : c + 1, g * SEG : (g + 1) * SEG] = whole[g : g + 1, :]


def call(body, out_shape, in_specs, scratch, flops, size):
    return pl.pallas_call(
        body,
        out_shape=out_shape,
        in_specs=in_specs,
        out_specs=jax.tree.map(lambda _: VMEM, out_shape),
        scratch_shapes=scratch,
        compiler_params=pltpu.CompilerParams(vmem_limit_bytes=size << 20),
        cost_estimate=pl.CostEstimate(flops=flops, bytes_accessed=1 << 20, transcendentals=0),
    )


def local(
    seg_offset,
    tangent,
    burgers,
    box_matrix,
    applied_stress,
    far_kernel,
    block_cell,
    fetch_table,
    pair_list,
    image_shift,
    pair_count,
    node_conn,
):
    blocks = block_cell.shape[0]
    segs = seg_offset.shape[1]
    peers = lax.axis_size("bulk")
    slabs = lax.axis_size("slab")
    shape = lambda *dims: jax.ShapeDtypeStruct(dims, f32)
    table = pltpu.VMEM((16, segs), f32)

    raw = [pair_list, box_matrix, block_cell]
    segments = [seg_offset, tangent, burgers]
    vectors = [image_shift, fetch_table.T, *segments]
    send = call(
        pack_kernel,
        shape(peers, ROWS, SEG),
        [HBM] * 8,
        [pltpu.SMEM(x.shape, x.dtype) for x in raw]
        + [pltpu.VMEM(x.shape, x.dtype) for x in vectors]
        + [pltpu.SemaphoreType.DMA((8,))]
        + [table, pltpu.VMEM((NM, segs), f32), pltpu.VMEM((CS, segs), f32)],
        10**6,
        60,
    )(*raw, *vectors)
    recv = lax.all_to_all(send, "bulk", 0, 0, tiled=True)

    features, near_own = call(
        own_kernel,
        (jax.ShapeDtypeStruct((blocks, SEG, FEATURES), bf16), shape(SEG, SEG)),
        [SMEM] * 4 + [VMEM] * 3,
        [
            table,
            pltpu.VMEM((blocks, 3, SEG, SEG), f32),
            pltpu.VMEM((blocks, 8, SEG), f32),
        ],
        10**9,
        12,
    )(pair_list, image_shift, box_matrix, pair_count, *segments)

    def from_slab(value, back):
        return lax.ppermute(value, "slab", [(s, (s + back) % slabs) for s in range(slabs)])

    half = slabs // 2
    moments = jnp.sum(recv[:, LAST:, :], axis=0)
    other = from_slab(moments, half)

    ret, near = call(
        pair_kernel,
        (shape(peers, 16, SEG), shape(SEG, SEG)),
        [VMEM] * 3,
        [
            pltpu.VMEM((blocks, 3, SEG, SEG), f32),
            pltpu.VMEM((peers, SEG), jnp.int32),
            pltpu.SMEM((peers, SEG), jnp.int32),
            pltpu.SemaphoreType.DMA,
        ],
        10**10,
        16,
    )(recv, features, near_own)
    ret, other = lax.optimization_barrier((ret, other))
    back = lax.all_to_all(ret, "bulk", 0, 0, tiled=True)
    two = jnp.concatenate([moments, other], axis=0)
    sources = [two] + [from_slab(two, k) for k in range(1, half)]
    raw = [block_cell, applied_stress]
    far = call(
        far_kernel_body,
        shape(3, segs),
        [HBM] * 6 + [VMEM] * half,
        [pltpu.SMEM(x.shape, x.dtype) for x in raw]
        + [pltpu.VMEM(x.shape, x.dtype) for x in segments + [far_kernel]]
        + [
            pltpu.SemaphoreType.DMA((6,)),
            pltpu.VMEM((slabs * CS + CS, SEG), f32),
            pltpu.VMEM((CS, slabs * CS * NM), f32),
            pltpu.VMEM((NM, segs), f32),
            pltpu.VMEM((CS, segs), f32),
        ],
        10**9,
        52,
    )(*raw, *segments, far_kernel, *sources)

    return call(
        final_kernel,
        shape(3, segs),
        [SMEM] + [VMEM] * 4,
        [pltpu.VMEM((blocks, 8, SEG), f32), pltpu.VMEM((8, segs), f32), pltpu.VMEM((8, segs), f32)],
        10**9,
        24,
    )(pair_list, back, near, far, node_conn)


def solution(mesh):
    both = P(None, ("slab", "bulk"))
    in_specs = (
        both,
        both,
        both,
        P(),
        P(),
        P(),
        P(("slab", "bulk")),
        P(("slab", "bulk"), None),
        both,
        both,
        P(("slab", "bulk")),
        both,
    )
    return jax.shard_map(local, mesh=mesh, in_specs=in_specs, out_specs=both, check_vma=False)
```

```python
import jax
import jax.numpy as jnp
from jax import lax
from jax.experimental import pallas as pl
from jax.experimental.pallas import tpu as pltpu
from jax.sharding import PartitionSpec as P

SEG = 128
CS = 16
NM = 84
SEND = 5
LAST = 40
MOMENTS = 45
ROWS = 56
GROUP = 11
META = 112
FEATURES = 64
KAPPA = 0.2
CORE_SQ = 0.25
VMEM = pl.BlockSpec(memory_space=pltpu.VMEM)
HBM = pl.BlockSpec(memory_space=pltpu.HBM)
SMEM = pl.BlockSpec(memory_space=pltpu.SMEM)
f32 = jnp.float32
bf16 = jnp.bfloat16


def exponents():
    return [(a, b, c) for a in range(7) for b in range(7 - a) for c in range(7 - a - b)]


def iota(shape, dim):
    return lax.broadcasted_iota(jnp.int32, shape, dim)


def lane_block(index):
    return pl.ds(pl.multiple_of(index * SEG, SEG), SEG)


def fill_table(table, off, tan, bur, diag, cross):
    b = [bur[i : i + 1, :] for i in range(3)]
    t = [tan[i : i + 1, :] for i in range(3)]
    table[0:3, :] = off[...]
    for i in range(3):
        table[3 + i : 4 + i, :] = diag * (b[i] * t[i])
    for row, (i, j) in enumerate(((0, 1), (0, 2), (1, 2))):
        table[6 + row : 7 + row, :] = cross * (b[i] * t[j] + b[j] * t[i])


def shift_of(box, shift, k):
    s = [shift[i, k].astype(f32) for i in range(3)]
    return [box[c, 0] * s[0] + box[c, 1] * s[1] + box[c, 2] * s[2] for c in range(3)]


def shift_rows(vec, shape):
    row = iota(shape, 0)
    return jnp.where(row == 0, vec[0], jnp.where(row == 1, vec[1], jnp.where(row == 2, vec[2], 0.0)))


def fetch_all(sources, targets, sems):
    copies = [
        pltpu.make_async_copy(source, target, sems.at[i])
        for i, (source, target) in enumerate(zip(sources, targets, strict=True))
    ]
    for copy in copies:
        copy.start()
    return copies


def shift_table(box, shift):
    steps = [shift[i : i + 1, :].astype(f32) for i in range(3)]
    rows = [box[c, 0] * steps[0] + box[c, 1] * steps[1] + box[c, 2] * steps[2] for c in range(3)]
    return jnp.concatenate(rows + [jnp.zeros((5, shift.shape[1]), f32)], axis=0)


def pack_kernel(*refs):
    sources, send, scratch = refs[:8], refs[8], refs[9:]
    pairs, box, cell, shift, fetch, off, tan, bur, sems, table, phi, charged = scratch
    for copy in fetch_all(sources, scratch[:8], sems):
        copy.wait()
    fill_table(table, off, tan, bur, 2.0 * KAPPA, KAPPA)
    packed = cell_moments(cell, off, tan, bur, phi, charged)
    vectors = shift_table(box, shift)
    peers = send.shape[0]
    wide = jnp.concatenate([fetch[...].astype(f32), jnp.zeros((SEND, SEG - peers), f32)], axis=1)
    tall = jnp.concatenate([wide, jnp.zeros((8 - SEND, SEG), f32)], axis=0).T
    meta = jnp.concatenate(
        [jnp.zeros((SEG, META), f32), tall, jnp.zeros((SEG, SEG - META - 8), f32)], axis=1
    )
    row, lane = iota((ROWS - LAST, SEG), 0), iota((ROWS - LAST, SEG), 1)
    mark = (row == ROWS - LAST - 1) & (lane >= META)
    for p in range(peers):
        rest = jnp.where(mark, meta[p : p + 1, :], packed)
        for s in range(SEND):
            k = p * SEND + s
            at = lane_block(pairs[0, k])
            vec = jnp.broadcast_to(vectors[:, k : k + 1], (8, SEG))
            send[p, 8 * s : 8 * s + 8, :] = table[0:8, at] - vec
            rest = jnp.where(row == s, table[8:9, at], rest)
        send[p, LAST:ROWS, :] = rest


def split(value):
    high = value.astype(bf16).astype(f32)
    rest = value - high
    mid = rest.astype(bf16).astype(f32)
    return high, mid, (rest - mid).astype(bf16).astype(f32)


def fill_features(table, features):
    first = iota((8, SEG), 0) < 3
    one, none = jnp.ones((3, SEG), f32), jnp.zeros((1, SEG), f32)

    def block(b, carry):
        at = lane_block(b)
        head = table[0:8, at]
        high, mid, low = split(head)
        last_high, last_mid, _ = split(table[8:9, at])
        square = split(jnp.sum(jnp.where(first, head * head, 0.0), axis=0, keepdims=True))
        groups = [jnp.where(first, 1.0, high)] * 2
        groups.append(
            jnp.concatenate([one, last_high, last_high, last_mid, square[0], square[1]], axis=0)
        )
        groups.append(jnp.where(first, high, mid))
        groups.append(jnp.concatenate([mid[0:3], low[0:3], square[2], none], axis=0))
        groups.append(jnp.concatenate([high[0:3], high[0:3], none, none], axis=0))
        groups.append(jnp.concatenate([mid[0:3], one, none, none], axis=0))
        groups.append(jnp.zeros((SEG - 56, SEG), f32))
        turned = jnp.concatenate(groups, axis=0).T
        features[b] = turned[:, 0:FEATURES].astype(bf16)
        return carry

    lax.fori_loop(0, features.shape[0], block, 0, unroll=4)


def weights(head, last):
    row = iota((8, SEG), 0)
    first, second = row < 3, (row >= 3) & (row < 6)
    high, mid, low = split(head)
    last_high, last_mid, _ = split(last)
    square = split(jnp.sum(jnp.where(first, head * head, 0.0), axis=0, keepdims=True) + CORE_SQ)
    none = jnp.zeros((8, SEG), f32)
    columns = []
    for i in range(3):
        own = row == i
        parts = [jnp.where(own, part, 0.0) for part in (high, mid, low, -1.0)]
        parts += [jnp.where(own | (row == i + 3), -1.0, 0.0), none, none, none]
        columns.append(jnp.concatenate(parts, axis=0))
    tail = jnp.where(first, 0.0, high)
    edge = jnp.where((row == 3) | (row == 5), last_high, jnp.where(row == 4, last_mid, 0.0))
    parts = [tail, jnp.where(first, 0.0, mid), edge, tail, none, none, none, none]
    columns.append(jnp.concatenate(parts, axis=0))
    twice = [-2.0 * part for part in (high, mid, low)]
    below = [jnp.concatenate([part[0:3], part[0:3], part[0:2]], axis=0) for part in twice]
    norm = jnp.where(row == 3, square[0], jnp.where(row == 4, square[1], square[2]))
    parts = [none, none, jnp.where(row >= 6, 1.0, 0.0), jnp.where(first, twice[0], 0.0)]
    parts.append(jnp.where(row < 6, below[0], jnp.where(row == 6, 1.0, 0.0)))
    parts.append(jnp.where(first, twice[1], jnp.where(second, below[2], 0.0)))
    parts += [jnp.where(first, twice[1], jnp.where(second, norm, 0.0)), none]
    columns.append(jnp.concatenate(parts, axis=0))
    return jnp.concatenate(columns, axis=1).astype(bf16)


def tile(head, last, features, acc, b):
    both = weights(head, last)
    sums = [jnp.zeros((8, SEG), f32) for _ in range(3)]
    step = 64
    for start in range(0, SEG, step):
        at = slice(start, start + step)
        made = jnp.dot(features[b, at, :], both, preferred_element_type=f32)
        inv = lax.rsqrt(made[:, 4 * SEG :])
        weight = made[:, 3 * SEG : 4 * SEG] * (inv * inv * inv)
        for c in range(3):
            push = weight * made[:, c * SEG : (c + 1) * SEG]
            acc[b, c, at, :] += push
            for r in range(0, step, 8):
                sums[c] = sums[c] + push[r : r + 8]
    return [jnp.sum(part, axis=0, keepdims=True) for part in sums]


def fold(acc, near, others):
    def pair(half, carry):
        at = pl.ds(pl.multiple_of(8 * half, 8), 8)
        rows = []
        for b in (2 * half, 2 * half + 1):
            rows += [jnp.sum(acc[b, c].T, axis=0, keepdims=True) for c in range(3)]
            rows.append(jnp.zeros((1, SEG), f32))
        near[at, :] = others[at, :] - jnp.concatenate(rows, axis=0)
        return carry

    lax.fori_loop(0, acc.shape[0] // 2, pair, 0, unroll=True)


def clear(acc):
    def block(b, carry):
        acc[b] = jnp.zeros(acc.shape[1:], f32)
        return carry

    lax.fori_loop(0, acc.shape[0], block, 0, unroll=4)


def left_rows(blocks, out_shape):
    slots = blocks.shape[1]
    slot, lane = iota((slots, out_shape[1]), 0), iota((slots, out_shape[1]), 1)
    peer, rest = lane >> 4, lane & 15
    third = (rest >= 3).astype(jnp.int32) + (rest >= 6) + (rest >= 9) + (rest >= 12)
    pick = (slot == SEND * peer + third) & (rest < 15)
    tall = jnp.broadcast_to(blocks.astype(f32), (16, slots)).astype(bf16)
    found = jnp.dot(tall, jnp.where(pick, 1.0, 0.0).astype(bf16), preferred_element_type=f32)
    lane = iota(out_shape, 1)
    rest = lane & 15
    third = (rest >= 3).astype(jnp.int32) + (rest >= 6) + (rest >= 9) + (rest >= 12)
    row = 4 * found[0 : out_shape[0]].astype(jnp.int32) + rest - 3 * third
    return jnp.where(rest < 15, row, -1)


def own_kernel(
    pairs, shift, box, count, off, tan, bur, pairs_row, features, near, left, table, acc, left_acc
):
    left[...] = left_rows(pairs_row[0:1, :], left.shape)
    clear(acc)
    left_acc[...] = jnp.zeros_like(left_acc)
    fill_table(table, off, tan, bur, 1.0, 1.0)
    fill_features(table, features)
    blocks = acc.shape[0]
    row = iota((8, SEG), 0)
    scale = jnp.where(row < 3, 1.0, jnp.where(row < 6, 2.0 * KAPPA, KAPPA))

    def pair(k, carry):
        a, b = pairs[0, k], pairs[1, k]
        at = lane_block(a)
        head = table[0:8, at] * scale - shift_rows(shift_of(box, shift, k), (8, SEG))
        rows = tile(head, table[8:9, at] * KAPPA, features, acc, b)
        for c in range(3):
            left_acc[a, c : c + 1, :] += rows[c]
        return carry

    lax.fori_loop(pairs.shape[1] - blocks, count[0], pair, 0)
    for b in range(blocks):
        near[4 * b : 4 * b + 4, :] = left_acc[b, 0:4, :]
    fold(acc, near, near)


def pair_kernel(recv, features, near_own, ret, near, acc, ids_vmem, ids, sem):
    peers = recv.shape[0]
    for p in range(peers):
        ids_vmem[p : p + 1, :] = recv[p, ROWS - 1 : ROWS, :].astype(jnp.int32)
    copy = pltpu.make_async_copy(ids_vmem, ids, sem)
    copy.start()
    clear(acc)
    copy.wait()

    def peer(p, carry):
        for s in range(SEND):
            head, last = recv[p, 8 * s : 8 * s + 8, :], recv[p, LAST + s : LAST + s + 1, :]
            rows = tile(head, last, features, acc, ids[p, META + s])
            for c in range(3):
                ret[p, 3 * s + c : 3 * s + c + 1, :] = rows[c]
        ret[p, 15:16, :] = jnp.zeros((1, SEG), f32)
        return carry

    lax.fori_loop(0, peers, peer, 0, unroll=8)
    fold(acc, near, near_own)


def fill_phi(phi, off):
    powers = []
    for i in range(3):
        x = off[i : i + 1, :]
        made = [None, x]
        for _ in range(5):
            made.append(made[-1] * x)
        powers.append(made)
    pairs_of = {}
    for k, (a, b, c) in enumerate(exponents()):
        if (a, b) not in pairs_of:
            got = [p for p in (powers[0][a], powers[1][b]) if p is not None]
            pairs_of[a, b] = got[0] * got[1] if len(got) == 2 else got[0] if got else None
        value = pairs_of[a, b]
        if c:
            value = powers[2][c] if value is None else value * powers[2][c]
        phi[k : k + 1, :] = jnp.ones_like(powers[0][1]) if value is None else value


def dot_nt(left, right):
    return lax.dot_general(
        left, right, (((1,), (1,)), ((), ())), preferred_element_type=f32
    )


def halves_of(value):
    high = value.astype(bf16)
    return high, (value - high.astype(f32)).astype(bf16)


def dot_halves(left, right, axis):
    left_high, left_low = halves_of(left)
    right_high, right_low = halves_of(right)
    dims = (((1,), (axis,)), ((), ()))
    count = right.shape[1 - axis]
    both = jnp.concatenate([right_high, right_low], axis=1 - axis)
    made = lax.dot_general(left_high, both, dims, preferred_element_type=f32)
    made = made[:, :count] + made[:, count:]
    return made + lax.dot_general(left_low, right_high, dims, preferred_element_type=f32)


def cell_moments(cell, off, tan, bur, phi, charged):
    fill_phi(phi, off)
    charge = jnp.sum(bur[...] * tan[...], axis=0, keepdims=True)
    row = iota((CS, SEG), 0)
    for b in range(cell.shape[0]):
        part = charge[:, b * SEG : (b + 1) * SEG]
        charged[:, b * SEG : (b + 1) * SEG] = jnp.where(row == cell[b], part, 0.0)
    part = dot_halves(phi[...], charged[...], 1)
    part = jnp.concatenate([part, jnp.zeros((8 * GROUP - NM, CS), f32)], axis=0)
    groups = [part[GROUP * g : GROUP * (g + 1), :] for g in range(8)]
    return jnp.concatenate([jnp.zeros((MOMENTS - LAST, SEG), f32), jnp.concatenate(groups, axis=1)], axis=0)


def far_kernel_body(*refs):
    raw, sources, out, scratch = refs[:6], refs[6:10], refs[10], refs[11:]
    cell, stress, off, tan, bur, operator, sems, around, shifted, phi, pots = scratch
    copies = fetch_all(raw, scratch[:6], sems)
    for copy in copies[:5]:
        copy.wait()
    fill_phi(phi, off)
    half = len(sources)
    count = 2 * half
    cells = count * CS
    turned = jnp.concatenate([source[...] for source in sources], axis=0).T
    first = MOMENTS - LAST
    for q in range(count):
        back = (count - q) % count
        at = CS * (2 * (back % half) + back // half) + first
        for g in range(8):
            piece = turned[CS * g : CS * (g + 1), at : at + GROUP]
            around[q * CS : (q + 1) * CS, GROUP * g : GROUP * (g + 1)] = piece
    around[cells : cells + CS, :] = around[0:CS, :]
    shifted[:, 0:NM] = jnp.zeros((CS, NM), f32)
    for o in range(1, cells):
        shifted[:, o * NM : (o + 1) * NM] = around[cells - o : cells - o + CS, 0:NM]
    copies[5].wait()
    local_exp = dot_halves(operator[...], shifted[...], 1).T
    high, low = halves_of(local_exp)
    phi_high, phi_low = halves_of(phi[...])
    made = jnp.dot(jnp.concatenate([high, low], axis=0), phi_high, preferred_element_type=f32)
    made = made[0:CS] + made[CS:]
    pots[...] = made + jnp.dot(high, phi_low, preferred_element_type=f32)
    b = [bur[i : i + 1, :] for i in range(3)]
    t = [tan[i : i + 1, :] for i in range(3)]
    sym = [[0.5 * (stress[i, j] + stress[j, i]) for j in range(3)] for i in range(3)]
    trac = [sym[i][0] * b[0] + sym[i][1] * b[1] + sym[i][2] * b[2] for i in range(3)]
    for i in range(3):
        j, k = (i + 1) % 3, (i + 2) % 3
        out[i : i + 1, :] = trac[j] * t[k] - trac[k] * t[j]
    row = iota((CS, SEG), 0)
    for block in range(cell.shape[0]):
        at = slice(block * SEG, (block + 1) * SEG)
        mine = jnp.where(row == cell[block], pots[:, at], 0.0)
        out[:, at] += jnp.sum(mine, axis=0, keepdims=True) * bur[:, at]


def final_kernel(back, near_all, far, conn, left, out, force, halves):
    groups = conn.shape[1] // SEG
    returned = back[...].reshape(back.shape[0] * 16, SEG)
    spread = jnp.where(iota((SEG, returned.shape[0]), 0) == left[0:1, :], 1.0, 0.0).astype(bf16)
    high, low = halves_of(returned)
    near = near_all[...] + jnp.dot(spread, high, preferred_element_type=f32)
    near = near + jnp.dot(spread, low, preferred_element_type=f32)
    for b in range(groups):
        at = slice(b * SEG, (b + 1) * SEG)
        force[0:3, at] = 0.5 * (far[:, at] + near[4 * b : 4 * b + 3, :])
    value = force[0:3, :]
    high = value.astype(bf16).astype(f32)
    halves[0:3, :] = high
    halves[3:6, :] = value - high
    chunk = 1024
    segs = conn.shape[1]
    total = jnp.zeros((6 * groups, SEG), f32)
    low_row, high_row = iota((SEG, chunk), 0), iota((groups, chunk), 0)
    for end in range(2):
        for start in range(0, segs, chunk):
            at = slice(start, start + chunk)
            node = conn[end : end + 1, at]
            low = jnp.where(low_row == (node & (SEG - 1)), 1.0, 0.0).astype(bf16)
            mark = high_row == (node >> 7)
            parts = [
                jnp.where(mark, halves[i : i + 1, at], 0.0).astype(bf16) for i in range(6)
            ]
            total = total + dot_nt(jnp.concatenate(parts, axis=0), low)
    for c in range(3):
        whole = total[c * groups : (c + 1) * groups] + total[(3 + c) * groups : (4 + c) * groups]
        for g in range(groups):
            out[c : c + 1, g * SEG : (g + 1) * SEG] = whole[g : g + 1, :]


def call(body, out_shape, in_specs, scratch, flops, size):
    return pl.pallas_call(
        body,
        out_shape=out_shape,
        in_specs=in_specs,
        out_specs=jax.tree.map(lambda _: VMEM, out_shape),
        scratch_shapes=scratch,
        compiler_params=pltpu.CompilerParams(vmem_limit_bytes=size << 20),
        cost_estimate=pl.CostEstimate(flops=flops, bytes_accessed=1 << 20, transcendentals=0),
    )


def local(
    seg_offset,
    tangent,
    burgers,
    box_matrix,
    applied_stress,
    far_kernel,
    block_cell,
    fetch_table,
    pair_list,
    image_shift,
    pair_count,
    node_conn,
):
    blocks = block_cell.shape[0]
    segs = seg_offset.shape[1]
    peers = lax.axis_size("bulk")
    slabs = lax.axis_size("slab")
    shape = lambda *dims: jax.ShapeDtypeStruct(dims, f32)
    table = pltpu.VMEM((16, segs), f32)

    raw = [pair_list, box_matrix, block_cell]
    segments = [seg_offset, tangent, burgers]
    vectors = [image_shift, fetch_table.T, *segments]
    send = call(
        pack_kernel,
        shape(peers, ROWS, SEG),
        [HBM] * 8,
        [pltpu.SMEM(x.shape, x.dtype) for x in raw]
        + [pltpu.VMEM(x.shape, x.dtype) for x in vectors]
        + [pltpu.SemaphoreType.DMA((8,))]
        + [table, pltpu.VMEM((NM, segs), f32), pltpu.VMEM((CS, segs), f32)],
        10**6,
        60,
    )(*raw, *vectors)
    recv = lax.all_to_all(send, "bulk", 0, 0, tiled=True)

    features, near_own, left = call(
        own_kernel,
        (
            jax.ShapeDtypeStruct((blocks, SEG, FEATURES), bf16),
            shape(SEG, SEG),
            jax.ShapeDtypeStruct((8, peers * 16), jnp.int32),
        ),
        [SMEM] * 4 + [VMEM] * 4,
        [
            table,
            pltpu.VMEM((blocks, 3, SEG, SEG), f32),
            pltpu.VMEM((blocks, 8, SEG), f32),
        ],
        10**9,
        12,
    )(pair_list, image_shift, box_matrix, pair_count, *segments, pair_list)

    def from_slab(value, back):
        return lax.ppermute(value, "slab", [(s, (s + back) % slabs) for s in range(slabs)])

    half = slabs // 2
    moments = jnp.sum(recv[:, LAST:, :], axis=0)
    other = from_slab(moments, half)

    ret, near = call(
        pair_kernel,
        (shape(peers, 16, SEG), shape(SEG, SEG)),
        [VMEM] * 3,
        [
            pltpu.VMEM((blocks, 3, SEG, SEG), f32),
            pltpu.VMEM((peers, SEG), jnp.int32),
            pltpu.SMEM((peers, SEG), jnp.int32),
            pltpu.SemaphoreType.DMA,
        ],
        10**10,
        16,
    )(recv, features, near_own)
    ret, other = lax.optimization_barrier((ret, other))
    back = lax.all_to_all(ret, "bulk", 0, 0, tiled=True)
    two = jnp.concatenate([moments, other], axis=0)
    sources = [two] + [from_slab(two, k) for k in range(1, half)]
    raw = [block_cell, applied_stress]
    far = call(
        far_kernel_body,
        shape(3, segs),
        [HBM] * 6 + [VMEM] * half,
        [pltpu.SMEM(x.shape, x.dtype) for x in raw]
        + [pltpu.VMEM(x.shape, x.dtype) for x in segments + [far_kernel]]
        + [
            pltpu.SemaphoreType.DMA((6,)),
            pltpu.VMEM((slabs * CS + CS, SEG), f32),
            pltpu.VMEM((CS, slabs * CS * NM), f32),
            pltpu.VMEM((NM, segs), f32),
            pltpu.VMEM((CS, segs), f32),
        ],
        10**9,
        52,
    )(*raw, *segments, far_kernel, *sources)

    return call(
        final_kernel,
        shape(3, segs),
        [VMEM] * 5,
        [pltpu.VMEM((8, segs), f32), pltpu.VMEM((8, segs), f32)],
        10**9,
        24,
    )(back, near, far, node_conn, left)


def solution(mesh):
    both = P(None, ("slab", "bulk"))
    in_specs = (
        both,
        both,
        both,
        P(),
        P(),
        P(),
        P(("slab", "bulk")),
        P(("slab", "bulk"), None),
        both,
        both,
        P(("slab", "bulk")),
        both,
    )
    return jax.shard_map(local, mesh=mesh, in_specs=in_specs, out_specs=both, check_vma=False)
```

```python
import jax
import jax.numpy as jnp
from jax import lax
from jax.experimental import pallas as pl
from jax.experimental.pallas import tpu as pltpu
from jax.sharding import PartitionSpec as P

SEG = 128
CS = 16
NM = 84
SEND = 5
LAST = 40
META = 45
ROWS = 48
FEATURES = 64
KAPPA = 0.2
CORE_SQ = 0.25
VMEM = pl.BlockSpec(memory_space=pltpu.VMEM)
HBM = pl.BlockSpec(memory_space=pltpu.HBM)
SMEM = pl.BlockSpec(memory_space=pltpu.SMEM)
f32 = jnp.float32
bf16 = jnp.bfloat16


def exponents():
    return [(a, b, c) for a in range(7) for b in range(7 - a) for c in range(7 - a - b)]


def iota(shape, dim):
    return lax.broadcasted_iota(jnp.int32, shape, dim)


def lane_block(index):
    return pl.ds(pl.multiple_of(index * SEG, SEG), SEG)


def fill_table(table, off, tan, bur, diag, cross):
    b = [bur[i : i + 1, :] for i in range(3)]
    t = [tan[i : i + 1, :] for i in range(3)]
    table[0:3, :] = off[...]
    for i in range(3):
        table[3 + i : 4 + i, :] = diag * (b[i] * t[i])
    for row, (i, j) in enumerate(((0, 1), (0, 2), (1, 2))):
        table[6 + row : 7 + row, :] = cross * (b[i] * t[j] + b[j] * t[i])


def shift_of(box, shift, k):
    s = [shift[i, k].astype(f32) for i in range(3)]
    return [box[c, 0] * s[0] + box[c, 1] * s[1] + box[c, 2] * s[2] for c in range(3)]


def shift_rows(vec, shape):
    row = iota(shape, 0)
    return jnp.where(row == 0, vec[0], jnp.where(row == 1, vec[1], jnp.where(row == 2, vec[2], 0.0)))


def fetch_all(sources, targets, sems):
    copies = [
        pltpu.make_async_copy(source, target, sems.at[i])
        for i, (source, target) in enumerate(zip(sources, targets, strict=True))
    ]
    for copy in copies:
        copy.start()
    return copies


def shift_table(box, shift):
    steps = [shift[i : i + 1, :].astype(f32) for i in range(3)]
    rows = [box[c, 0] * steps[0] + box[c, 1] * steps[1] + box[c, 2] * steps[2] for c in range(3)]
    return jnp.concatenate(rows + [jnp.zeros((5, shift.shape[1]), f32)], axis=0)


def pack_kernel(*refs):
    sources, send, scratch = refs[:7], refs[7], refs[8:]
    pairs, box, shift, fetch, off, tan, bur, sems, table = scratch
    for copy in fetch_all(sources, scratch[:7], sems):
        copy.wait()
    fill_table(table, off, tan, bur, 2.0 * KAPPA, KAPPA)
    vectors = shift_table(box, shift)
    peers = send.shape[0]
    wide = jnp.concatenate([fetch[...].astype(f32), jnp.zeros((SEND, SEG - peers), f32)], axis=1)
    meta = jnp.concatenate([wide, jnp.zeros((8 - SEND, SEG), f32)], axis=0).T
    meta = jnp.concatenate([meta, jnp.zeros((SEG, SEG - 8), f32)], axis=1)
    row = iota((ROWS - LAST, SEG), 0)
    for p in range(peers):
        rest = jnp.where(row == META - LAST, meta[p : p + 1, :], 0.0)
        for s in range(SEND):
            k = p * SEND + s
            at = lane_block(pairs[0, k])
            vec = jnp.broadcast_to(vectors[:, k : k + 1], (8, SEG))
            send[p, 8 * s : 8 * s + 8, :] = table[0:8, at] - vec
            rest = jnp.where(row == s, table[8:9, at], rest)
        send[p, LAST:ROWS, :] = rest


def split(value):
    high = value.astype(bf16).astype(f32)
    rest = value - high
    mid = rest.astype(bf16).astype(f32)
    return high, mid, (rest - mid).astype(bf16).astype(f32)


def fill_features(table, features):
    first = iota((8, SEG), 0) < 3
    one, none = jnp.ones((3, SEG), f32), jnp.zeros((1, SEG), f32)

    def block(b, carry):
        at = lane_block(b)
        head = table[0:8, at]
        high, mid, low = split(head)
        last_high, last_mid, _ = split(table[8:9, at])
        square = split(jnp.sum(jnp.where(first, head * head, 0.0), axis=0, keepdims=True))
        groups = [jnp.where(first, 1.0, high)] * 2
        groups.append(
            jnp.concatenate([one, last_high, last_high, last_mid, square[0], square[1]], axis=0)
        )
        groups.append(jnp.where(first, high, mid))
        groups.append(jnp.concatenate([mid[0:3], low[0:3], square[2], none], axis=0))
        groups.append(jnp.concatenate([high[0:3], high[0:3], none, none], axis=0))
        groups.append(jnp.concatenate([mid[0:3], one, none, none], axis=0))
        groups.append(jnp.zeros((SEG - 56, SEG), f32))
        turned = jnp.concatenate(groups, axis=0).T
        features[b] = turned[:, 0:FEATURES].astype(bf16)
        return carry

    lax.fori_loop(0, features.shape[0], block, 0, unroll=4)


def weights(head, last):
    row = iota((8, SEG), 0)
    first, second = row < 3, (row >= 3) & (row < 6)
    high, mid, low = split(head)
    last_high, last_mid, _ = split(last)
    square = split(jnp.sum(jnp.where(first, head * head, 0.0), axis=0, keepdims=True) + CORE_SQ)
    none = jnp.zeros((8, SEG), f32)
    columns = []
    for i in range(3):
        own = row == i
        parts = [jnp.where(own, part, 0.0) for part in (high, mid, low, -1.0)]
        parts += [jnp.where(own | (row == i + 3), -1.0, 0.0), none, none, none]
        columns.append(jnp.concatenate(parts, axis=0))
    tail = jnp.where(first, 0.0, high)
    edge = jnp.where((row == 3) | (row == 5), last_high, jnp.where(row == 4, last_mid, 0.0))
    parts = [tail, jnp.where(first, 0.0, mid), edge, tail, none, none, none, none]
    columns.append(jnp.concatenate(parts, axis=0))
    twice = [-2.0 * part for part in (high, mid, low)]
    below = [jnp.concatenate([part[0:3], part[0:3], part[0:2]], axis=0) for part in twice]
    norm = jnp.where(row == 3, square[0], jnp.where(row == 4, square[1], square[2]))
    parts = [none, none, jnp.where(row >= 6, 1.0, 0.0), jnp.where(first, twice[0], 0.0)]
    parts.append(jnp.where(row < 6, below[0], jnp.where(row == 6, 1.0, 0.0)))
    parts.append(jnp.where(first, twice[1], jnp.where(second, below[2], 0.0)))
    parts += [jnp.where(first, twice[1], jnp.where(second, norm, 0.0)), none]
    columns.append(jnp.concatenate(parts, axis=0))
    return jnp.concatenate(columns, axis=1).astype(bf16)


def tile(head, last, features, acc, b):
    both = weights(head, last)
    sums = [jnp.zeros((8, SEG), f32) for _ in range(3)]
    step = 64
    for start in range(0, SEG, step):
        at = slice(start, start + step)
        made = jnp.dot(features[b, at, :], both, preferred_element_type=f32)
        inv = lax.rsqrt(made[:, 4 * SEG :])
        weight = made[:, 3 * SEG : 4 * SEG] * (inv * inv * inv)
        for c in range(3):
            push = weight * made[:, c * SEG : (c + 1) * SEG]
            acc[b, c, at, :] += push
            for r in range(0, step, 8):
                sums[c] = sums[c] + push[r : r + 8]
    return [jnp.sum(part, axis=0, keepdims=True) for part in sums]


def fold(acc, near, others):
    def pair(half, carry):
        at = pl.ds(pl.multiple_of(8 * half, 8), 8)
        rows = []
        for b in (2 * half, 2 * half + 1):
            rows += [jnp.sum(acc[b, c].T, axis=0, keepdims=True) for c in range(3)]
            rows.append(jnp.zeros((1, SEG), f32))
        near[at, :] = others[at, :] - jnp.concatenate(rows, axis=0)
        return carry

    lax.fori_loop(0, acc.shape[0] // 2, pair, 0, unroll=True)


def clear(acc):
    def block(b, carry):
        acc[b] = jnp.zeros(acc.shape[1:], f32)
        return carry

    lax.fori_loop(0, acc.shape[0], block, 0, unroll=4)


def left_rows(blocks, out_shape):
    slots = blocks.shape[1]
    slot, lane = iota((slots, out_shape[1]), 0), iota((slots, out_shape[1]), 1)
    peer, rest = lane >> 4, lane & 15
    third = (rest >= 3).astype(jnp.int32) + (rest >= 6) + (rest >= 9) + (rest >= 12)
    pick = (slot == SEND * peer + third) & (rest < 15)
    tall = jnp.broadcast_to(blocks.astype(f32), (16, slots)).astype(bf16)
    found = jnp.dot(tall, jnp.where(pick, 1.0, 0.0).astype(bf16), preferred_element_type=f32)
    lane = iota(out_shape, 1)
    rest = lane & 15
    third = (rest >= 3).astype(jnp.int32) + (rest >= 6) + (rest >= 9) + (rest >= 12)
    row = 4 * found[0 : out_shape[0]].astype(jnp.int32) + rest - 3 * third
    return jnp.where(rest < 15, row, -1)


def own_kernel(
    pairs, shift, box, count, off, tan, bur, pairs_row, features, near, left, table, acc, left_acc
):
    left[...] = left_rows(pairs_row[0:1, :], left.shape)
    clear(acc)
    left_acc[...] = jnp.zeros_like(left_acc)
    fill_table(table, off, tan, bur, 1.0, 1.0)
    fill_features(table, features)
    blocks = acc.shape[0]
    row = iota((8, SEG), 0)
    scale = jnp.where(row < 3, 1.0, jnp.where(row < 6, 2.0 * KAPPA, KAPPA))

    def pair(k, carry):
        a, b = pairs[0, k], pairs[1, k]
        at = lane_block(a)
        head = table[0:8, at] * scale - shift_rows(shift_of(box, shift, k), (8, SEG))
        rows = tile(head, table[8:9, at] * KAPPA, features, acc, b)
        for c in range(3):
            left_acc[a, c : c + 1, :] += rows[c]
        return carry

    lax.fori_loop(pairs.shape[1] - blocks, count[0], pair, 0)
    for b in range(blocks):
        near[4 * b : 4 * b + 4, :] = left_acc[b, 0:4, :]
    fold(acc, near, near)


def pair_kernel(recv, features, near_own, ret, near, acc, ids_vmem, ids, sem):
    peers = recv.shape[0]
    for p in range(peers):
        ids_vmem[p : p + 1, :] = recv[p, META : META + 1, :].astype(jnp.int32)
    copy = pltpu.make_async_copy(ids_vmem, ids, sem)
    copy.start()
    clear(acc)
    copy.wait()

    def peer(p, carry):
        for s in range(SEND):
            head, last = recv[p, 8 * s : 8 * s + 8, :], recv[p, LAST + s : LAST + s + 1, :]
            rows = tile(head, last, features, acc, ids[p, s])
            for c in range(3):
                ret[p, 3 * s + c : 3 * s + c + 1, :] = rows[c]
        ret[p, 15:16, :] = jnp.zeros((1, SEG), f32)
        return carry

    lax.fori_loop(0, peers, peer, 0, unroll=8)
    fold(acc, near, near_own)


def fill_phi(phi, off):
    powers = []
    for i in range(3):
        x = off[i : i + 1, :]
        made = [None, x]
        for _ in range(5):
            made.append(made[-1] * x)
        powers.append(made)
    pairs_of = {}
    for k, (a, b, c) in enumerate(exponents()):
        if (a, b) not in pairs_of:
            got = [p for p in (powers[0][a], powers[1][b]) if p is not None]
            pairs_of[a, b] = got[0] * got[1] if len(got) == 2 else got[0] if got else None
        value = pairs_of[a, b]
        if c:
            value = powers[2][c] if value is None else value * powers[2][c]
        phi[k : k + 1, :] = jnp.ones_like(powers[0][1]) if value is None else value


def dot_nt(left, right):
    return lax.dot_general(
        left, right, (((1,), (1,)), ((), ())), preferred_element_type=f32
    )


def halves_of(value):
    high = value.astype(bf16)
    return high, (value - high.astype(f32)).astype(bf16)


def dot_halves(left, right, axis):
    left_high, left_low = halves_of(left)
    right_high, right_low = halves_of(right)
    dims = (((1,), (axis,)), ((), ()))
    count = right.shape[1 - axis]
    both = jnp.concatenate([right_high, right_low], axis=1 - axis)
    made = lax.dot_general(left_high, both, dims, preferred_element_type=f32)
    made = made[:, :count] + made[:, count:]
    return made + lax.dot_general(left_low, right_high, dims, preferred_element_type=f32)


def moment_kernel(cell, off, tan, bur, out, phi, charged):
    fill_phi(phi, off)
    charge = jnp.sum(bur[...] * tan[...], axis=0, keepdims=True)
    row = iota((CS, SEG), 0)
    for b in range(cell.shape[0]):
        part = charge[:, b * SEG : (b + 1) * SEG]
        charged[:, b * SEG : (b + 1) * SEG] = jnp.where(row == cell[b], part, 0.0)
    part = dot_halves(phi[...], charged[...], 1).T
    out[...] = jnp.concatenate([part, jnp.zeros((CS, SEG - NM), f32)], axis=1)


def far_kernel_body(*refs):
    raw, sources, out, scratch = refs[:6], refs[6:10], refs[10], refs[11:]
    cell, stress, off, tan, bur, operator, sems, around, shifted, phi, pots = scratch
    copies = fetch_all(raw, scratch[:6], sems)
    for copy in copies[:5]:
        copy.wait()
    fill_phi(phi, off)
    half = len(sources)
    count = 2 * half
    cells = count * CS
    for q in range(count):
        back = (count - q) % count
        at = CS * (back // half)
        around[q * CS : (q + 1) * CS, :] = sources[back % half][at : at + CS, :]
    around[cells : cells + CS, :] = around[0:CS, :]
    shifted[:, 0:NM] = jnp.zeros((CS, NM), f32)
    for o in range(1, cells):
        shifted[:, o * NM : (o + 1) * NM] = around[cells - o : cells - o + CS, 0:NM]
    copies[5].wait()
    local_exp = dot_halves(operator[...], shifted[...], 1).T
    high, low = halves_of(local_exp)
    phi_high, phi_low = halves_of(phi[...])
    made = jnp.dot(jnp.concatenate([high, low], axis=0), phi_high, preferred_element_type=f32)
    made = made[0:CS] + made[CS:]
    pots[...] = made + jnp.dot(high, phi_low, preferred_element_type=f32)
    b = [bur[i : i + 1, :] for i in range(3)]
    t = [tan[i : i + 1, :] for i in range(3)]
    sym = [[0.5 * (stress[i, j] + stress[j, i]) for j in range(3)] for i in range(3)]
    trac = [sym[i][0] * b[0] + sym[i][1] * b[1] + sym[i][2] * b[2] for i in range(3)]
    for i in range(3):
        j, k = (i + 1) % 3, (i + 2) % 3
        out[i : i + 1, :] = trac[j] * t[k] - trac[k] * t[j]
    row = iota((CS, SEG), 0)
    for block in range(cell.shape[0]):
        at = slice(block * SEG, (block + 1) * SEG)
        mine = jnp.where(row == cell[block], pots[:, at], 0.0)
        out[:, at] += jnp.sum(mine, axis=0, keepdims=True) * bur[:, at]


def final_kernel(back, near_all, far, conn, left, out, force, halves):
    groups = conn.shape[1] // SEG
    returned = back[...].reshape(back.shape[0] * 16, SEG)
    spread = jnp.where(iota((SEG, returned.shape[0]), 0) == left[0:1, :], 1.0, 0.0).astype(bf16)
    high, low = halves_of(returned)
    near = near_all[...] + jnp.dot(spread, high, preferred_element_type=f32)
    near = near + jnp.dot(spread, low, preferred_element_type=f32)
    for b in range(groups):
        at = slice(b * SEG, (b + 1) * SEG)
        force[0:3, at] = 0.5 * (far[:, at] + near[4 * b : 4 * b + 3, :])
    value = force[0:3, :]
    high = value.astype(bf16).astype(f32)
    halves[0:3, :] = high
    halves[3:6, :] = value - high
    chunk = 1024
    segs = conn.shape[1]
    total = jnp.zeros((6 * groups, SEG), f32)
    low_row, high_row = iota((SEG, chunk), 0), iota((groups, chunk), 0)
    for end in range(2):
        for start in range(0, segs, chunk):
            at = slice(start, start + chunk)
            node = conn[end : end + 1, at]
            low = jnp.where(low_row == (node & (SEG - 1)), 1.0, 0.0).astype(bf16)
            mark = high_row == (node >> 7)
            parts = [
                jnp.where(mark, halves[i : i + 1, at], 0.0).astype(bf16) for i in range(6)
            ]
            total = total + dot_nt(jnp.concatenate(parts, axis=0), low)
    for c in range(3):
        whole = total[c * groups : (c + 1) * groups] + total[(3 + c) * groups : (4 + c) * groups]
        for g in range(groups):
            out[c : c + 1, g * SEG : (g + 1) * SEG] = whole[g : g + 1, :]


def call(body, out_shape, in_specs, scratch, flops, size):
    return pl.pallas_call(
        body,
        out_shape=out_shape,
        in_specs=in_specs,
        out_specs=jax.tree.map(lambda _: VMEM, out_shape),
        scratch_shapes=scratch,
        compiler_params=pltpu.CompilerParams(vmem_limit_bytes=size << 20),
        cost_estimate=pl.CostEstimate(flops=flops, bytes_accessed=1 << 20, transcendentals=0),
    )


def local(
    seg_offset,
    tangent,
    burgers,
    box_matrix,
    applied_stress,
    far_kernel,
    block_cell,
    fetch_table,
    pair_list,
    image_shift,
    pair_count,
    node_conn,
):
    blocks = block_cell.shape[0]
    segs = seg_offset.shape[1]
    peers = lax.axis_size("bulk")
    slabs = lax.axis_size("slab")
    shape = lambda *dims: jax.ShapeDtypeStruct(dims, f32)
    table = pltpu.VMEM((16, segs), f32)

    raw = [pair_list, box_matrix]
    segments = [seg_offset, tangent, burgers]
    vectors = [image_shift, fetch_table.T, *segments]
    send = call(
        pack_kernel,
        shape(peers, ROWS, SEG),
        [HBM] * 7,
        [pltpu.SMEM(x.shape, x.dtype) for x in raw]
        + [pltpu.VMEM(x.shape, x.dtype) for x in vectors]
        + [pltpu.SemaphoreType.DMA((7,)), table],
        10**6,
        60,
    )(*raw, *vectors)
    recv = lax.all_to_all(send, "bulk", 0, 0, tiled=True)

    moments = call(
        moment_kernel,
        shape(CS, SEG),
        [SMEM] + [VMEM] * 3,
        [pltpu.VMEM((NM, segs), f32), pltpu.VMEM((CS, segs), f32)],
        10**9,
        12,
    )(block_cell, *segments)
    inner = 8
    outer = peers // inner

    def from_bulk(value, up, along):
        to = lambda j: (j // inner + up) % outer * inner + (j % inner + along) % inner
        return lax.ppermute(value, "bulk", [(j, to(j)) for j in range(peers)])

    moments = moments + sum(from_bulk(moments, k, 0) for k in range(1, outer))
    moments = moments + from_bulk(moments, 0, inner // 2)
    moments = moments + sum(from_bulk(moments, 0, k) for k in range(1, inner // 2))

    features, near_own, left = call(
        own_kernel,
        (
            jax.ShapeDtypeStruct((blocks, SEG, FEATURES), bf16),
            shape(SEG, SEG),
            jax.ShapeDtypeStruct((8, peers * 16), jnp.int32),
        ),
        [SMEM] * 4 + [VMEM] * 4,
        [
            table,
            pltpu.VMEM((blocks, 3, SEG, SEG), f32),
            pltpu.VMEM((blocks, 8, SEG), f32),
        ],
        10**9,
        12,
    )(pair_list, image_shift, box_matrix, pair_count, *segments, pair_list)

    def from_slab(value, back):
        return lax.ppermute(value, "slab", [(s, (s + back) % slabs) for s in range(slabs)])

    half = slabs // 2
    other = from_slab(moments, half)

    ret, near = call(
        pair_kernel,
        (shape(peers, 16, SEG), shape(SEG, SEG)),
        [VMEM] * 3,
        [
            pltpu.VMEM((blocks, 3, SEG, SEG), f32),
            pltpu.VMEM((peers, SEG), jnp.int32),
            pltpu.SMEM((peers, SEG), jnp.int32),
            pltpu.SemaphoreType.DMA,
        ],
        10**10,
        16,
    )(recv, features, near_own)
    ret, other = lax.optimization_barrier((ret, other))
    back = lax.all_to_all(ret, "bulk", 0, 0, tiled=True)
    two = jnp.concatenate([moments, other], axis=0)
    sources = [two] + [from_slab(two, k) for k in range(1, half)]
    raw = [block_cell, applied_stress]
    far = call(
        far_kernel_body,
        shape(3, segs),
        [HBM] * 6 + [VMEM] * half,
        [pltpu.SMEM(x.shape, x.dtype) for x in raw]
        + [pltpu.VMEM(x.shape, x.dtype) for x in segments + [far_kernel]]
        + [
            pltpu.SemaphoreType.DMA((6,)),
            pltpu.VMEM((slabs * CS + CS, SEG), f32),
            pltpu.VMEM((CS, slabs * CS * NM), f32),
            pltpu.VMEM((NM, segs), f32),
            pltpu.VMEM((CS, segs), f32),
        ],
        10**9,
        52,
    )(*raw, *segments, far_kernel, *sources)

    return call(
        final_kernel,
        shape(3, segs),
        [VMEM] * 5,
        [pltpu.VMEM((8, segs), f32), pltpu.VMEM((8, segs), f32)],
        10**9,
        24,
    )(back, near, far, node_conn, left)


def solution(mesh):
    both = P(None, ("slab", "bulk"))
    in_specs = (
        both,
        both,
        both,
        P(),
        P(),
        P(),
        P(("slab", "bulk")),
        P(("slab", "bulk"), None),
        both,
        both,
        P(("slab", "bulk")),
        both,
    )
    return jax.shard_map(local, mesh=mesh, in_specs=in_specs, out_specs=both, check_vma=False)
```

```python
import jax
import jax.numpy as jnp
from jax import lax
from jax.experimental import pallas as pl
from jax.experimental.pallas import tpu as pltpu
from jax.sharding import PartitionSpec as P

SEG = 128
CS = 16
NM = 84
TALL = 96
SEND = 5
LAST = 40
MOMENTS = 45
ROWS = 56
GROUP = 11
META = 112
FEATURES = 64
KAPPA = 0.2
CORE_SQ = 0.25
VMEM = pl.BlockSpec(memory_space=pltpu.VMEM)
HBM = pl.BlockSpec(memory_space=pltpu.HBM)
SMEM = pl.BlockSpec(memory_space=pltpu.SMEM)
f32 = jnp.float32
bf16 = jnp.bfloat16


def exponents():
    return [(a, b, c) for a in range(7) for b in range(7 - a) for c in range(7 - a - b)]


def iota(shape, dim):
    return lax.broadcasted_iota(jnp.int32, shape, dim)


def lane_block(index):
    return pl.ds(pl.multiple_of(index * SEG, SEG), SEG)


def fill_table(table, off, tan, bur, diag, cross):
    b = [bur[i : i + 1, :] for i in range(3)]
    t = [tan[i : i + 1, :] for i in range(3)]
    table[0:3, :] = off[...]
    for i in range(3):
        table[3 + i : 4 + i, :] = diag * (b[i] * t[i])
    for row, (i, j) in enumerate(((0, 1), (0, 2), (1, 2))):
        table[6 + row : 7 + row, :] = cross * (b[i] * t[j] + b[j] * t[i])


def shift_of(box, shift, k):
    s = [shift[i, k].astype(f32) for i in range(3)]
    return [box[c, 0] * s[0] + box[c, 1] * s[1] + box[c, 2] * s[2] for c in range(3)]


def shift_rows(vec, shape):
    row = iota(shape, 0)
    return jnp.where(row == 0, vec[0], jnp.where(row == 1, vec[1], jnp.where(row == 2, vec[2], 0.0)))


def fetch_all(sources, targets, sems):
    copies = [
        pltpu.make_async_copy(source, target, sems.at[i])
        for i, (source, target) in enumerate(zip(sources, targets, strict=True))
    ]
    for copy in copies:
        copy.start()
    return copies


def shift_table(box, shift):
    steps = [shift[i : i + 1, :].astype(f32) for i in range(3)]
    rows = [box[c, 0] * steps[0] + box[c, 1] * steps[1] + box[c, 2] * steps[2] for c in range(3)]
    return jnp.concatenate(rows + [jnp.zeros((5, shift.shape[1]), f32)], axis=0)


def pack_kernel(*refs):
    sources, send, scratch = refs[:8], refs[8], refs[9:]
    pairs, box, cell, shift, fetch, off, tan, bur, sems, table, phi, charged = scratch
    for copy in fetch_all(sources, scratch[:8], sems):
        copy.wait()
    fill_table(table, off, tan, bur, 2.0 * KAPPA, KAPPA)
    packed = cell_moments(cell, off, tan, bur, phi, charged)
    vectors = shift_table(box, shift)
    peers = send.shape[0]
    wide = jnp.concatenate([fetch[...].astype(f32), jnp.zeros((SEND, SEG - peers), f32)], axis=1)
    tall = jnp.concatenate([wide, jnp.zeros((8 - SEND, SEG), f32)], axis=0).T
    meta = jnp.concatenate(
        [jnp.zeros((SEG, META), f32), tall, jnp.zeros((SEG, SEG - META - 8), f32)], axis=1
    )
    row, lane = iota((ROWS - LAST, SEG), 0), iota((ROWS - LAST, SEG), 1)
    mark = (row == ROWS - LAST - 1) & (lane >= META)
    for p in range(peers):
        rest = jnp.where(mark, meta[p : p + 1, :], packed)
        for s in range(SEND):
            k = p * SEND + s
            at = lane_block(pairs[0, k])
            vec = jnp.broadcast_to(vectors[:, k : k + 1], (8, SEG))
            send[p, 8 * s : 8 * s + 8, :] = table[0:8, at] - vec
            rest = jnp.where(row == s, table[8:9, at], rest)
        send[p, LAST:ROWS, :] = rest


def split(value):
    high = value.astype(bf16).astype(f32)
    rest = value - high
    mid = rest.astype(bf16).astype(f32)
    return high, mid, (rest - mid).astype(bf16).astype(f32)


def fill_features(table, features):
    first = iota((8, SEG), 0) < 3
    one, none = jnp.ones((3, SEG), f32), jnp.zeros((1, SEG), f32)

    def block(b, carry):
        at = lane_block(b)
        head = table[0:8, at]
        high, mid, low = split(head)
        last_high, last_mid, _ = split(table[8:9, at])
        square = split(jnp.sum(jnp.where(first, head * head, 0.0), axis=0, keepdims=True))
        groups = [jnp.where(first, 1.0, high)] * 2
        groups.append(
            jnp.concatenate([one, last_high, last_high, last_mid, square[0], square[1]], axis=0)
        )
        groups.append(jnp.where(first, high, mid))
        groups.append(jnp.concatenate([mid[0:3], low[0:3], square[2], none], axis=0))
        groups.append(jnp.concatenate([high[0:3], high[0:3], none, none], axis=0))
        groups.append(jnp.concatenate([mid[0:3], one, none, none], axis=0))
        groups.append(jnp.zeros((SEG - 56, SEG), f32))
        turned = jnp.concatenate(groups, axis=0).T
        features[b] = turned[:, 0:FEATURES].astype(bf16)
        return carry

    lax.fori_loop(0, features.shape[0], block, 0, unroll=4)


def weights(head, last):
    row = iota((8, SEG), 0)
    first, second = row < 3, (row >= 3) & (row < 6)
    high, mid, low = split(head)
    last_high, last_mid, _ = split(last)
    square = split(jnp.sum(jnp.where(first, head * head, 0.0), axis=0, keepdims=True) + CORE_SQ)
    none = jnp.zeros((8, SEG), f32)
    columns = []
    for i in range(3):
        own = row == i
        parts = [jnp.where(own, part, 0.0) for part in (high, mid, low, -1.0)]
        parts += [jnp.where(own | (row == i + 3), -1.0, 0.0), none, none, none]
        columns.append(jnp.concatenate(parts, axis=0))
    tail = jnp.where(first, 0.0, high)
    edge = jnp.where((row == 3) | (row == 5), last_high, jnp.where(row == 4, last_mid, 0.0))
    parts = [tail, jnp.where(first, 0.0, mid), edge, tail, none, none, none, none]
    columns.append(jnp.concatenate(parts, axis=0))
    twice = [-2.0 * part for part in (high, mid, low)]
    below = [jnp.concatenate([part[0:3], part[0:3], part[0:2]], axis=0) for part in twice]
    norm = jnp.where(row == 3, square[0], jnp.where(row == 4, square[1], square[2]))
    parts = [none, none, jnp.where(row >= 6, 1.0, 0.0), jnp.where(first, twice[0], 0.0)]
    parts.append(jnp.where(row < 6, below[0], jnp.where(row == 6, 1.0, 0.0)))
    parts.append(jnp.where(first, twice[1], jnp.where(second, below[2], 0.0)))
    parts += [jnp.where(first, twice[1], jnp.where(second, norm, 0.0)), none]
    columns.append(jnp.concatenate(parts, axis=0))
    return jnp.concatenate(columns, axis=1).astype(bf16)


def tile(head, last, features, acc, b):
    both = weights(head, last)
    sums = [jnp.zeros((8, SEG), f32) for _ in range(3)]
    step = 64
    for start in range(0, SEG, step):
        at = slice(start, start + step)
        made = jnp.dot(features[b, at, :], both, preferred_element_type=f32)
        inv = lax.rsqrt(made[:, 4 * SEG :])
        weight = made[:, 3 * SEG : 4 * SEG] * (inv * inv * inv)
        for c in range(3):
            push = weight * made[:, c * SEG : (c + 1) * SEG]
            acc[b, c, at, :] += push
            for r in range(0, step, 8):
                sums[c] = sums[c] + push[r : r + 8]
    return [jnp.sum(part, axis=0, keepdims=True) for part in sums]


def fold(acc, near, others):
    def pair(half, carry):
        at = pl.ds(pl.multiple_of(8 * half, 8), 8)
        rows = []
        for b in (2 * half, 2 * half + 1):
            rows += [jnp.sum(acc[b, c].T, axis=0, keepdims=True) for c in range(3)]
            rows.append(jnp.zeros((1, SEG), f32))
        near[at, :] = others[at, :] - jnp.concatenate(rows, axis=0)
        return carry

    lax.fori_loop(0, acc.shape[0] // 2, pair, 0, unroll=True)


def clear(acc):
    def block(b, carry):
        acc[b] = jnp.zeros(acc.shape[1:], f32)
        return carry

    lax.fori_loop(0, acc.shape[0], block, 0, unroll=4)


def left_rows(blocks, out_shape):
    slots = blocks.shape[1]
    slot, lane = iota((slots, out_shape[1]), 0), iota((slots, out_shape[1]), 1)
    peer, rest = lane >> 4, lane & 15
    third = (rest >= 3).astype(jnp.int32) + (rest >= 6) + (rest >= 9) + (rest >= 12)
    pick = (slot == SEND * peer + third) & (rest < 15)
    tall = jnp.broadcast_to(blocks.astype(f32), (16, slots)).astype(bf16)
    found = jnp.dot(tall, jnp.where(pick, 1.0, 0.0).astype(bf16), preferred_element_type=f32)
    lane = iota(out_shape, 1)
    rest = lane & 15
    third = (rest >= 3).astype(jnp.int32) + (rest >= 6) + (rest >= 9) + (rest >= 12)
    row = 4 * found[0 : out_shape[0]].astype(jnp.int32) + rest - 3 * third
    return jnp.where(rest < 15, row, -1)


def own_kernel(
    pairs, shift, box, count, off, tan, bur, pairs_row, features, near, left, table, acc, left_acc
):
    left[...] = left_rows(pairs_row[0:1, :], left.shape)
    clear(acc)
    left_acc[...] = jnp.zeros_like(left_acc)
    fill_table(table, off, tan, bur, 1.0, 1.0)
    fill_features(table, features)
    blocks = acc.shape[0]
    row = iota((8, SEG), 0)
    scale = jnp.where(row < 3, 1.0, jnp.where(row < 6, 2.0 * KAPPA, KAPPA))

    def pair(k, carry):
        a, b = pairs[0, k], pairs[1, k]
        at = lane_block(a)
        head = table[0:8, at] * scale - shift_rows(shift_of(box, shift, k), (8, SEG))
        rows = tile(head, table[8:9, at] * KAPPA, features, acc, b)
        for c in range(3):
            left_acc[a, c : c + 1, :] += rows[c]
        return carry

    lax.fori_loop(pairs.shape[1] - blocks, count[0], pair, 0)
    for b in range(blocks):
        near[4 * b : 4 * b + 4, :] = left_acc[b, 0:4, :]
    fold(acc, near, near)


def pair_kernel(recv, features, near_own, ret, near, acc, ids_vmem, ids, sem):
    peers = recv.shape[0]
    for p in range(peers):
        ids_vmem[p : p + 1, :] = recv[p, ROWS - 1 : ROWS, :].astype(jnp.int32)
    copy = pltpu.make_async_copy(ids_vmem, ids, sem)
    copy.start()
    clear(acc)
    copy.wait()

    def peer(p, carry):
        for s in range(SEND):
            head, last = recv[p, 8 * s : 8 * s + 8, :], recv[p, LAST + s : LAST + s + 1, :]
            rows = tile(head, last, features, acc, ids[p, META + s])
            for c in range(3):
                ret[p, 3 * s + c : 3 * s + c + 1, :] = rows[c]
        ret[p, 15:16, :] = jnp.zeros((1, SEG), f32)
        return carry

    lax.fori_loop(0, peers, peer, 0, unroll=8)
    fold(acc, near, near_own)


def fill_phi(phi, off):
    powers = []
    for i in range(3):
        x = off[i : i + 1, :]
        made = [None, x]
        for _ in range(5):
            made.append(made[-1] * x)
        powers.append(made)
    pairs_of = {}
    for k, (a, b, c) in enumerate(exponents()):
        if (a, b) not in pairs_of:
            got = [p for p in (powers[0][a], powers[1][b]) if p is not None]
            pairs_of[a, b] = got[0] * got[1] if len(got) == 2 else got[0] if got else None
        value = pairs_of[a, b]
        if c:
            value = powers[2][c] if value is None else value * powers[2][c]
        phi[k : k + 1, :] = jnp.ones_like(powers[0][1]) if value is None else value


def dot_nt(left, right):
    return lax.dot_general(
        left, right, (((1,), (1,)), ((), ())), preferred_element_type=f32
    )


def halves_of(value):
    high = value.astype(bf16)
    return high, (value - high.astype(f32)).astype(bf16)


def dot_halves(left, right, axis):
    left_high, left_low = halves_of(left)
    right_high, right_low = halves_of(right)
    dims = (((1,), (axis,)), ((), ()))
    count = right.shape[1 - axis]
    both = jnp.concatenate([right_high, right_low], axis=1 - axis)
    made = lax.dot_general(left_high, both, dims, preferred_element_type=f32)
    made = made[:, :count] + made[:, count:]
    return made + lax.dot_general(left_low, right_high, dims, preferred_element_type=f32)


def cell_moments(cell, off, tan, bur, phi, charged):
    fill_phi(phi, off)
    charge = jnp.sum(bur[...] * tan[...], axis=0, keepdims=True)
    row = iota((CS, SEG), 0)
    for b in range(cell.shape[0]):
        part = charge[:, b * SEG : (b + 1) * SEG]
        charged[:, b * SEG : (b + 1) * SEG] = jnp.where(row == cell[b], part, 0.0)
    part = dot_halves(phi[...], charged[...], 1)
    part = jnp.concatenate([part, jnp.zeros((8 * GROUP - NM, CS), f32)], axis=0)
    groups = [part[GROUP * g : GROUP * (g + 1), :] for g in range(8)]
    return jnp.concatenate([jnp.zeros((MOMENTS - LAST, SEG), f32), jnp.concatenate(groups, axis=1)], axis=0)


def far_parts_kernel(*refs):
    raw, outs, scratch = refs[:5], refs[5:10], refs[10:]
    stress, off, tan, bur, operator, sems, phi = scratch
    out, op_high, op_low, phi_high, phi_low = outs
    copies = fetch_all(raw, scratch[:5], sems)
    for copy in copies[:4]:
        copy.wait()
    phi[NM:TALL, :] = jnp.zeros((TALL - NM, phi.shape[1]), f32)
    fill_phi(phi, off)
    phi_high[...], phi_low[...] = halves_of(phi[...])
    b = [bur[i : i + 1, :] for i in range(3)]
    t = [tan[i : i + 1, :] for i in range(3)]
    sym = [[0.5 * (stress[i, j] + stress[j, i]) for j in range(3)] for i in range(3)]
    trac = [sym[i][0] * b[0] + sym[i][1] * b[1] + sym[i][2] * b[2] for i in range(3)]
    for i in range(3):
        j, k = (i + 1) % 3, (i + 2) % 3
        out[i : i + 1, :] = trac[j] * t[k] - trac[k] * t[j]
    copies[4].wait()
    none = jnp.zeros((TALL - NM, operator.shape[1]), f32)
    op_high[...], op_low[...] = halves_of(jnp.concatenate([operator[...], none], axis=0))


def far_kernel_body(cell, bur, applied, op_high, op_low, phi_high, phi_low, *rest):
    sources, (out, around, shifted, pots) = rest[:-4], rest[-4:]
    count = len(sources)
    cells = count * CS
    turned = jnp.concatenate([source[...] for source in sources], axis=0).T
    first = MOMENTS - LAST
    for q in range(count):
        at = CS * ((count - q) % count) + first
        for g in range(8):
            piece = turned[CS * g : CS * (g + 1), at : at + GROUP]
            around[q * CS : (q + 1) * CS, GROUP * g : GROUP * (g + 1)] = piece
    around[cells : cells + CS, :] = around[0:CS, :]
    shifted[:, 0:NM] = jnp.zeros((CS, NM), f32)
    for o in range(1, cells):
        shifted[:, o * NM : (o + 1) * NM] = around[cells - o : cells - o + CS, 0:NM]
    high, low = halves_of(shifted[...])
    made = dot_nt(op_high[...], jnp.concatenate([high, low], axis=0))
    local_exp = (made[:, 0:CS] + made[:, CS:] + dot_nt(op_low[...], high)).T
    high, low = halves_of(local_exp)
    both = jnp.concatenate([high, low], axis=0)
    made = jnp.dot(both, phi_high[...], preferred_element_type=f32)
    pots[...] = made[0:CS] + made[CS:] + jnp.dot(high, phi_low[...], preferred_element_type=f32)
    row = iota((CS, SEG), 0)
    for block in range(cell.shape[0]):
        at = slice(block * SEG, (block + 1) * SEG)
        mine = jnp.where(row == cell[block], pots[:, at], 0.0)
        out[:, at] = applied[:, at] + jnp.sum(mine, axis=0, keepdims=True) * bur[:, at]


def final_kernel(back, near_all, far, conn, left, out, force, halves):
    groups = conn.shape[1] // SEG
    returned = back[...].reshape(back.shape[0] * 16, SEG)
    spread = jnp.where(iota((SEG, returned.shape[0]), 0) == left[0:1, :], 1.0, 0.0).astype(bf16)
    high, low = halves_of(returned)
    near = near_all[...] + jnp.dot(spread, high, preferred_element_type=f32)
    near = near + jnp.dot(spread, low, preferred_element_type=f32)
    for b in range(groups):
        at = slice(b * SEG, (b + 1) * SEG)
        force[0:3, at] = 0.5 * (far[:, at] + near[4 * b : 4 * b + 3, :])
    value = force[0:3, :]
    high = value.astype(bf16).astype(f32)
    halves[0:3, :] = high
    halves[3:6, :] = value - high
    chunk = 1024
    segs = conn.shape[1]
    total = jnp.zeros((6 * groups, SEG), f32)
    low_row, high_row = iota((SEG, chunk), 0), iota((groups, chunk), 0)
    for end in range(2):
        for start in range(0, segs, chunk):
            at = slice(start, start + chunk)
            node = conn[end : end + 1, at]
            low = jnp.where(low_row == (node & (SEG - 1)), 1.0, 0.0).astype(bf16)
            mark = high_row == (node >> 7)
            parts = [
                jnp.where(mark, halves[i : i + 1, at], 0.0).astype(bf16) for i in range(6)
            ]
            total = total + dot_nt(jnp.concatenate(parts, axis=0), low)
    for c in range(3):
        whole = total[c * groups : (c + 1) * groups] + total[(3 + c) * groups : (4 + c) * groups]
        for g in range(groups):
            out[c : c + 1, g * SEG : (g + 1) * SEG] = whole[g : g + 1, :]


def call(body, out_shape, in_specs, scratch, flops, size):
    return pl.pallas_call(
        body,
        out_shape=out_shape,
        in_specs=in_specs,
        out_specs=jax.tree.map(lambda _: VMEM, out_shape),
        scratch_shapes=scratch,
        compiler_params=pltpu.CompilerParams(vmem_limit_bytes=size << 20),
        cost_estimate=pl.CostEstimate(flops=flops, bytes_accessed=1 << 20, transcendentals=0),
    )


def local(
    seg_offset,
    tangent,
    burgers,
    box_matrix,
    applied_stress,
    far_kernel,
    block_cell,
    fetch_table,
    pair_list,
    image_shift,
    pair_count,
    node_conn,
):
    blocks = block_cell.shape[0]
    segs = seg_offset.shape[1]
    peers = lax.axis_size("bulk")
    slabs = lax.axis_size("slab")
    shape = lambda *dims: jax.ShapeDtypeStruct(dims, f32)
    table = pltpu.VMEM((16, segs), f32)

    raw = [pair_list, box_matrix, block_cell]
    segments = [seg_offset, tangent, burgers]
    vectors = [image_shift, fetch_table.T, *segments]
    send = call(
        pack_kernel,
        shape(peers, ROWS, SEG),
        [HBM] * 8,
        [pltpu.SMEM(x.shape, x.dtype) for x in raw]
        + [pltpu.VMEM(x.shape, x.dtype) for x in vectors]
        + [pltpu.SemaphoreType.DMA((8,))]
        + [table, pltpu.VMEM((NM, segs), f32), pltpu.VMEM((CS, segs), f32)],
        10**6,
        60,
    )(*raw, *vectors)
    recv = lax.all_to_all(send, "bulk", 0, 0, tiled=True)

    features, near_own, left = call(
        own_kernel,
        (
            jax.ShapeDtypeStruct((blocks, SEG, FEATURES), bf16),
            shape(SEG, SEG),
            jax.ShapeDtypeStruct((8, peers * 16), jnp.int32),
        ),
        [SMEM] * 4 + [VMEM] * 4,
        [
            table,
            pltpu.VMEM((blocks, 3, SEG, SEG), f32),
            pltpu.VMEM((blocks, 8, SEG), f32),
        ],
        10**9,
        12,
    )(pair_list, image_shift, box_matrix, pair_count, *segments, pair_list)

    def from_slab(value, back):
        return lax.ppermute(value, "slab", [(s, (s + back) % slabs) for s in range(slabs)])

    moments = jnp.sum(recv[:, LAST:, :], axis=0)

    ret, near = call(
        pair_kernel,
        (shape(peers, 16, SEG), shape(SEG, SEG)),
        [VMEM] * 3,
        [
            pltpu.VMEM((blocks, 3, SEG, SEG), f32),
            pltpu.VMEM((peers, SEG), jnp.int32),
            pltpu.SMEM((peers, SEG), jnp.int32),
            pltpu.SemaphoreType.DMA,
        ],
        10**10,
        16,
    )(recv, features, near_own)
    ret, stress = lax.optimization_barrier((ret, applied_stress))
    back = lax.all_to_all(ret, "bulk", 0, 0, tiled=True)
    sources = [moments] + [from_slab(moments, k) for k in range(1, slabs)]

    halves = lambda width: [jax.ShapeDtypeStruct((TALL, width), bf16)] * 2
    raw = [*segments, far_kernel]
    parts = call(
        far_parts_kernel,
        (shape(3, segs), *halves(far_kernel.shape[1]), *halves(segs)),
        [HBM] * 5,
        [pltpu.SMEM(stress.shape, f32)]
        + [pltpu.VMEM(x.shape, x.dtype) for x in raw]
        + [pltpu.SemaphoreType.DMA((5,)), pltpu.VMEM((TALL, segs), f32)],
        10**9,
        48,
    )(stress, *raw)
    far = call(
        far_kernel_body,
        shape(3, segs),
        [SMEM] + [VMEM] * (6 + slabs),
        [
            pltpu.VMEM((slabs * CS + CS, SEG), f32),
            pltpu.VMEM((CS, slabs * CS * NM), f32),
            pltpu.VMEM((CS, segs), f32),
        ],
        10**9,
        16,
    )(block_cell, burgers, *parts, *sources)

    return call(
        final_kernel,
        shape(3, segs),
        [VMEM] * 5,
        [pltpu.VMEM((8, segs), f32), pltpu.VMEM((8, segs), f32)],
        10**9,
        24,
    )(back, near, far, node_conn, left)


def solution(mesh):
    both = P(None, ("slab", "bulk"))
    in_specs = (
        both,
        both,
        both,
        P(),
        P(),
        P(),
        P(("slab", "bulk")),
        P(("slab", "bulk"), None),
        both,
        both,
        P(("slab", "bulk")),
        both,
    )
    return jax.shard_map(local, mesh=mesh, in_specs=in_specs, out_specs=both, check_vma=False)
```

```python
import jax
import jax.numpy as jnp
from jax import lax
from jax.experimental import pallas as pl
from jax.experimental.pallas import tpu as pltpu
from jax.sharding import PartitionSpec as P

SEG = 128
CS = 16
NM = 84
SEND = 5
LAST = 40
MOMENTS = 45
ROWS = 56
GROUP = 11
META = 112
FEATURES = 64
KAPPA = 0.2
CORE_SQ = 0.25
VMEM = pl.BlockSpec(memory_space=pltpu.VMEM)
HBM = pl.BlockSpec(memory_space=pltpu.HBM)
SMEM = pl.BlockSpec(memory_space=pltpu.SMEM)
f32 = jnp.float32
bf16 = jnp.bfloat16


def exponents():
    return [(a, b, c) for a in range(7) for b in range(7 - a) for c in range(7 - a - b)]


def iota(shape, dim):
    return lax.broadcasted_iota(jnp.int32, shape, dim)


def lane_block(index):
    return pl.ds(pl.multiple_of(index * SEG, SEG), SEG)


def fill_table(table, off, tan, bur, diag, cross):
    b = [bur[i : i + 1, :] for i in range(3)]
    t = [tan[i : i + 1, :] for i in range(3)]
    table[0:3, :] = off[...]
    for i in range(3):
        table[3 + i : 4 + i, :] = diag * (b[i] * t[i])
    for row, (i, j) in enumerate(((0, 1), (0, 2), (1, 2))):
        table[6 + row : 7 + row, :] = cross * (b[i] * t[j] + b[j] * t[i])


def shift_of(box, shift, k):
    s = [shift[i, k].astype(f32) for i in range(3)]
    return [box[c, 0] * s[0] + box[c, 1] * s[1] + box[c, 2] * s[2] for c in range(3)]


def shift_rows(vec, shape):
    row = iota(shape, 0)
    return jnp.where(row == 0, vec[0], jnp.where(row == 1, vec[1], jnp.where(row == 2, vec[2], 0.0)))


def fetch_all(sources, targets, sems):
    copies = [
        pltpu.make_async_copy(source, target, sems.at[i])
        for i, (source, target) in enumerate(zip(sources, targets, strict=True))
    ]
    for copy in copies:
        copy.start()
    return copies


def shift_table(box, shift):
    steps = [shift[i : i + 1, :].astype(f32) for i in range(3)]
    rows = [box[c, 0] * steps[0] + box[c, 1] * steps[1] + box[c, 2] * steps[2] for c in range(3)]
    return jnp.concatenate(rows + [jnp.zeros((5, shift.shape[1]), f32)], axis=0)


def pack_kernel(*refs):
    sources, send, scratch = refs[:8], refs[8], refs[9:]
    pairs, box, cell, shift, fetch, off, tan, bur, sems, table, phi, charged = scratch
    for copy in fetch_all(sources, scratch[:8], sems):
        copy.wait()
    fill_table(table, off, tan, bur, 2.0 * KAPPA, KAPPA)
    packed = cell_moments(cell, off, tan, bur, phi, charged)
    vectors = shift_table(box, shift)
    peers = send.shape[0]
    wide = jnp.concatenate([fetch[...].astype(f32), jnp.zeros((SEND, SEG - peers), f32)], axis=1)
    tall = jnp.concatenate([wide, jnp.zeros((8 - SEND, SEG), f32)], axis=0).T
    meta = jnp.concatenate(
        [jnp.zeros((SEG, META), f32), tall, jnp.zeros((SEG, SEG - META - 8), f32)], axis=1
    )
    row, lane = iota((ROWS - LAST, SEG), 0), iota((ROWS - LAST, SEG), 1)
    mark = (row == ROWS - LAST - 1) & (lane >= META)
    for p in range(peers):
        rest = jnp.where(mark, meta[p : p + 1, :], packed)
        for s in range(SEND):
            k = p * SEND + s
            at = lane_block(pairs[0, k])
            vec = jnp.broadcast_to(vectors[:, k : k + 1], (8, SEG))
            send[p, 8 * s : 8 * s + 8, :] = table[0:8, at] - vec
            rest = jnp.where(row == s, table[8:9, at], rest)
        send[p, LAST:ROWS, :] = rest


def split(value):
    high = value.astype(bf16).astype(f32)
    rest = value - high
    mid = rest.astype(bf16).astype(f32)
    return high, mid, (rest - mid).astype(bf16).astype(f32)


def fill_features(table, features):
    first = iota((8, SEG), 0) < 3
    one, none = jnp.ones((3, SEG), f32), jnp.zeros((1, SEG), f32)

    def block(b, carry):
        at = lane_block(b)
        head = table[0:8, at]
        high, mid, low = split(head)
        last_high, last_mid, _ = split(table[8:9, at])
        square = split(jnp.sum(jnp.where(first, head * head, 0.0), axis=0, keepdims=True))
        groups = [jnp.where(first, 1.0, high)] * 2
        groups.append(
            jnp.concatenate([one, last_high, last_high, last_mid, square[0], square[1]], axis=0)
        )
        groups.append(jnp.where(first, high, mid))
        groups.append(jnp.concatenate([mid[0:3], low[0:3], square[2], none], axis=0))
        groups.append(jnp.concatenate([high[0:3], high[0:3], none, none], axis=0))
        groups.append(jnp.concatenate([mid[0:3], one, none, none], axis=0))
        groups.append(jnp.zeros((SEG - 56, SEG), f32))
        turned = jnp.concatenate(groups, axis=0).T
        features[b] = turned[:, 0:FEATURES].astype(bf16)
        return carry

    lax.fori_loop(0, features.shape[0], block, 0, unroll=4)


def weights(head, last):
    row = iota((8, SEG), 0)
    first, second = row < 3, (row >= 3) & (row < 6)
    high, mid, low = split(head)
    last_high, last_mid, _ = split(last)
    square = split(jnp.sum(jnp.where(first, head * head, 0.0), axis=0, keepdims=True) + CORE_SQ)
    none = jnp.zeros((8, SEG), f32)
    columns = []
    for i in range(3):
        own = row == i
        parts = [jnp.where(own, part, 0.0) for part in (high, mid, low, -1.0)]
        parts += [jnp.where(own | (row == i + 3), -1.0, 0.0), none, none, none]
        columns.append(jnp.concatenate(parts, axis=0))
    tail = jnp.where(first, 0.0, high)
    edge = jnp.where((row == 3) | (row == 5), last_high, jnp.where(row == 4, last_mid, 0.0))
    parts = [tail, jnp.where(first, 0.0, mid), edge, tail, none, none, none, none]
    columns.append(jnp.concatenate(parts, axis=0))
    twice = [-2.0 * part for part in (high, mid, low)]
    below = [jnp.concatenate([part[0:3], part[0:3], part[0:2]], axis=0) for part in twice]
    norm = jnp.where(row == 3, square[0], jnp.where(row == 4, square[1], square[2]))
    parts = [none, none, jnp.where(row >= 6, 1.0, 0.0), jnp.where(first, twice[0], 0.0)]
    parts.append(jnp.where(row < 6, below[0], jnp.where(row == 6, 1.0, 0.0)))
    parts.append(jnp.where(first, twice[1], jnp.where(second, below[2], 0.0)))
    parts += [jnp.where(first, twice[1], jnp.where(second, norm, 0.0)), none]
    columns.append(jnp.concatenate(parts, axis=0))
    return jnp.concatenate(columns, axis=1).astype(bf16)


def tile(head, last, features, acc, b):
    both = weights(head, last)
    sums = [jnp.zeros((8, SEG), f32) for _ in range(3)]
    step = 64
    for start in range(0, SEG, step):
        at = slice(start, start + step)
        made = jnp.dot(features[b, at, :], both, preferred_element_type=f32)
        inv = lax.rsqrt(made[:, 4 * SEG :])
        weight = made[:, 3 * SEG : 4 * SEG] * (inv * inv * inv)
        for c in range(3):
            push = weight * made[:, c * SEG : (c + 1) * SEG]
            acc[b, c, at, :] += push
            for r in range(0, step, 8):
                sums[c] = sums[c] + push[r : r + 8]
    return [jnp.sum(part, axis=0, keepdims=True) for part in sums]


def fold(acc, near, others):
    ones = jnp.ones((16, SEG), bf16)

    def pair(half, carry):
        at = pl.ds(pl.multiple_of(8 * half, 8), 8)
        rows = []
        for b in (2 * half, 2 * half + 1):
            rows += [jnp.sum(acc[b, c].T, axis=0, keepdims=True) for c in range(2)]
            high, low = halves_of(acc[b, 2])
            rows.append((dot_nt(ones, high) + dot_nt(ones, low))[0:1])
            rows.append(jnp.zeros((1, SEG), f32))
        near[at, :] = others[at, :] - jnp.concatenate(rows, axis=0)
        return carry

    lax.fori_loop(0, acc.shape[0] // 2, pair, 0, unroll=True)


def clear(acc):
    def block(b, carry):
        acc[b] = jnp.zeros(acc.shape[1:], f32)
        return carry

    lax.fori_loop(0, acc.shape[0], block, 0, unroll=4)


def left_rows(blocks, out_shape):
    slots = blocks.shape[1]
    slot, lane = iota((slots, out_shape[1]), 0), iota((slots, out_shape[1]), 1)
    peer, rest = lane >> 4, lane & 15
    third = (rest >= 3).astype(jnp.int32) + (rest >= 6) + (rest >= 9) + (rest >= 12)
    pick = (slot == SEND * peer + third) & (rest < 15)
    tall = jnp.broadcast_to(blocks.astype(f32), (16, slots)).astype(bf16)
    found = jnp.dot(tall, jnp.where(pick, 1.0, 0.0).astype(bf16), preferred_element_type=f32)
    lane = iota(out_shape, 1)
    rest = lane & 15
    third = (rest >= 3).astype(jnp.int32) + (rest >= 6) + (rest >= 9) + (rest >= 12)
    row = 4 * found[0 : out_shape[0]].astype(jnp.int32) + rest - 3 * third
    return jnp.where(rest < 15, row, -1)


def own_kernel(
    pairs, shift, box, count, off, tan, bur, pairs_row, features, near, left, table, acc, left_acc
):
    left[...] = left_rows(pairs_row[0:1, :], left.shape)
    clear(acc)
    left_acc[...] = jnp.zeros_like(left_acc)
    fill_table(table, off, tan, bur, 1.0, 1.0)
    fill_features(table, features)
    blocks = acc.shape[0]
    row = iota((8, SEG), 0)
    scale = jnp.where(row < 3, 1.0, jnp.where(row < 6, 2.0 * KAPPA, KAPPA))

    def pair(k, carry):
        a, b = pairs[0, k], pairs[1, k]
        at = lane_block(a)
        head = table[0:8, at] * scale - shift_rows(shift_of(box, shift, k), (8, SEG))
        rows = tile(head, table[8:9, at] * KAPPA, features, acc, b)
        for c in range(3):
            left_acc[a, c : c + 1, :] += rows[c]
        return carry

    lax.fori_loop(pairs.shape[1] - blocks, count[0], pair, 0)
    for b in range(blocks):
        near[4 * b : 4 * b + 4, :] = left_acc[b, 0:4, :]
    fold(acc, near, near)


def pair_kernel(recv, features, near_own, ret, near, acc, ids_vmem, ids, sem):
    peers = recv.shape[0]
    for p in range(peers):
        ids_vmem[p : p + 1, :] = recv[p, ROWS - 1 : ROWS, :].astype(jnp.int32)
    copy = pltpu.make_async_copy(ids_vmem, ids, sem)
    copy.start()
    clear(acc)
    copy.wait()

    def peer(p, carry):
        for s in range(SEND):
            head, last = recv[p, 8 * s : 8 * s + 8, :], recv[p, LAST + s : LAST + s + 1, :]
            rows = tile(head, last, features, acc, ids[p, META + s])
            for c in range(3):
                ret[p, 3 * s + c : 3 * s + c + 1, :] = rows[c]
        ret[p, 15:16, :] = jnp.zeros((1, SEG), f32)
        return carry

    lax.fori_loop(0, peers, peer, 0, unroll=8)
    fold(acc, near, near_own)


def fill_phi(phi, off):
    powers = []
    for i in range(3):
        x = off[i : i + 1, :]
        made = [None, x]
        for _ in range(5):
            made.append(made[-1] * x)
        powers.append(made)
    pairs_of = {}
    for k, (a, b, c) in enumerate(exponents()):
        if (a, b) not in pairs_of:
            got = [p for p in (powers[0][a], powers[1][b]) if p is not None]
            pairs_of[a, b] = got[0] * got[1] if len(got) == 2 else got[0] if got else None
        value = pairs_of[a, b]
        if c:
            value = powers[2][c] if value is None else value * powers[2][c]
        phi[k : k + 1, :] = jnp.ones_like(powers[0][1]) if value is None else value


def dot_nt(left, right):
    return lax.dot_general(
        left, right, (((1,), (1,)), ((), ())), preferred_element_type=f32
    )


def halves_of(value):
    high = value.astype(bf16)
    return high, (value - high.astype(f32)).astype(bf16)


def dot_halves(left, right, axis):
    left_high, left_low = halves_of(left)
    right_high, right_low = halves_of(right)
    dims = (((1,), (axis,)), ((), ()))
    count = right.shape[1 - axis]
    both = jnp.concatenate([right_high, right_low], axis=1 - axis)
    made = lax.dot_general(left_high, both, dims, preferred_element_type=f32)
    made = made[:, :count] + made[:, count:]
    return made + lax.dot_general(left_low, right_high, dims, preferred_element_type=f32)


def cell_moments(cell, off, tan, bur, phi, charged):
    fill_phi(phi, off)
    charge = jnp.sum(bur[...] * tan[...], axis=0, keepdims=True)
    row = iota((CS, SEG), 0)
    for b in range(cell.shape[0]):
        part = charge[:, b * SEG : (b + 1) * SEG]
        charged[:, b * SEG : (b + 1) * SEG] = jnp.where(row == cell[b], part, 0.0)
    part = dot_halves(phi[...], charged[...], 1)
    part = jnp.concatenate([part, jnp.zeros((8 * GROUP - NM, CS), f32)], axis=0)
    groups = [part[GROUP * g : GROUP * (g + 1), :] for g in range(8)]
    return jnp.concatenate([jnp.zeros((MOMENTS - LAST, SEG), f32), jnp.concatenate(groups, axis=1)], axis=0)


def far_kernel_body(*refs):
    core, raw, sources, out, scratch = refs[0], refs[1:7], refs[7:11], refs[11], refs[12:]
    cell, stress, off, tan, bur, operator, sems, wide, around, shifted, phi, pots = scratch
    copies = fetch_all(raw, scratch[:6], sems)
    for copy in copies[:5]:
        copy.wait()
    fill_phi(phi, off)
    half = len(sources)
    count = 2 * half
    cells = count * CS
    turned = jnp.concatenate([source[...] for source in sources], axis=0).T
    first = MOMENTS - LAST
    for q in range(count):
        at = CS * (2 * ((count + q % 2 - q) // 2 % half) + q % 2) + first
        for g in range(8):
            piece = turned[CS * g : CS * (g + 1), at : at + GROUP]
            wide[q * CS : (q + 1) * CS, GROUP * g : GROUP * (g + 1)] = piece
    wide[cells : cells + 2 * CS, :] = wide[0 : 2 * CS, :]
    around[...] = wide[pl.ds(pl.multiple_of(CS * core[0], CS), cells + CS), :]
    shifted[:, 0:NM] = jnp.zeros((CS, NM), f32)
    for o in range(1, cells):
        shifted[:, o * NM : (o + 1) * NM] = around[cells - o : cells - o + CS, 0:NM]
    copies[5].wait()
    local_exp = dot_halves(operator[...], shifted[...], 1).T
    high, low = halves_of(local_exp)
    phi_high, phi_low = halves_of(phi[...])
    made = jnp.dot(jnp.concatenate([high, low], axis=0), phi_high, preferred_element_type=f32)
    made = made[0:CS] + made[CS:]
    pots[...] = made + jnp.dot(high, phi_low, preferred_element_type=f32)
    b = [bur[i : i + 1, :] for i in range(3)]
    t = [tan[i : i + 1, :] for i in range(3)]
    sym = [[0.5 * (stress[i, j] + stress[j, i]) for j in range(3)] for i in range(3)]
    trac = [sym[i][0] * b[0] + sym[i][1] * b[1] + sym[i][2] * b[2] for i in range(3)]
    for i in range(3):
        j, k = (i + 1) % 3, (i + 2) % 3
        out[i : i + 1, :] = trac[j] * t[k] - trac[k] * t[j]
    row = iota((CS, SEG), 0)
    for block in range(cell.shape[0]):
        at = slice(block * SEG, (block + 1) * SEG)
        mine = jnp.where(row == cell[block], pots[:, at], 0.0)
        out[:, at] += jnp.sum(mine, axis=0, keepdims=True) * bur[:, at]


def final_kernel(back, near_all, far, conn, left, out, force, halves):
    groups = conn.shape[1] // SEG
    returned = back[...].reshape(back.shape[0] * 16, SEG)
    spread = jnp.where(iota((SEG, returned.shape[0]), 0) == left[0:1, :], 1.0, 0.0).astype(bf16)
    high, low = halves_of(returned)
    near = near_all[...] + jnp.dot(spread, high, preferred_element_type=f32)
    near = near + jnp.dot(spread, low, preferred_element_type=f32)
    for b in range(groups):
        at = slice(b * SEG, (b + 1) * SEG)
        force[0:3, at] = 0.5 * (far[:, at] + near[4 * b : 4 * b + 3, :])
    value = force[0:3, :]
    high = value.astype(bf16).astype(f32)
    halves[0:3, :] = high
    halves[3:6, :] = value - high
    chunk = 1024
    segs = conn.shape[1]
    total = jnp.zeros((6 * groups, SEG), f32)
    low_row, high_row = iota((SEG, chunk), 0), iota((groups, chunk), 0)
    for end in range(2):
        for start in range(0, segs, chunk):
            at = slice(start, start + chunk)
            node = conn[end : end + 1, at]
            low = jnp.where(low_row == (node & (SEG - 1)), 1.0, 0.0).astype(bf16)
            mark = high_row == (node >> 7)
            parts = [
                jnp.where(mark, halves[i : i + 1, at], 0.0).astype(bf16) for i in range(6)
            ]
            total = total + dot_nt(jnp.concatenate(parts, axis=0), low)
    for c in range(3):
        whole = total[c * groups : (c + 1) * groups] + total[(3 + c) * groups : (4 + c) * groups]
        for g in range(groups):
            out[c : c + 1, g * SEG : (g + 1) * SEG] = whole[g : g + 1, :]


def call(body, out_shape, in_specs, scratch, flops, size):
    return pl.pallas_call(
        body,
        out_shape=out_shape,
        in_specs=in_specs,
        out_specs=jax.tree.map(lambda _: VMEM, out_shape),
        scratch_shapes=scratch,
        compiler_params=pltpu.CompilerParams(vmem_limit_bytes=size << 20),
        cost_estimate=pl.CostEstimate(flops=flops, bytes_accessed=1 << 20, transcendentals=0),
    )


def local(
    seg_offset,
    tangent,
    burgers,
    box_matrix,
    applied_stress,
    far_kernel,
    block_cell,
    fetch_table,
    pair_list,
    image_shift,
    pair_count,
    node_conn,
):
    blocks = block_cell.shape[0]
    segs = seg_offset.shape[1]
    peers = lax.axis_size("bulk")
    slabs = lax.axis_size("slab")
    shape = lambda *dims: jax.ShapeDtypeStruct(dims, f32)
    table = pltpu.VMEM((16, segs), f32)

    raw = [pair_list, box_matrix, block_cell]
    segments = [seg_offset, tangent, burgers]
    vectors = [image_shift, fetch_table.T, *segments]
    send = call(
        pack_kernel,
        shape(peers, ROWS, SEG),
        [HBM] * 8,
        [pltpu.SMEM(x.shape, x.dtype) for x in raw]
        + [pltpu.VMEM(x.shape, x.dtype) for x in vectors]
        + [pltpu.SemaphoreType.DMA((8,))]
        + [table, pltpu.VMEM((NM, segs), f32), pltpu.VMEM((CS, segs), f32)],
        10**6,
        60,
    )(*raw, *vectors)
    recv = lax.all_to_all(send, "bulk", 0, 0, tiled=True)

    features, near_own, left = call(
        own_kernel,
        (
            jax.ShapeDtypeStruct((blocks, SEG, FEATURES), bf16),
            shape(SEG, SEG),
            jax.ShapeDtypeStruct((8, peers * 16), jnp.int32),
        ),
        [SMEM] * 4 + [VMEM] * 4,
        [
            table,
            pltpu.VMEM((blocks, 3, SEG, SEG), f32),
            pltpu.VMEM((blocks, 8, SEG), f32),
        ],
        10**9,
        12,
    )(pair_list, image_shift, box_matrix, pair_count, *segments, pair_list)

    half = slabs // 2
    core = lax.axis_index("slab") % 2
    moments = jnp.sum(recv[:, LAST:, :], axis=0)
    other = lax.ppermute(moments, "slab", [(s, s ^ 1) for s in range(slabs)])

    ret, near = call(
        pair_kernel,
        (shape(peers, 16, SEG), shape(SEG, SEG)),
        [VMEM] * 3,
        [
            pltpu.VMEM((blocks, 3, SEG, SEG), f32),
            pltpu.VMEM((peers, SEG), jnp.int32),
            pltpu.SMEM((peers, SEG), jnp.int32),
            pltpu.SemaphoreType.DMA,
        ],
        10**10,
        16,
    )(recv, features, near_own)
    ret, other = lax.optimization_barrier((ret, other))
    back = lax.all_to_all(ret, "bulk", 0, 0, tiled=True)
    even, odd = jnp.where(core == 0, moments, other), jnp.where(core == 0, other, moments)
    two = jnp.concatenate([even, odd], axis=0)

    def from_chip(back):
        to = [(s, (s + 2 * back) % slabs) for s in range(slabs)]
        return lax.ppermute(two, "slab", to)

    sources = [two] + [from_chip(k) for k in range(1, half)]
    raw = [block_cell, applied_stress]
    far = call(
        far_kernel_body,
        shape(3, segs),
        [SMEM] + [HBM] * 6 + [VMEM] * half,
        [pltpu.SMEM(x.shape, x.dtype) for x in raw]
        + [pltpu.VMEM(x.shape, x.dtype) for x in segments + [far_kernel]]
        + [
            pltpu.SemaphoreType.DMA((6,)),
            pltpu.VMEM((slabs * CS + 2 * CS, SEG), f32),
            pltpu.VMEM((slabs * CS + CS, SEG), f32),
            pltpu.VMEM((CS, slabs * CS * NM), f32),
            pltpu.VMEM((NM, segs), f32),
            pltpu.VMEM((CS, segs), f32),
        ],
        10**9,
        52,
    )(jnp.full((1,), core, jnp.int32), *raw, *segments, far_kernel, *sources)

    return call(
        final_kernel,
        shape(3, segs),
        [VMEM] * 5,
        [pltpu.VMEM((8, segs), f32), pltpu.VMEM((8, segs), f32)],
        10**9,
        24,
    )(back, near, far, node_conn, left)


def solution(mesh):
    both = P(None, ("slab", "bulk"))
    in_specs = (
        both,
        both,
        both,
        P(),
        P(),
        P(),
        P(("slab", "bulk")),
        P(("slab", "bulk"), None),
        both,
        both,
        P(("slab", "bulk")),
        both,
    )
    return jax.shard_map(local, mesh=mesh, in_specs=in_specs, out_specs=both, check_vma=False)
```

```python
import jax
import jax.numpy as jnp
from jax import lax
from jax.experimental import pallas as pl
from jax.experimental.pallas import tpu as pltpu
from jax.sharding import PartitionSpec as P

SEG = 128
CS = 16
NM = 84
SEND = 5
LAST = 40
MOMENTS = 45
ROWS = 56
GROUP = 11
META = 112
FEATURES = 64
KAPPA = 0.2
CORE_SQ = 0.25
VMEM = pl.BlockSpec(memory_space=pltpu.VMEM)
HBM = pl.BlockSpec(memory_space=pltpu.HBM)
SMEM = pl.BlockSpec(memory_space=pltpu.SMEM)
f32 = jnp.float32
bf16 = jnp.bfloat16


def exponents():
    return [(a, b, c) for a in range(7) for b in range(7 - a) for c in range(7 - a - b)]


def iota(shape, dim):
    return lax.broadcasted_iota(jnp.int32, shape, dim)


def lane_block(index):
    return pl.ds(pl.multiple_of(index * SEG, SEG), SEG)


def fill_table(table, off, tan, bur, diag, cross):
    b = [bur[i : i + 1, :] for i in range(3)]
    t = [tan[i : i + 1, :] for i in range(3)]
    table[0:3, :] = off[...]
    for i in range(3):
        table[3 + i : 4 + i, :] = diag * (b[i] * t[i])
    for row, (i, j) in enumerate(((0, 1), (0, 2), (1, 2))):
        table[6 + row : 7 + row, :] = cross * (b[i] * t[j] + b[j] * t[i])


def shift_of(box, shift, k):
    s = [shift[i, k].astype(f32) for i in range(3)]
    return [box[c, 0] * s[0] + box[c, 1] * s[1] + box[c, 2] * s[2] for c in range(3)]


def shift_rows(vec, shape):
    row = iota(shape, 0)
    return jnp.where(row == 0, vec[0], jnp.where(row == 1, vec[1], jnp.where(row == 2, vec[2], 0.0)))


def fetch_all(sources, targets, sems):
    copies = [
        pltpu.make_async_copy(source, target, sems.at[i])
        for i, (source, target) in enumerate(zip(sources, targets, strict=True))
    ]
    for copy in copies:
        copy.start()
    return copies


def shift_table(box, shift):
    steps = [shift[i : i + 1, :].astype(f32) for i in range(3)]
    rows = [box[c, 0] * steps[0] + box[c, 1] * steps[1] + box[c, 2] * steps[2] for c in range(3)]
    return jnp.concatenate(rows + [jnp.zeros((5, shift.shape[1]), f32)], axis=0)


def pack_kernel(*refs):
    sources, send, scratch = refs[:8], refs[8], refs[9:]
    pairs, box, cell, shift, fetch, off, tan, bur, sems, table, phi, charged, stage, done = scratch
    for copy in fetch_all(sources, scratch[:8], sems):
        copy.wait()
    fill_table(table, off, tan, bur, 2.0 * KAPPA, KAPPA)
    vectors = shift_table(box, shift)
    peers = send.shape[0]
    wide = jnp.concatenate([fetch[...].astype(f32), jnp.zeros((SEND, SEG - peers), f32)], axis=1)
    tall = jnp.concatenate([wide, jnp.zeros((8 - SEND, SEG), f32)], axis=0).T
    meta = jnp.concatenate(
        [jnp.zeros((SEG, META), f32), tall, jnp.zeros((SEG, SEG - META - 8), f32)], axis=1
    )
    row, lane = iota((ROWS - LAST, SEG), 0), iota((ROWS - LAST, SEG), 1)
    mark = (row == ROWS - LAST - 1) & (lane >= META)
    for p in range(peers):
        for s in range(SEND):
            k = p * SEND + s
            vec = jnp.broadcast_to(vectors[:, k : k + 1], (8, SEG))
            stage[p, 8 * s : 8 * s + 8, :] = table[0:8, lane_block(pairs[0, k])] - vec
    heads, tails = (
        pltpu.make_async_copy(stage.at[:, rows, :], send.at[:, rows, :], done.at[i])
        for i, rows in enumerate((pl.ds(0, LAST), pl.ds(LAST, ROWS - LAST)))
    )
    heads.start()
    packed = cell_moments(cell, off, tan, bur, phi, charged)
    for p in range(peers):
        rest = jnp.where(mark, meta[p : p + 1, :], packed)
        for s in range(SEND):
            last = table[8:9, lane_block(pairs[0, p * SEND + s])]
            rest = jnp.where(row == s, last, rest)
        stage[p, LAST:ROWS, :] = rest
    tails.start()
    heads.wait()
    tails.wait()


def split(value):
    high = value.astype(bf16).astype(f32)
    rest = value - high
    mid = rest.astype(bf16).astype(f32)
    return high, mid, (rest - mid).astype(bf16).astype(f32)


def fill_features(table, features):
    first = iota((8, SEG), 0) < 3
    one, none = jnp.ones((3, SEG), f32), jnp.zeros((1, SEG), f32)

    def block(b, carry):
        at = lane_block(b)
        head = table[0:8, at]
        high, mid, low = split(head)
        last_high, last_mid, _ = split(table[8:9, at])
        square = split(jnp.sum(jnp.where(first, head * head, 0.0), axis=0, keepdims=True))
        groups = [jnp.where(first, 1.0, high)] * 2
        groups.append(
            jnp.concatenate([one, last_high, last_high, last_mid, square[0], square[1]], axis=0)
        )
        groups.append(jnp.where(first, high, mid))
        groups.append(jnp.concatenate([mid[0:3], low[0:3], square[2], none], axis=0))
        groups.append(jnp.concatenate([high[0:3], high[0:3], none, none], axis=0))
        groups.append(jnp.concatenate([mid[0:3], one, none, none], axis=0))
        groups.append(jnp.zeros((SEG - 56, SEG), f32))
        turned = jnp.concatenate(groups, axis=0).T
        features[b] = turned[:, 0:FEATURES].astype(bf16)
        return carry

    lax.fori_loop(0, features.shape[0], block, 0, unroll=4)


def weights(head, last):
    row = iota((8, SEG), 0)
    first, second = row < 3, (row >= 3) & (row < 6)
    high, mid, low = split(head)
    last_high, last_mid, _ = split(last)
    square = split(jnp.sum(jnp.where(first, head * head, 0.0), axis=0, keepdims=True) + CORE_SQ)
    none = jnp.zeros((8, SEG), f32)
    columns = []
    for i in range(3):
        own = row == i
        parts = [jnp.where(own, part, 0.0) for part in (high, mid, low, -1.0)]
        parts += [jnp.where(own | (row == i + 3), -1.0, 0.0), none, none, none]
        columns.append(jnp.concatenate(parts, axis=0))
    tail = jnp.where(first, 0.0, high)
    edge = jnp.where((row == 3) | (row == 5), last_high, jnp.where(row == 4, last_mid, 0.0))
    parts = [tail, jnp.where(first, 0.0, mid), edge, tail, none, none, none, none]
    columns.append(jnp.concatenate(parts, axis=0))
    twice = [-2.0 * part for part in (high, mid, low)]
    below = [jnp.concatenate([part[0:3], part[0:3], part[0:2]], axis=0) for part in twice]
    norm = jnp.where(row == 3, square[0], jnp.where(row == 4, square[1], square[2]))
    parts = [none, none, jnp.where(row >= 6, 1.0, 0.0), jnp.where(first, twice[0], 0.0)]
    parts.append(jnp.where(row < 6, below[0], jnp.where(row == 6, 1.0, 0.0)))
    parts.append(jnp.where(first, twice[1], jnp.where(second, below[2], 0.0)))
    parts += [jnp.where(first, twice[1], jnp.where(second, norm, 0.0)), none]
    columns.append(jnp.concatenate(parts, axis=0))
    return jnp.concatenate(columns, axis=1).astype(bf16)


def tile(head, last, features, acc, b):
    both = weights(head, last)
    sums = [jnp.zeros((8, SEG), f32) for _ in range(3)]
    step = 64
    for start in range(0, SEG, step):
        at = slice(start, start + step)
        made = jnp.dot(features[b, at, :], both, preferred_element_type=f32)
        inv = lax.rsqrt(made[:, 4 * SEG :])
        weight = made[:, 3 * SEG : 4 * SEG] * (inv * inv * inv)
        for c in range(3):
            push = weight * made[:, c * SEG : (c + 1) * SEG]
            acc[b, c, at, :] += push
            for r in range(0, step, 8):
                sums[c] = sums[c] + push[r : r + 8]
    return [jnp.sum(part, axis=0, keepdims=True) for part in sums]


def fold(acc, near, others):
    ones = jnp.ones((16, SEG), bf16)

    def pair(half, carry):
        at = pl.ds(pl.multiple_of(8 * half, 8), 8)
        rows = []
        for b in (2 * half, 2 * half + 1):
            rows += [jnp.sum(acc[b, c].T, axis=0, keepdims=True) for c in range(2)]
            high, low = halves_of(acc[b, 2])
            rows.append((dot_nt(ones, high) + dot_nt(ones, low))[0:1])
            rows.append(jnp.zeros((1, SEG), f32))
        near[at, :] = others[at, :] - jnp.concatenate(rows, axis=0)
        return carry

    lax.fori_loop(0, acc.shape[0] // 2, pair, 0, unroll=True)


def clear(acc):
    def block(b, carry):
        acc[b] = jnp.zeros(acc.shape[1:], f32)
        return carry

    lax.fori_loop(0, acc.shape[0], block, 0, unroll=4)


def left_rows(blocks, out_shape):
    slots = blocks.shape[1]
    slot, lane = iota((slots, out_shape[1]), 0), iota((slots, out_shape[1]), 1)
    peer, rest = lane >> 4, lane & 15
    third = (rest >= 3).astype(jnp.int32) + (rest >= 6) + (rest >= 9) + (rest >= 12)
    pick = (slot == SEND * peer + third) & (rest < 15)
    tall = jnp.broadcast_to(blocks.astype(f32), (16, slots)).astype(bf16)
    found = jnp.dot(tall, jnp.where(pick, 1.0, 0.0).astype(bf16), preferred_element_type=f32)
    lane = iota(out_shape, 1)
    rest = lane & 15
    third = (rest >= 3).astype(jnp.int32) + (rest >= 6) + (rest >= 9) + (rest >= 12)
    row = 4 * found[0 : out_shape[0]].astype(jnp.int32) + rest - 3 * third
    return jnp.where(rest < 15, row, -1)


def own_kernel(
    pairs, shift, box, count, off, tan, bur, pairs_row, features, near, left, table, acc, left_acc
):
    left[...] = left_rows(pairs_row[0:1, :], left.shape)
    clear(acc)
    left_acc[...] = jnp.zeros_like(left_acc)
    fill_table(table, off, tan, bur, 1.0, 1.0)
    fill_features(table, features)
    blocks = acc.shape[0]
    row = iota((8, SEG), 0)
    scale = jnp.where(row < 3, 1.0, jnp.where(row < 6, 2.0 * KAPPA, KAPPA))

    def pair(k, carry):
        a, b = pairs[0, k], pairs[1, k]
        at = lane_block(a)
        head = table[0:8, at] * scale - shift_rows(shift_of(box, shift, k), (8, SEG))
        rows = tile(head, table[8:9, at] * KAPPA, features, acc, b)
        for c in range(3):
            left_acc[a, c : c + 1, :] += rows[c]
        return carry

    lax.fori_loop(pairs.shape[1] - blocks, count[0], pair, 0)
    for b in range(blocks):
        near[4 * b : 4 * b + 4, :] = left_acc[b, 0:4, :]
    fold(acc, near, near)


def pair_kernel(recv, features, near_own, ret, near, acc, ids_vmem, ids, sem):
    peers = recv.shape[0]
    for p in range(peers):
        ids_vmem[p : p + 1, :] = recv[p, ROWS - 1 : ROWS, :].astype(jnp.int32)
    copy = pltpu.make_async_copy(ids_vmem, ids, sem)
    copy.start()
    clear(acc)
    copy.wait()

    def peer(p, carry):
        for s in range(SEND):
            head, last = recv[p, 8 * s : 8 * s + 8, :], recv[p, LAST + s : LAST + s + 1, :]
            rows = tile(head, last, features, acc, ids[p, META + s])
            for c in range(3):
                ret[p, 3 * s + c : 3 * s + c + 1, :] = rows[c]
        ret[p, 15:16, :] = jnp.zeros((1, SEG), f32)
        return carry

    lax.fori_loop(0, peers, peer, 0, unroll=8)
    fold(acc, near, near_own)


def fill_phi(phi, off):
    powers = []
    for i in range(3):
        x = off[i : i + 1, :]
        made = [None, x]
        for _ in range(5):
            made.append(made[-1] * x)
        powers.append(made)
    pairs_of = {}
    for k, (a, b, c) in enumerate(exponents()):
        if (a, b) not in pairs_of:
            got = [p for p in (powers[0][a], powers[1][b]) if p is not None]
            pairs_of[a, b] = got[0] * got[1] if len(got) == 2 else got[0] if got else None
        value = pairs_of[a, b]
        if c:
            value = powers[2][c] if value is None else value * powers[2][c]
        phi[k : k + 1, :] = jnp.ones_like(powers[0][1]) if value is None else value


def dot_nt(left, right):
    return lax.dot_general(
        left, right, (((1,), (1,)), ((), ())), preferred_element_type=f32
    )


def halves_of(value):
    high = value.astype(bf16)
    return high, (value - high.astype(f32)).astype(bf16)


def dot_halves(left, right, axis):
    left_high, left_low = halves_of(left)
    right_high, right_low = halves_of(right)
    dims = (((1,), (axis,)), ((), ()))
    count = right.shape[1 - axis]
    both = jnp.concatenate([right_high, right_low], axis=1 - axis)
    made = lax.dot_general(left_high, both, dims, preferred_element_type=f32)
    made = made[:, :count] + made[:, count:]
    return made + lax.dot_general(left_low, right_high, dims, preferred_element_type=f32)


def cell_moments(cell, off, tan, bur, phi, charged):
    fill_phi(phi, off)
    charge = jnp.sum(bur[...] * tan[...], axis=0, keepdims=True)
    row = iota((CS, SEG), 0)
    for b in range(cell.shape[0]):
        part = charge[:, b * SEG : (b + 1) * SEG]
        charged[:, b * SEG : (b + 1) * SEG] = jnp.where(row == cell[b], part, 0.0)
    part = dot_halves(phi[...], charged[...], 1)
    part = jnp.concatenate([part, jnp.zeros((8 * GROUP - NM, CS), f32)], axis=0)
    groups = [part[GROUP * g : GROUP * (g + 1), :] for g in range(8)]
    return jnp.concatenate([jnp.zeros((MOMENTS - LAST, SEG), f32), jnp.concatenate(groups, axis=1)], axis=0)


def far_kernel_body(*refs):
    core, raw, sources, out, scratch = refs[0], refs[1:7], refs[7:11], refs[11], refs[12:]
    cell, stress, off, tan, bur, operator, sems, wide, around, shifted, phi, pots = scratch
    copies = fetch_all(raw, scratch[:6], sems)
    for copy in copies[:5]:
        copy.wait()
    fill_phi(phi, off)
    half = len(sources)
    count = 2 * half
    cells = count * CS
    turned = jnp.concatenate([source[...] for source in sources], axis=0).T
    first = MOMENTS - LAST
    for q in range(count):
        at = CS * (2 * ((count + q % 2 - q) // 2 % half) + q % 2) + first
        for g in range(8):
            piece = turned[CS * g : CS * (g + 1), at : at + GROUP]
            wide[q * CS : (q + 1) * CS, GROUP * g : GROUP * (g + 1)] = piece
    wide[cells : cells + 2 * CS, :] = wide[0 : 2 * CS, :]
    around[...] = wide[pl.ds(pl.multiple_of(CS * core[0], CS), cells + CS), :]
    shifted[:, 0:NM] = jnp.zeros((CS, NM), f32)
    for o in range(1, cells):
        shifted[:, o * NM : (o + 1) * NM] = around[cells - o : cells - o + CS, 0:NM]
    copies[5].wait()
    local_exp = dot_halves(operator[...], shifted[...], 1).T
    high, low = halves_of(local_exp)
    phi_high, phi_low = halves_of(phi[...])
    made = jnp.dot(jnp.concatenate([high, low], axis=0), phi_high, preferred_element_type=f32)
    made = made[0:CS] + made[CS:]
    pots[...] = made + jnp.dot(high, phi_low, preferred_element_type=f32)
    b = [bur[i : i + 1, :] for i in range(3)]
    t = [tan[i : i + 1, :] for i in range(3)]
    sym = [[0.5 * (stress[i, j] + stress[j, i]) for j in range(3)] for i in range(3)]
    trac = [sym[i][0] * b[0] + sym[i][1] * b[1] + sym[i][2] * b[2] for i in range(3)]
    for i in range(3):
        j, k = (i + 1) % 3, (i + 2) % 3
        out[i : i + 1, :] = trac[j] * t[k] - trac[k] * t[j]
    row = iota((CS, SEG), 0)
    for block in range(cell.shape[0]):
        at = slice(block * SEG, (block + 1) * SEG)
        mine = jnp.where(row == cell[block], pots[:, at], 0.0)
        out[:, at] += jnp.sum(mine, axis=0, keepdims=True) * bur[:, at]


def final_kernel(back, near_all, far, conn, left, out, force, halves):
    groups = conn.shape[1] // SEG
    returned = back[...].reshape(back.shape[0] * 16, SEG)
    spread = jnp.where(iota((SEG, returned.shape[0]), 0) == left[0:1, :], 1.0, 0.0).astype(bf16)
    high, low = halves_of(returned)
    near = near_all[...] + jnp.dot(spread, high, preferred_element_type=f32)
    near = near + jnp.dot(spread, low, preferred_element_type=f32)
    for b in range(groups):
        at = slice(b * SEG, (b + 1) * SEG)
        force[0:3, at] = 0.5 * (far[:, at] + near[4 * b : 4 * b + 3, :])
    value = force[0:3, :]
    high = value.astype(bf16).astype(f32)
    halves[0:3, :] = high
    halves[3:6, :] = value - high
    chunk = 1024
    segs = conn.shape[1]
    total = jnp.zeros((6 * groups, SEG), f32)
    low_row, high_row = iota((SEG, chunk), 0), iota((groups, chunk), 0)
    for end in range(2):
        for start in range(0, segs, chunk):
            at = slice(start, start + chunk)
            node = conn[end : end + 1, at]
            low = jnp.where(low_row == (node & (SEG - 1)), 1.0, 0.0).astype(bf16)
            mark = high_row == (node >> 7)
            parts = [
                jnp.where(mark, halves[i : i + 1, at], 0.0).astype(bf16) for i in range(6)
            ]
            total = total + dot_nt(jnp.concatenate(parts, axis=0), low)
    for c in range(3):
        whole = total[c * groups : (c + 1) * groups] + total[(3 + c) * groups : (4 + c) * groups]
        for g in range(groups):
            out[c : c + 1, g * SEG : (g + 1) * SEG] = whole[g : g + 1, :]


def call(body, out_shape, in_specs, scratch, flops, size, out_spec=VMEM):
    return pl.pallas_call(
        body,
        out_shape=out_shape,
        in_specs=in_specs,
        out_specs=jax.tree.map(lambda _: out_spec, out_shape),
        scratch_shapes=scratch,
        compiler_params=pltpu.CompilerParams(vmem_limit_bytes=size << 20),
        cost_estimate=pl.CostEstimate(flops=flops, bytes_accessed=1 << 20, transcendentals=0),
    )


def local(
    seg_offset,
    tangent,
    burgers,
    box_matrix,
    applied_stress,
    far_kernel,
    block_cell,
    fetch_table,
    pair_list,
    image_shift,
    pair_count,
    node_conn,
):
    blocks = block_cell.shape[0]
    segs = seg_offset.shape[1]
    peers = lax.axis_size("bulk")
    slabs = lax.axis_size("slab")
    shape = lambda *dims: jax.ShapeDtypeStruct(dims, f32)
    table = pltpu.VMEM((16, segs), f32)

    raw = [pair_list, box_matrix, block_cell]
    segments = [seg_offset, tangent, burgers]
    vectors = [image_shift, fetch_table.T, *segments]
    send = call(
        pack_kernel,
        shape(peers, ROWS, SEG),
        [HBM] * 8,
        [pltpu.SMEM(x.shape, x.dtype) for x in raw]
        + [pltpu.VMEM(x.shape, x.dtype) for x in vectors]
        + [pltpu.SemaphoreType.DMA((8,))]
        + [table, pltpu.VMEM((NM, segs), f32), pltpu.VMEM((CS, segs), f32)]
        + [pltpu.VMEM((peers, ROWS, SEG), f32), pltpu.SemaphoreType.DMA((2,))],
        10**6,
        60,
        HBM,
    )(*raw, *vectors)
    recv = lax.all_to_all(send, "bulk", 0, 0, tiled=True)

    features, near_own, left = call(
        own_kernel,
        (
            jax.ShapeDtypeStruct((blocks, SEG, FEATURES), bf16),
            shape(SEG, SEG),
            jax.ShapeDtypeStruct((8, peers * 16), jnp.int32),
        ),
        [SMEM] * 4 + [VMEM] * 4,
        [
            table,
            pltpu.VMEM((blocks, 3, SEG, SEG), f32),
            pltpu.VMEM((blocks, 8, SEG), f32),
        ],
        10**9,
        12,
    )(pair_list, image_shift, box_matrix, pair_count, *segments, pair_list)

    half = slabs // 2
    core = lax.axis_index("slab") % 2
    moments = jnp.sum(recv[:, LAST:, :], axis=0)
    other = lax.ppermute(moments, "slab", [(s, s ^ 1) for s in range(slabs)])

    ret, near = call(
        pair_kernel,
        (shape(peers, 16, SEG), shape(SEG, SEG)),
        [VMEM] * 3,
        [
            pltpu.VMEM((blocks, 3, SEG, SEG), f32),
            pltpu.VMEM((peers, SEG), jnp.int32),
            pltpu.SMEM((peers, SEG), jnp.int32),
            pltpu.SemaphoreType.DMA,
        ],
        10**10,
        16,
    )(recv, features, near_own)
    ret, other = lax.optimization_barrier((ret, other))
    back = lax.all_to_all(ret, "bulk", 0, 0, tiled=True)
    even, odd = jnp.where(core == 0, moments, other), jnp.where(core == 0, other, moments)
    two = jnp.concatenate([even, odd], axis=0)

    def from_chip(back):
        to = [(s, (s + 2 * back) % slabs) for s in range(slabs)]
        return lax.ppermute(two, "slab", to)

    sources = [two] + [from_chip(k) for k in range(1, half)]
    raw = [block_cell, applied_stress]
    far = call(
        far_kernel_body,
        shape(3, segs),
        [SMEM] + [HBM] * 6 + [VMEM] * half,
        [pltpu.SMEM(x.shape, x.dtype) for x in raw]
        + [pltpu.VMEM(x.shape, x.dtype) for x in segments + [far_kernel]]
        + [
            pltpu.SemaphoreType.DMA((6,)),
            pltpu.VMEM((slabs * CS + 2 * CS, SEG), f32),
            pltpu.VMEM((slabs * CS + CS, SEG), f32),
            pltpu.VMEM((CS, slabs * CS * NM), f32),
            pltpu.VMEM((NM, segs), f32),
            pltpu.VMEM((CS, segs), f32),
        ],
        10**9,
        52,
    )(jnp.full((1,), core, jnp.int32), *raw, *segments, far_kernel, *sources)

    return call(
        final_kernel,
        shape(3, segs),
        [VMEM] * 5,
        [pltpu.VMEM((8, segs), f32), pltpu.VMEM((8, segs), f32)],
        10**9,
        24,
    )(back, near, far, node_conn, left)


def solution(mesh):
    both = P(None, ("slab", "bulk"))
    in_specs = (
        both,
        both,
        both,
        P(),
        P(),
        P(),
        P(("slab", "bulk")),
        P(("slab", "bulk"), None),
        both,
        both,
        P(("slab", "bulk")),
        both,
    )
    return jax.shard_map(local, mesh=mesh, in_specs=in_specs, out_specs=both, check_vma=False)
```

```python
import jax
import jax.numpy as jnp
from jax import lax
from jax.experimental import pallas as pl
from jax.experimental.pallas import tpu as pltpu
from jax.sharding import PartitionSpec as P

SEG = 128
CS = 16
NM = 84
SEND = 5
LAST = 40
MOMENTS = 45
ROWS = 56
GROUP = 11
META = 112
FEATURES = 64
KAPPA = 0.2
CORE_SQ = 0.25
VMEM = pl.BlockSpec(memory_space=pltpu.VMEM)
HBM = pl.BlockSpec(memory_space=pltpu.HBM)
SMEM = pl.BlockSpec(memory_space=pltpu.SMEM)
f32 = jnp.float32
bf16 = jnp.bfloat16


def exponents():
    return [(a, b, c) for a in range(7) for b in range(7 - a) for c in range(7 - a - b)]


def iota(shape, dim):
    return lax.broadcasted_iota(jnp.int32, shape, dim)


def lane_block(index):
    return pl.ds(pl.multiple_of(index * SEG, SEG), SEG)


def fill_table(table, off, tan, bur, diag, cross):
    b = [bur[i : i + 1, :] for i in range(3)]
    t = [tan[i : i + 1, :] for i in range(3)]
    table[0:3, :] = off[...]
    for i in range(3):
        table[3 + i : 4 + i, :] = diag * (b[i] * t[i])
    for row, (i, j) in enumerate(((0, 1), (0, 2), (1, 2))):
        table[6 + row : 7 + row, :] = cross * (b[i] * t[j] + b[j] * t[i])


def shift_of(box, shift, k):
    s = [shift[i, k].astype(f32) for i in range(3)]
    return [box[c, 0] * s[0] + box[c, 1] * s[1] + box[c, 2] * s[2] for c in range(3)]


def shift_rows(vec, shape):
    row = iota(shape, 0)
    return jnp.where(row == 0, vec[0], jnp.where(row == 1, vec[1], jnp.where(row == 2, vec[2], 0.0)))


def fetch_all(sources, targets, sems):
    copies = [
        pltpu.make_async_copy(source, target, sems.at[i])
        for i, (source, target) in enumerate(zip(sources, targets, strict=True))
    ]
    for copy in copies:
        copy.start()
    return copies


def shift_table(box, shift):
    steps = [shift[i : i + 1, :].astype(f32) for i in range(3)]
    rows = [box[c, 0] * steps[0] + box[c, 1] * steps[1] + box[c, 2] * steps[2] for c in range(3)]
    return jnp.concatenate(rows + [jnp.zeros((5, shift.shape[1]), f32)], axis=0)


def pack_kernel(*refs):
    sources, send, scratch = refs[:8], refs[8], refs[9:]
    pairs, box, cell, shift, fetch, off, tan, bur, sems, table, phi, charged, stage, done = scratch
    for copy in fetch_all(sources, scratch[:8], sems):
        copy.wait()
    fill_table(table, off, tan, bur, 2.0 * KAPPA, KAPPA)
    vectors = shift_table(box, shift)
    peers = send.shape[0]
    wide = jnp.concatenate([fetch[...].astype(f32), jnp.zeros((SEND, SEG - peers), f32)], axis=1)
    tall = jnp.concatenate([wide, jnp.zeros((8 - SEND, SEG), f32)], axis=0).T
    meta = jnp.concatenate(
        [jnp.zeros((SEG, META), f32), tall, jnp.zeros((SEG, SEG - META - 8), f32)], axis=1
    )
    row, lane = iota((ROWS - LAST, SEG), 0), iota((ROWS - LAST, SEG), 1)
    mark = (row == ROWS - LAST - 1) & (lane >= META)
    for p in range(peers):
        for s in range(SEND):
            k = p * SEND + s
            vec = jnp.broadcast_to(vectors[:, k : k + 1], (8, SEG))
            stage[p, 8 * s : 8 * s + 8, :] = table[0:8, lane_block(pairs[0, k])] - vec
    heads, tails = (
        pltpu.make_async_copy(stage.at[:, rows, :], send.at[:, rows, :], done.at[i])
        for i, rows in enumerate((pl.ds(0, LAST), pl.ds(LAST, ROWS - LAST)))
    )
    heads.start()
    packed = cell_moments(cell, off, tan, bur, phi, charged)
    for p in range(peers):
        rest = jnp.where(mark, meta[p : p + 1, :], packed)
        for s in range(SEND):
            last = table[8:9, lane_block(pairs[0, p * SEND + s])]
            rest = jnp.where(row == s, last, rest)
        stage[p, LAST:ROWS, :] = rest
    tails.start()
    heads.wait()
    tails.wait()


def split(value):
    high = value.astype(bf16).astype(f32)
    rest = value - high
    mid = rest.astype(bf16).astype(f32)
    return high, mid, (rest - mid).astype(bf16).astype(f32)


def fill_features(table, features):
    first = iota((8, SEG), 0) < 3
    one, none = jnp.ones((3, SEG), f32), jnp.zeros((1, SEG), f32)

    def block(b, carry):
        at = lane_block(b)
        head = table[0:8, at]
        high, mid, low = split(head)
        last_high, last_mid, _ = split(table[8:9, at])
        square = split(jnp.sum(jnp.where(first, head * head, 0.0), axis=0, keepdims=True))
        groups = [jnp.where(first, 1.0, high)] * 2
        groups.append(
            jnp.concatenate([one, last_high, last_high, last_mid, square[0], square[1]], axis=0)
        )
        groups.append(jnp.where(first, high, mid))
        groups.append(jnp.concatenate([mid[0:3], low[0:3], square[2], none], axis=0))
        groups.append(jnp.concatenate([high[0:3], high[0:3], none, none], axis=0))
        groups.append(jnp.concatenate([mid[0:3], one, none, none], axis=0))
        groups.append(jnp.zeros((SEG - 56, SEG), f32))
        turned = jnp.concatenate(groups, axis=0).T
        features[b] = turned[:, 0:FEATURES].astype(bf16)
        return carry

    lax.fori_loop(0, features.shape[0], block, 0, unroll=4)


def weights(head, last):
    row = iota((8, SEG), 0)
    first, second = row < 3, (row >= 3) & (row < 6)
    high, mid, low = split(head)
    last_high, last_mid, _ = split(last)
    square = split(jnp.sum(jnp.where(first, head * head, 0.0), axis=0, keepdims=True) + CORE_SQ)
    none = jnp.zeros((8, SEG), f32)
    columns = []
    for i in range(3):
        own = row == i
        parts = [jnp.where(own, part, 0.0) for part in (high, mid, low, -1.0)]
        parts += [jnp.where(own | (row == i + 3), -1.0, 0.0), none, none, none]
        columns.append(jnp.concatenate(parts, axis=0))
    tail = jnp.where(first, 0.0, high)
    edge = jnp.where((row == 3) | (row == 5), last_high, jnp.where(row == 4, last_mid, 0.0))
    parts = [tail, jnp.where(first, 0.0, mid), edge, tail, none, none, none, none]
    columns.append(jnp.concatenate(parts, axis=0))
    twice = [-2.0 * part for part in (high, mid, low)]
    below = [jnp.concatenate([part[0:3], part[0:3], part[0:2]], axis=0) for part in twice]
    norm = jnp.where(row == 3, square[0], jnp.where(row == 4, square[1], square[2]))
    parts = [none, none, jnp.where(row >= 6, 1.0, 0.0), jnp.where(first, twice[0], 0.0)]
    parts.append(jnp.where(row < 6, below[0], jnp.where(row == 6, 1.0, 0.0)))
    parts.append(jnp.where(first, twice[1], jnp.where(second, below[2], 0.0)))
    parts += [jnp.where(first, twice[1], jnp.where(second, norm, 0.0)), none]
    columns.append(jnp.concatenate(parts, axis=0))
    return jnp.concatenate(columns, axis=1).astype(bf16)


def tile(head, last, features, acc, b):
    both = weights(head, last)
    sums = [jnp.zeros((8, SEG), f32) for _ in range(3)]
    step = 64
    for start in range(0, SEG, step):
        at = slice(start, start + step)
        made = jnp.dot(features[b, at, :], both, preferred_element_type=f32)
        inv = lax.rsqrt(made[:, 4 * SEG :])
        weight = made[:, 3 * SEG : 4 * SEG] * (inv * inv * inv)
        for c in range(3):
            push = weight * made[:, c * SEG : (c + 1) * SEG]
            acc[b, c, at, :] += push
            for r in range(0, step, 8):
                sums[c] = sums[c] + push[r : r + 8]
    return [jnp.sum(part, axis=0, keepdims=True) for part in sums]


def fold(acc, near, others):
    ones = jnp.ones((16, SEG), bf16)

    def pair(half, carry):
        at = pl.ds(pl.multiple_of(8 * half, 8), 8)
        rows = []
        for b in (2 * half, 2 * half + 1):
            rows += [jnp.sum(acc[b, c].T, axis=0, keepdims=True) for c in range(2)]
            high, low = halves_of(acc[b, 2])
            rows.append((dot_nt(ones, high) + dot_nt(ones, low))[0:1])
            rows.append(jnp.zeros((1, SEG), f32))
        near[at, :] = others[at, :] - jnp.concatenate(rows, axis=0)
        return carry

    lax.fori_loop(0, acc.shape[0] // 2, pair, 0, unroll=True)


def clear(acc):
    def block(b, carry):
        acc[b] = jnp.zeros(acc.shape[1:], f32)
        return carry

    lax.fori_loop(0, acc.shape[0], block, 0, unroll=4)


def left_rows(blocks, out_shape):
    slots = blocks.shape[1]
    slot, lane = iota((slots, out_shape[1]), 0), iota((slots, out_shape[1]), 1)
    peer, rest = lane >> 4, lane & 15
    third = (rest >= 3).astype(jnp.int32) + (rest >= 6) + (rest >= 9) + (rest >= 12)
    pick = (slot == SEND * peer + third) & (rest < 15)
    tall = jnp.broadcast_to(blocks.astype(f32), (16, slots)).astype(bf16)
    found = jnp.dot(tall, jnp.where(pick, 1.0, 0.0).astype(bf16), preferred_element_type=f32)
    lane = iota(out_shape, 1)
    rest = lane & 15
    third = (rest >= 3).astype(jnp.int32) + (rest >= 6) + (rest >= 9) + (rest >= 12)
    row = 4 * found[0 : out_shape[0]].astype(jnp.int32) + rest - 3 * third
    return jnp.where(rest < 15, row, -1)


def own_kernel(
    pairs, shift, box, count, off, tan, bur, pairs_row, features, near, left, table, acc, left_acc
):
    left[...] = left_rows(pairs_row[0:1, :], left.shape)
    clear(acc)
    left_acc[...] = jnp.zeros_like(left_acc)
    fill_table(table, off, tan, bur, 1.0, 1.0)
    fill_features(table, features)
    blocks = acc.shape[0]
    row = iota((8, SEG), 0)
    scale = jnp.where(row < 3, 1.0, jnp.where(row < 6, 2.0 * KAPPA, KAPPA))

    def pair(k, carry):
        a, b = pairs[0, k], pairs[1, k]
        at = lane_block(a)
        head = table[0:8, at] * scale - shift_rows(shift_of(box, shift, k), (8, SEG))
        rows = tile(head, table[8:9, at] * KAPPA, features, acc, b)
        for c in range(3):
            left_acc[a, c : c + 1, :] += rows[c]
        return carry

    lax.fori_loop(pairs.shape[1] - blocks, count[0], pair, 0)
    for b in range(blocks):
        near[4 * b : 4 * b + 4, :] = left_acc[b, 0:4, :]
    fold(acc, near, near)


def pair_kernel(recv, features, near_own, ret, near, acc, ids_vmem, ids, sem):
    peers = recv.shape[0]
    for p in range(peers):
        ids_vmem[p : p + 1, :] = recv[p, ROWS - 1 : ROWS, :].astype(jnp.int32)
    copy = pltpu.make_async_copy(ids_vmem, ids, sem)
    copy.start()
    clear(acc)
    copy.wait()

    def peer(p, carry):
        for s in range(SEND):
            head, last = recv[p, 8 * s : 8 * s + 8, :], recv[p, LAST + s : LAST + s + 1, :]
            rows = tile(head, last, features, acc, ids[p, META + s])
            for c in range(3):
                ret[p, 3 * s + c : 3 * s + c + 1, :] = rows[c]
        ret[p, 15:16, :] = jnp.zeros((1, SEG), f32)
        return carry

    lax.fori_loop(0, peers, peer, 0, unroll=16)
    fold(acc, near, near_own)


def fill_phi(phi, off):
    powers = []
    for i in range(3):
        x = off[i : i + 1, :]
        made = [None, x]
        for _ in range(5):
            made.append(made[-1] * x)
        powers.append(made)
    pairs_of = {}
    for k, (a, b, c) in enumerate(exponents()):
        if (a, b) not in pairs_of:
            got = [p for p in (powers[0][a], powers[1][b]) if p is not None]
            pairs_of[a, b] = got[0] * got[1] if len(got) == 2 else got[0] if got else None
        value = pairs_of[a, b]
        if c:
            value = powers[2][c] if value is None else value * powers[2][c]
        phi[k : k + 1, :] = jnp.ones_like(powers[0][1]) if value is None else value


def dot_nt(left, right):
    return lax.dot_general(
        left, right, (((1,), (1,)), ((), ())), preferred_element_type=f32
    )


def halves_of(value):
    high = value.astype(bf16)
    return high, (value - high.astype(f32)).astype(bf16)


def dot_halves(left, right, axis):
    left_high, left_low = halves_of(left)
    right_high, right_low = halves_of(right)
    dims = (((1,), (axis,)), ((), ()))
    count = right.shape[1 - axis]
    both = jnp.concatenate([right_high, right_low], axis=1 - axis)
    made = lax.dot_general(left_high, both, dims, preferred_element_type=f32)
    made = made[:, :count] + made[:, count:]
    return made + lax.dot_general(left_low, right_high, dims, preferred_element_type=f32)


def cell_moments(cell, off, tan, bur, phi, charged):
    fill_phi(phi, off)
    charge = jnp.sum(bur[...] * tan[...], axis=0, keepdims=True)
    row = iota((CS, SEG), 0)
    for b in range(cell.shape[0]):
        part = charge[:, b * SEG : (b + 1) * SEG]
        charged[:, b * SEG : (b + 1) * SEG] = jnp.where(row == cell[b], part, 0.0)
    part = dot_halves(phi[...], charged[...], 1)
    part = jnp.concatenate([part, jnp.zeros((8 * GROUP - NM, CS), f32)], axis=0)
    groups = [part[GROUP * g : GROUP * (g + 1), :] for g in range(8)]
    return jnp.concatenate([jnp.zeros((MOMENTS - LAST, SEG), f32), jnp.concatenate(groups, axis=1)], axis=0)


def far_kernel_body(*refs):
    core, raw, sources, out, scratch = refs[0], refs[1:7], refs[7:11], refs[11], refs[12:]
    cell, stress, off, tan, bur, operator, sems, wide, around, shifted, phi, pots = scratch
    copies = fetch_all(raw, scratch[:6], sems)
    for copy in copies[:5]:
        copy.wait()
    fill_phi(phi, off)
    half = len(sources)
    count = 2 * half
    cells = count * CS
    turned = jnp.concatenate([source[...] for source in sources], axis=0).T
    first = MOMENTS - LAST
    for q in range(count):
        at = CS * (2 * ((count + q % 2 - q) // 2 % half) + q % 2) + first
        for g in range(8):
            piece = turned[CS * g : CS * (g + 1), at : at + GROUP]
            wide[q * CS : (q + 1) * CS, GROUP * g : GROUP * (g + 1)] = piece
    wide[cells : cells + 2 * CS, :] = wide[0 : 2 * CS, :]
    around[...] = wide[pl.ds(pl.multiple_of(CS * core[0], CS), cells + CS), :]
    shifted[:, 0:NM] = jnp.zeros((CS, NM), f32)
    for o in range(1, cells):
        shifted[:, o * NM : (o + 1) * NM] = around[cells - o : cells - o + CS, 0:NM]
    copies[5].wait()
    local_exp = dot_halves(operator[...], shifted[...], 1).T
    high, low = halves_of(local_exp)
    phi_high, phi_low = halves_of(phi[...])
    made = jnp.dot(jnp.concatenate([high, low], axis=0), phi_high, preferred_element_type=f32)
    made = made[0:CS] + made[CS:]
    pots[...] = made + jnp.dot(high, phi_low, preferred_element_type=f32)
    b = [bur[i : i + 1, :] for i in range(3)]
    t = [tan[i : i + 1, :] for i in range(3)]
    sym = [[0.5 * (stress[i, j] + stress[j, i]) for j in range(3)] for i in range(3)]
    trac = [sym[i][0] * b[0] + sym[i][1] * b[1] + sym[i][2] * b[2] for i in range(3)]
    for i in range(3):
        j, k = (i + 1) % 3, (i + 2) % 3
        out[i : i + 1, :] = trac[j] * t[k] - trac[k] * t[j]
    row = iota((CS, SEG), 0)
    for block in range(cell.shape[0]):
        at = slice(block * SEG, (block + 1) * SEG)
        mine = jnp.where(row == cell[block], pots[:, at], 0.0)
        out[:, at] += jnp.sum(mine, axis=0, keepdims=True) * bur[:, at]


def final_kernel(back, near_all, far, conn, left, out, force, halves):
    groups = conn.shape[1] // SEG
    returned = back[...].reshape(back.shape[0] * 16, SEG)
    spread = jnp.where(iota((SEG, returned.shape[0]), 0) == left[0:1, :], 1.0, 0.0).astype(bf16)
    high, low = halves_of(returned)
    near = near_all[...] + jnp.dot(spread, high, preferred_element_type=f32)
    near = near + jnp.dot(spread, low, preferred_element_type=f32)
    for b in range(groups):
        at = slice(b * SEG, (b + 1) * SEG)
        force[0:3, at] = 0.5 * (far[:, at] + near[4 * b : 4 * b + 3, :])
    value = force[0:3, :]
    high = value.astype(bf16).astype(f32)
    halves[0:3, :] = high
    halves[3:6, :] = value - high
    chunk = 1024
    segs = conn.shape[1]
    total = jnp.zeros((6 * groups, SEG), f32)
    low_row, high_row = iota((SEG, chunk), 0), iota((groups, chunk), 0)
    for end in range(2):
        for start in range(0, segs, chunk):
            at = slice(start, start + chunk)
            node = conn[end : end + 1, at]
            low = jnp.where(low_row == (node & (SEG - 1)), 1.0, 0.0).astype(bf16)
            mark = high_row == (node >> 7)
            parts = [
                jnp.where(mark, halves[i : i + 1, at], 0.0).astype(bf16) for i in range(6)
            ]
            total = total + dot_nt(jnp.concatenate(parts, axis=0), low)
    for c in range(3):
        whole = total[c * groups : (c + 1) * groups] + total[(3 + c) * groups : (4 + c) * groups]
        for g in range(groups):
            out[c : c + 1, g * SEG : (g + 1) * SEG] = whole[g : g + 1, :]


def call(body, out_shape, in_specs, scratch, flops, size, out_spec=VMEM):
    return pl.pallas_call(
        body,
        out_shape=out_shape,
        in_specs=in_specs,
        out_specs=jax.tree.map(lambda _: out_spec, out_shape),
        scratch_shapes=scratch,
        compiler_params=pltpu.CompilerParams(vmem_limit_bytes=size << 20),
        cost_estimate=pl.CostEstimate(flops=flops, bytes_accessed=1 << 20, transcendentals=0),
    )


def local(
    seg_offset,
    tangent,
    burgers,
    box_matrix,
    applied_stress,
    far_kernel,
    block_cell,
    fetch_table,
    pair_list,
    image_shift,
    pair_count,
    node_conn,
):
    blocks = block_cell.shape[0]
    segs = seg_offset.shape[1]
    peers = lax.axis_size("bulk")
    slabs = lax.axis_size("slab")
    shape = lambda *dims: jax.ShapeDtypeStruct(dims, f32)
    table = pltpu.VMEM((16, segs), f32)

    raw = [pair_list, box_matrix, block_cell]
    segments = [seg_offset, tangent, burgers]
    vectors = [image_shift, fetch_table.T, *segments]
    send = call(
        pack_kernel,
        shape(peers, ROWS, SEG),
        [HBM] * 8,
        [pltpu.SMEM(x.shape, x.dtype) for x in raw]
        + [pltpu.VMEM(x.shape, x.dtype) for x in vectors]
        + [pltpu.SemaphoreType.DMA((8,))]
        + [table, pltpu.VMEM((NM, segs), f32), pltpu.VMEM((CS, segs), f32)]
        + [pltpu.VMEM((peers, ROWS, SEG), f32), pltpu.SemaphoreType.DMA((2,))],
        10**6,
        60,
        HBM,
    )(*raw, *vectors)
    recv = lax.all_to_all(send, "bulk", 0, 0, tiled=True)

    features, near_own, left = call(
        own_kernel,
        (
            jax.ShapeDtypeStruct((blocks, SEG, FEATURES), bf16),
            shape(SEG, SEG),
            jax.ShapeDtypeStruct((8, peers * 16), jnp.int32),
        ),
        [SMEM] * 4 + [VMEM] * 4,
        [
            table,
            pltpu.VMEM((blocks, 3, SEG, SEG), f32),
            pltpu.VMEM((blocks, 8, SEG), f32),
        ],
        10**9,
        12,
    )(pair_list, image_shift, box_matrix, pair_count, *segments, pair_list)

    half = slabs // 2
    core = lax.axis_index("slab") % 2
    moments = jnp.sum(recv[:, LAST:, :], axis=0)
    other = lax.ppermute(moments, "slab", [(s, s ^ 1) for s in range(slabs)])

    ret, near = call(
        pair_kernel,
        (shape(peers, 16, SEG), shape(SEG, SEG)),
        [VMEM] * 3,
        [
            pltpu.VMEM((blocks, 3, SEG, SEG), f32),
            pltpu.VMEM((peers, SEG), jnp.int32),
            pltpu.SMEM((peers, SEG), jnp.int32),
            pltpu.SemaphoreType.DMA,
        ],
        10**10,
        16,
    )(recv, features, near_own)
    ret, other = lax.optimization_barrier((ret, other))
    back = lax.all_to_all(ret, "bulk", 0, 0, tiled=True)
    even, odd = jnp.where(core == 0, moments, other), jnp.where(core == 0, other, moments)
    two = jnp.concatenate([even, odd], axis=0)

    def from_chip(back):
        to = [(s, (s + 2 * back) % slabs) for s in range(slabs)]
        return lax.ppermute(two, "slab", to)

    sources = [two] + [from_chip(k) for k in range(1, half)]
    raw = [block_cell, applied_stress]
    far = call(
        far_kernel_body,
        shape(3, segs),
        [SMEM] + [HBM] * 6 + [VMEM] * half,
        [pltpu.SMEM(x.shape, x.dtype) for x in raw]
        + [pltpu.VMEM(x.shape, x.dtype) for x in segments + [far_kernel]]
        + [
            pltpu.SemaphoreType.DMA((6,)),
            pltpu.VMEM((slabs * CS + 2 * CS, SEG), f32),
            pltpu.VMEM((slabs * CS + CS, SEG), f32),
            pltpu.VMEM((CS, slabs * CS * NM), f32),
            pltpu.VMEM((NM, segs), f32),
            pltpu.VMEM((CS, segs), f32),
        ],
        10**9,
        52,
    )(jnp.full((1,), core, jnp.int32), *raw, *segments, far_kernel, *sources)

    return call(
        final_kernel,
        shape(3, segs),
        [VMEM] * 5,
        [pltpu.VMEM((8, segs), f32), pltpu.VMEM((8, segs), f32)],
        10**9,
        24,
    )(back, near, far, node_conn, left)


def solution(mesh):
    both = P(None, ("slab", "bulk"))
    in_specs = (
        both,
        both,
        both,
        P(),
        P(),
        P(),
        P(("slab", "bulk")),
        P(("slab", "bulk"), None),
        both,
        both,
        P(("slab", "bulk")),
        both,
    )
    return jax.shard_map(local, mesh=mesh, in_specs=in_specs, out_specs=both, check_vma=False)
```
